256 devices in a mesh: dp: 64 (over y, z_hi, x, core), tensor: 4 (over z_lo).
Axes of the slice: x: 4, y: 4, z: 8 (z_hi: 2, z_lo: 4; z = z_hi * 4 + z_lo), core: 2. Of those that a mesh axis runs over, the one named last changes fastest.
Arguments:
- tokens: bfloat16 [8192, 16384], P('dp', 'tensor'), may hold values from -6 to 6
- norm_gain: float32 [16384], P('tensor'), may hold values from 0.5 to 3, as said below
- query_weight: bfloat16 [16384, 1536], P('dp', 'tensor'), may hold values from -0.046875 to 0.046875
- kv_weight: bfloat16 [16384, 256], P('dp', 'tensor'), may hold values from -0.046875 to 0.046875
- out_weight: bfloat16 [1536, 16384], P('dp', 'tensor'), may hold values from -0.15625 to 0.15625
- lengths: int32 [64], P('dp'), may hold values from 32 to 128, as said below
Outputs:
- mixed: bfloat16 [8192, 16384], P('dp', 'tensor')
The draws below stay inside these ranges and needn't reach their ends.
Inputs may be any that keep to these rules, and one draw needn't show every extreme that they name: `norm_gain`: gains of the norm, one a feature. `lengths`: valid tokens of each trajectory, counted from its start; some trajectory fills all 128 positions.
All inputs are finite; a program needn't handle non-finite values.
Results may differ from the reference program's by a relative error of at most 0.04.
Values may be sent and summed in bfloat16 or wider, within the bound.
No kernel may reach another device: no remote copies, remote signals or barrier semaphores. Data moves between devices by JAX's collectives and lax.ppermute only.
A program may use at most 128 MiB of HBM per device.

```python
import math
import jax
import jax.numpy as jnp
from jax import lax

D = 16384
HD = 128
HQ = 12
LEN = 128
TRAJ = 64
TOKENS = 8192


def draw_norm_gain(key, part):
    key = jax.random.fold_in(key, 11)
    unit = jax.random.uniform(key, (D,), jnp.float32)
    lowest, highest = (0.5, 2.0)
    return lowest * jnp.exp(unit * math.log(highest / lowest))


def draw_lengths(key, part):
    key = jax.random.fold_in(key, 7)
    first_key, second_key = jax.random.split(key)
    base = jax.random.randint(first_key, (TRAJ,), max(1, LEN // 4), LEN + 1)
    chosen = jax.random.randint(second_key, (), 0, TRAJ)
    places = jnp.arange(TRAJ, dtype=jnp.int32)
    return jnp.where(places == chosen, LEN, base).astype(jnp.int32)


def steps_of(stream_key, dims, shards, low, top_value):
    level, own = 1.0, jax.random.fold_in(stream_key, 6)
    for axis_at, blocks in shards:
        steps = jnp.exp(jax.random.uniform(jax.random.fold_in(own, axis_at), (blocks,), jnp.float32, low / len(shards), top_value / len(shards)))
        level = level * jnp.repeat(steps, dims[axis_at] // blocks).reshape([-1 if axis == axis_at else 1 for axis in range(len(dims))])
    return level


def centred(stream_key, shape, deviation, most, cuts=(), kind=jnp.bfloat16):
    drawn = jax.random.normal(stream_key, shape, jnp.float32) * deviation
    if len(cuts) > 0:
        drawn = steps_of(stream_key, shape, cuts, -0.22, 0.18) * drawn
    return jnp.clip(drawn, min=-most, max=most).astype(kind)


def setup_inputs(seed: int = 0) -> dict:
    splits = jax.random.split(jax.random.key(seed), 7)
    return {
        "tokens": centred(splits[0], (TOKENS, D), 1.0, 6.0, ((0, 64), (1, 4))),
        "norm_gain": draw_norm_gain(jax.random.fold_in(splits[6], 71), 0),
        "query_weight": centred(splits[2], (D, HQ * HD), D ** -0.5, 0.046875, ((0, 64), (1, 4))),
        "kv_weight": centred(splits[3], (D, 2 * HD), D ** -0.5, 0.046875, ((0, 64), (1, 4))),
        "out_weight": centred(splits[4], (HQ * HD, D), (HQ * HD) ** -0.5, 0.15625, ((0, 64), (1, 4))),
        "lengths": draw_lengths(jax.random.fold_in(splits[6], 71), 0),
    }


def rotary(values):
    length = values.shape[0]
    width = values.shape[-1]
    position = jnp.arange(length, dtype=jnp.float32)
    freqs = jnp.exp(jnp.arange(width // 2, dtype=jnp.float32) * (-2.0 * math.log(500000.0) / width))
    angle = position[:, None] * freqs[None, :]
    angle = angle.reshape((length,) + (1,) * (values.ndim - 2) + (width // 2,))
    cosine = jnp.cos(angle)
    sine = jnp.sin(angle)
    pairs = values.reshape(values.shape[:-1] + (width // 2, 2))
    former = pairs[..., 0]
    latter = pairs[..., 1]
    turned = jnp.stack([former * cosine - latter * sine, former * sine + latter * cosine], axis=-1)
    return turned.reshape(values.shape)

def attend(query, keys, values, limit):
    length = query.shape[0]
    scale = query.shape[-1] ** (-0.5)
    scores = jnp.einsum('qhd,kd->hqk', query.astype(jnp.float32), keys.astype(jnp.float32)) * scale
    rows_idx = jnp.arange(length, dtype=jnp.int32)
    valid = (rows_idx[None, :] <= rows_idx[:, None]) & (rows_idx[None, :] < limit)
    scores = jnp.where(valid[None], scores, -jnp.inf)
    highest = lax.optimization_barrier(jnp.max(scores, axis=-1, keepdims=True))
    raised = jnp.exp(scores - highest)
    totals = lax.optimization_barrier(jnp.sum(raised, axis=-1, keepdims=True))
    weights = (raised / totals).astype(jnp.bfloat16)
    output = jnp.einsum('hqk,kd->qhd', weights.astype(jnp.float32), values.astype(jnp.float32))
    live = rows_idx < limit
    output = jnp.where(live[:, None, None], output, 0.0).astype(jnp.bfloat16)
    return output.reshape(length, query.shape[1] * query.shape[2])

def one_trajectory(hidden, limit, norm_gain, query_weight, kv_weight, out_weight):
    widened = hidden.astype(jnp.float32)
    meansq = lax.optimization_barrier(jnp.mean(widened * widened, axis=-1, keepdims=True))
    normed = (widened * lax.rsqrt(meansq + 1e-05) * norm_gain).astype(jnp.bfloat16)
    query_raw = jnp.dot(normed, query_weight, preferred_element_type=jnp.float32)
    kv_rows = jnp.dot(normed, kv_weight, preferred_element_type=jnp.float32).astype(jnp.bfloat16)
    query = rotary(query_raw.reshape(LEN, HQ, HD)).astype(jnp.bfloat16)
    keys = rotary(kv_rows[:, :HD].astype(jnp.float32)).astype(jnp.bfloat16)
    values = kv_rows[:, HD:]
    attended = attend(query, keys, values, limit)
    return jnp.dot(attended, out_weight, preferred_element_type=jnp.float32).astype(jnp.bfloat16)

def reference(tokens, norm_gain, query_weight, kv_weight, out_weight, lengths):
    stacked = tokens.reshape(TRAJ, LEN, D)

    def single(pair):
        return one_trajectory(pair[0], pair[1], norm_gain, query_weight, kv_weight, out_weight)
    result = lax.map(single, (stacked, lengths))
    return result.reshape(TOKENS, D)
```

```python
import math

import jax
import jax.numpy as jnp
import numpy as np
from jax import lax
from jax.sharding import Mesh
from jax.sharding import PartitionSpec as P

AXES = ("y", "zh", "x", "core", "zl")
SIZES = (4, 2, 4, 2, 4)
D = 16384
HD = 128
ROWS = 128
BF = jnp.bfloat16
F32 = jnp.float32


def flat(*coords):
    index = 0
    for size, coord in zip(SIZES, coords):
        index = index * size + coord
    return index


def every():
    for y in range(4):
        for zh in range(2):
            for x in range(4):
                for c in range(2):
                    for t in range(4):
                        yield y, zh, x, c, t


def swap(value, axis, d):
    n = SIZES[AXES.index(axis)]
    return lax.ppermute(value, axis, [(i, i ^ d) for i in range(n)])


def move(value, where):
    return lax.ppermute(value, AXES, [(flat(*at), flat(*where(*at))) for at in every()])


def tables():
    freqs = np.exp(np.arange(HD // 2, dtype=np.float32) * np.float32(-2.0 * math.log(500000.0) / HD))
    angle = np.arange(ROWS, dtype=np.float32)[:, None] * freqs.astype(np.float32)[None, :]
    cosine = np.repeat(np.cos(angle), 2, axis=1).astype(np.float32)
    sine = np.repeat(np.sin(angle), 2, axis=1).astype(np.float32)
    sine[:, 0::2] *= -1.0
    return cosine, sine


COSINE, SINE = tables()


def rotate(values):
    shape = (ROWS,) + (1,) * (values.ndim - 2) + (HD,)
    even = (jnp.arange(HD) % 2 == 0)
    partner = jnp.where(even, jnp.roll(values, -1, axis=-1), jnp.roll(values, 1, axis=-1))
    return values * COSINE.reshape(shape) + partner * SINE.reshape(shape)


def attend(query, keys, values, limit):
    scale = HD ** (-0.5)
    scores = jnp.einsum("qhd,kd->hqk", query, keys, preferred_element_type=F32) * scale
    at = jnp.arange(ROWS, dtype=jnp.int32)
    valid = (at[None, :] <= at[:, None]) & (at[None, :] < limit)
    scores = jnp.where(valid[None], scores, -jnp.inf)
    raised = jnp.exp(scores - jnp.max(scores, axis=-1, keepdims=True))
    weights = (raised / jnp.sum(raised, axis=-1, keepdims=True)).astype(BF)
    output = jnp.einsum("hqk,kd->qhd", weights, values, preferred_element_type=F32)
    output = jnp.where((at < limit)[:, None, None], output, 0.0).astype(BF)
    return output.reshape(ROWS, query.shape[1] * HD)


def pick(flag, first, second):
    return jnp.where(flag, second, first)


def body(tokens, norm_gain, query_weight, kv_weight, out_weight, lengths):
    y, zh, x, c, t = (lax.axis_index(name) for name in AXES)

    packed = jnp.concatenate(
        [query_weight[:, :128], query_weight[:, 128:256], query_weight[:, 256:]]
        + [kv_weight.T[:, :128], kv_weight.T[:, 128:]],
        axis=0,
    )
    near = move(packed, lambda y, zh, x, c, t: (x ^ y, zh, 2 * c + (t & 1), t >> 1, y))
    far = move(packed, lambda y, zh, x, c, t: (x ^ y, zh ^ 1, 2 * c + (t & 1), t >> 1, y))
    mine = jnp.stack([near, far])
    blocks = [mine] + [swap(mine, "x", d) for d in (1, 2, 3)]

    def heads_of(block):
        return jnp.concatenate([block[:, 0:256], block[:, 256:512], block[:, 512:768]], axis=2)

    def kv_of(block):
        return jnp.concatenate([block[:, 768:832], block[:, 832:896]], axis=2)

    q_w = jnp.stack(
        [jnp.concatenate([heads_of(blocks[2 * cr]), heads_of(blocks[2 * cr + 1])], axis=2) for cr in (0, 1)], axis=1
    ).reshape(1024, 768)
    kv_w = jnp.stack(
        [jnp.concatenate([kv_of(blocks[2 * cr]), kv_of(blocks[2 * cr + 1])], axis=1) for cr in (0, 1)], axis=2
    )
    kv_w = jnp.swapaxes(kv_w, 0, 1).reshape(128, 1024)

    widened = tokens.astype(F32)
    squares = jnp.sum(widened * widened, axis=1)
    gained = (widened * norm_gain[None, :]).astype(BF)
    parts = gained.reshape(ROWS, 16, 256)

    def features(d):
        s = y ^ d ^ t
        picked = [
            lax.dynamic_slice(gained, (0, (((zh ^ a) * 4 + s) * 2 + ((x >> 1) ^ b)) * 256), (ROWS, 256))
            for a in (0, 1)
            for b in (0, 1)
        ]
        return jnp.concatenate(picked, axis=1)

    ring = [features(0)] + [swap(features(d), "y", d) for d in (1, 2, 3)]
    ring = jnp.stack(ring)
    other = swap(ring, "core", 1)
    inputs = jnp.stack([ring, other], axis=1).reshape(1024, 1024)

    note = jnp.stack([squares, jnp.full((ROWS,), lengths[0], jnp.int32).astype(F32)])
    note_other = swap(note, "core", 1)
    both = jnp.stack([squares, note_other[0]])
    total = both
    for d in (1, 2, 3):
        total = total + swap(both, "zl", d)
    scales = lax.rsqrt(total / D + 1e-05)

    q_part = jnp.dot(inputs, q_w, preferred_element_type=F32)
    kv_part = lax.dot_general(inputs, kv_w, (((1,), (1,)), ((), ())), preferred_element_type=F32)
    part = jnp.concatenate([q_part, kv_part], axis=1).reshape(4, 256, 896)
    summed = part[0]
    for d in (1, 2, 3):
        summed = summed + swap(part[d].astype(BF), "y", d).astype(F32)
    summed = summed.reshape(2, ROWS, 896)

    def share(d):
        target = t ^ d
        rows = lax.dynamic_index_in_dim(summed, (target & 1) ^ c, 0, keepdims=False)
        heads = lax.dynamic_slice(rows, (0, (target >> 1) * 384), (ROWS, 384))
        return jnp.concatenate([heads, rows[:, 768:]], axis=1)

    raw = share(0)
    for d in (1, 2, 3):
        raw = raw + swap(share(d).astype(BF), "zl", d).astype(F32)
    mine_here = (t & 1) ^ c
    scale = lax.dynamic_index_in_dim(scales, mine_here, 0, keepdims=False)
    raw = raw * scale[:, None]
    limit = jnp.where(mine_here == 0, lengths[0], note_other[1, 0].astype(jnp.int32))
    kv_half = raw[:, 384:]
    kv_half = pick((x & 1) == 1, kv_half, jnp.roll(kv_half, 64, axis=1)).astype(BF)
    kv_other = swap(kv_half, "core", 1)
    keys = rotate(pick(c == 1, kv_half, kv_other).astype(F32)).astype(BF)
    values = pick(c == 1, kv_other, kv_half)
    query = rotate(raw[:, :384].reshape(ROWS, 3, HD)).astype(BF)
    attended = attend(query, keys, values, limit)

    got = [attended] + [swap(attended, "zl", d) for d in (1, 2, 3)]
    flip_heads = ((t >> 1) ^ (x & 1)) == 1
    flip_rows = mine_here == 1
    by_rows = []
    for a in (0, 1):
        first, second = got[a], got[2 + a]
        by_rows.append(
            jnp.concatenate([pick(flip_heads, first, second), pick(flip_heads, second, first)], axis=1)
        )
    half = jnp.stack([pick(flip_rows, by_rows[0], by_rows[1]), pick(flip_rows, by_rows[1], by_rows[0])])
    other_half = swap(half, "core", 1)[::-1]
    whole = jnp.concatenate([pick(c == 1, half, other_half), pick(c == 1, other_half, half)], axis=2)
    whole = whole.reshape(256, 1536)

    wo = out_weight.reshape(24, 2, 2048)
    here = lax.dynamic_index_in_dim(wo, c, 1, keepdims=False)
    there = swap(lax.dynamic_index_in_dim(wo, 1 - c, 1, keepdims=False), "core", 1)
    pair = jnp.concatenate([pick(c == 1, here, there), pick(c == 1, there, here)], axis=0)

    def gathered(piece, first_axis, last_axis, first_at, exchange):
        width = piece.shape[1]
        if exchange:
            own = move(piece, lambda y, zh, x, c, t: (x, zh, y, c, t))
            away = move(piece, lambda y, zh, x, c, t: (x, zh ^ 1, y, c, t))
        else:
            own = piece
            away = swap(piece, "zh", 1)
        level = jnp.stack([pick(zh == 1, own, away), pick(zh == 1, away, own)])
        ringed = [level] + [swap(level, first_axis, d) for d in (1, 2, 3)]
        low = [(pick((first_at & 1) == 1, ringed[2 * h], ringed[2 * h + 1]),
                pick((first_at & 1) == 1, ringed[2 * h + 1], ringed[2 * h])) for h in (0, 1)]
        high = (first_at >> 1) == 1
        ordered = [pick(high, low[0][0], low[1][0]), pick(high, low[0][1], low[1][1]),
                   pick(high, low[1][0], low[0][0]), pick(high, low[1][1], low[0][1])]
        block = jnp.stack(ordered, axis=1).reshape(384, width)
        return [block] + [swap(block, last_axis, d) for d in (1, 2, 3)]

    a_blocks = gathered(pair[:, :1024], "y", "x", y, True)
    b_blocks = gathered(pair[:, 1024:], "x", "y", x, False)
    outs = []
    for blocks_here, at in ((a_blocks, x), (b_blocks, y)):
        acc = None
        for d in range(4):
            rows = lax.dynamic_slice(whole, (0, (at ^ d) * 384), (256, 384))
            term = jnp.dot(rows, blocks_here[d], preferred_element_type=F32)
            acc = term if acc is None else acc + term
        outs.append(acc.astype(BF))
    out = jnp.concatenate(outs, axis=1)
    kept, sent = out[:ROWS], out[ROWS:]
    came = swap(sent, "core", 1)
    return jnp.concatenate([pick(c == 1, kept, came), pick(c == 1, came, kept)], axis=1)


def solution(mesh):
    fine = Mesh(mesh.devices.reshape(SIZES), AXES)
    rows = ("y", "zh", "x", "core")
    placed = (P(rows, "zl"), P("zl"), P(rows, "zl"), P(rows, "zl"), P(rows, "zl"), P(rows))
    return jax.shard_map(body, mesh=fine, in_specs=placed, out_specs=P(rows, "zl"), check_vma=False)
```

```python
import math

import jax
import jax.numpy as jnp
import numpy as np
from jax import lax
from jax.experimental import pallas as pl
from jax.experimental.pallas import tpu as pltpu
from jax.sharding import Mesh
from jax.sharding import PartitionSpec as P

AXES = ("y", "zh", "x", "core", "zl")
SIZES = (4, 2, 4, 2, 4)
D = 16384
HD = 128
ROWS = 128
BF = jnp.bfloat16
F32 = jnp.float32


def flat(*coords):
    index = 0
    for size, coord in zip(SIZES, coords):
        index = index * size + coord
    return index


def every():
    for y in range(4):
        for zh in range(2):
            for x in range(4):
                for c in range(2):
                    for t in range(4):
                        yield y, zh, x, c, t


def swap(value, axis, d):
    n = SIZES[AXES.index(axis)]
    return lax.ppermute(value, axis, [(i, i ^ d) for i in range(n)])


def move(value, where):
    return lax.ppermute(value, AXES, [(flat(*at), flat(*where(*at))) for at in every()])


def tables():
    freqs = np.exp(np.arange(HD // 2, dtype=np.float32) * np.float32(-2.0 * math.log(500000.0) / HD))
    angle = np.arange(ROWS, dtype=np.float32)[:, None] * freqs.astype(np.float32)[None, :]
    cosine = np.repeat(np.cos(angle), 2, axis=1).astype(np.float32)
    sine = np.repeat(np.sin(angle), 2, axis=1).astype(np.float32)
    sine[:, 0::2] *= -1.0
    return cosine, sine


COSINE, SINE = tables()


def rotate(values, cosine, sine):
    shape = (values.shape[0],) + (1,) * (values.ndim - 2) + (HD,)
    even = jnp.arange(HD) % 2 == 0
    partner = jnp.where(even, jnp.roll(values, -1, axis=-1), jnp.roll(values, 1, axis=-1))
    return values * cosine.reshape(shape) + partner * sine.reshape(shape)


def pick(flag, first, second):
    return jnp.where(flag, second, first)


def by_index(parts, at):
    odd = (at & 1) == 1
    high = (at >> 1) == 1
    a, b = pick(odd, parts[0], parts[1]), pick(odd, parts[1], parts[0])
    c, d = pick(odd, parts[2], parts[3]), pick(odd, parts[3], parts[2])
    return [pick(high, a, c), pick(high, b, d), pick(high, c, a), pick(high, d, b)]


def whole(shape):
    return pl.BlockSpec(memory_space=pltpu.VMEM)


def pack_kernel(q_ref, kv_ref, out_ref):
    for h in range(3):
        out_ref[256 * h : 256 * h + 256, :] = q_ref[:, 128 * h : 128 * h + 128]
    for h in range(2):
        out_ref[768 + 64 * h : 832 + 64 * h, :] = kv_ref[:, 128 * h : 128 * h + 128]


def pack(query_weight, kv_turned):
    return pl.pallas_call(
        pack_kernel,
        out_shape=jax.ShapeDtypeStruct((896, 128), BF),
        in_specs=[whole(0)] * 2,
        out_specs=whole(0),
        compiler_params=pltpu.CompilerParams(vmem_limit_bytes=32 * 2**20),
        cost_estimate=pl.CostEstimate(flops=0, bytes_accessed=460000, transcendentals=0),
    )(query_weight, kv_turned)


def project_kernel(x_ref, a0, b0, a1, b1, out_ref, own_ref):
    q_columns = []
    kv_rows = []
    for pair in ((a0, b0), (a1, b1)):
        for h in range(3):
            q_columns.append(
                jnp.concatenate([ref[a, 256 * h : 256 * h + 256, :] for ref in pair for a in (0, 1)], axis=0)
            )
        kv_rows.append(
            jnp.concatenate(
                [ref[a, 768 + 64 * h : 832 + 64 * h, :] for ref in pair for a in (0, 1) for h in (0, 1)], axis=1
            )
        )
    inputs = x_ref[...]
    q = jnp.dot(inputs, jnp.concatenate(q_columns, axis=1), preferred_element_type=F32)
    kv = lax.dot_general(
        inputs, jnp.concatenate(kv_rows, axis=0), (((1,), (1,)), ((), ())), preferred_element_type=F32
    )
    own_ref[:, :768] = q[:ROWS]
    own_ref[:, 768:] = kv[:ROWS]
    for e in (1, 2, 3):
        out_ref[e - 1, :, :768] = q[ROWS * e : ROWS * e + ROWS].astype(BF)
        out_ref[e - 1, :, 768:] = kv[ROWS * e : ROWS * e + ROWS].astype(BF)


def project(inputs, first, second):
    return pl.pallas_call(
        project_kernel,
        out_shape=(jax.ShapeDtypeStruct((3, ROWS, 896), BF), jax.ShapeDtypeStruct((ROWS, 896), F32)),
        in_specs=[whole(0)] * 5,
        out_specs=(whole(0),) * 2,
        compiler_params=pltpu.CompilerParams(vmem_limit_bytes=32 * 2**20),
        cost_estimate=pl.CostEstimate(flops=2 * 512 * 1024 * 896, bytes_accessed=4000000, transcendentals=0),
    )(inputs, *first, *second)


def attend(query, keys, values, limit, first):
    scores = jnp.einsum("qhd,kd->hqk", query, keys, preferred_element_type=F32) * HD ** (-0.5)
    keys_at = jnp.arange(ROWS, dtype=jnp.int32)
    rows_at = first + jnp.arange(32, dtype=jnp.int32)
    valid = (keys_at[None, :] <= rows_at[:, None]) & (keys_at[None, :] < limit)
    scores = jnp.where(valid[None], scores, -jnp.inf)
    raised = jnp.exp(scores - jnp.max(scores, axis=-1, keepdims=True))
    weights = (raised / jnp.sum(raised, axis=-1, keepdims=True)).astype(BF)
    output = jnp.einsum("hqk,kd->qhd", weights, values, preferred_element_type=F32)
    return jnp.where((rows_at < limit)[:, None, None], output, 0.0).astype(BF)


def body(tokens, norm_gain, query_weight, kv_weight, out_weight, lengths):
    y, zh, x, c, t = (lax.axis_index(name) for name in AXES)

    packed = pack(query_weight, kv_weight.T)
    near = move(packed, lambda y, zh, x, c, t: (x ^ y, zh, t, c, y))
    far = move(packed, lambda y, zh, x, c, t: (x ^ y, zh ^ 1, t, c, y))
    mine = jnp.stack([near, far])
    blocks = [mine] + [swap(mine, "x", d) for d in (1, 2, 3)]
    pairs = [(block, swap(block, "core", 1)) for block in blocks]

    wo_near = move(out_weight, lambda y, zh, x, c, t: (y, c, 2 * zh + (x >> 1), x & 1, t))
    wo_far = move(out_weight, lambda y, zh, x, c, t: (y, 1 - c, 2 * zh + (x >> 1), x & 1, t))
    wo_piece = jnp.concatenate([pick(zh == 1, wo_near, wo_far), pick(zh == 1, wo_far, wo_near)], axis=0)
    wo = lax.all_gather(wo_piece, ("y", "x", "core"), axis=0, tiled=True)

    widened = tokens.astype(F32)
    squares = jnp.sum(widened * widened, axis=1)
    gained = (widened * norm_gain[None, :]).astype(BF)

    def features(d):
        s = y ^ d ^ t
        picked = [
            lax.dynamic_slice(gained, (0, (((zh ^ a) * 4 + s) * 2 + (c ^ b)) * 256), (ROWS, 256))
            for b in (0, 1)
            for a in (0, 1)
        ]
        return jnp.concatenate(picked, axis=1)

    inputs = jnp.concatenate([features(0)] + [swap(features(d), "y", d) for d in (1, 2, 3)], axis=0)

    squares, _ = lax.optimization_barrier((squares, inputs))
    total = squares
    for d in (1, 2, 3):
        total = total + swap(squares, "zl", d)
    scales = lax.rsqrt(total / D + 1e-05)

    q_sums, kv_sums = [], []
    for first, second in ((0, 1), (2, 3)):
        sent, summed = project(inputs, pairs[first], pairs[second])
        for d in (1, 2, 3):
            summed = summed + swap(sent[d - 1], "y", d).astype(F32)
        q_sums.append(summed[:, :768])
        kv_sums.append(summed[:, 768:])
    q_sum = jnp.concatenate(q_sums, axis=1)
    kv_sum = jnp.concatenate(kv_sums, axis=1)

    kv_short = kv_sum.astype(BF)
    kv_flat = jnp.concatenate([kv_short[32 * r : 32 * r + 32] for r in range(4)], axis=1)

    def rows_for(d):
        return lax.dynamic_slice(q_sum, ((t ^ d) * 32, 0), (32, 1536))

    q_raw, kv_raw = rows_for(0), kv_sum
    for d in (1, 2, 3):
        came = swap(jnp.concatenate([rows_for(d).astype(BF), kv_flat], axis=1), "zl", d).astype(F32)
        q_raw = q_raw + came[:, :1536]
        kv_raw = kv_raw + jnp.concatenate([came[:, 1536 + 256 * r : 1792 + 256 * r] for r in range(4)], axis=0)

    limit = lengths[0]
    kv = (kv_raw * scales[:, None]).astype(BF)
    kv = by_index([kv[:, 64 * d : 64 * d + 64] for d in range(4)], x)
    keys = rotate(jnp.concatenate(kv[:2], axis=1).astype(F32), COSINE, SINE).astype(BF)
    values = jnp.concatenate(kv[2:], axis=1)
    mine_rows = [lax.dynamic_slice(table, (t * 32, 0), (32, HD)) for table in (COSINE, SINE)]
    scale_here = lax.dynamic_slice(scales, (t * 32,), (32,))
    query = rotate((q_raw * scale_here[:, None]).reshape(32, 12, HD), *mine_rows).astype(BF)
    attended = attend(query, keys, values, limit, t * 32).reshape(32, 1536)
    attended = jnp.concatenate(by_index([attended[:, 384 * d : 384 * d + 384] for d in range(4)], x), axis=1)

    got = [attended] + [swap(attended, "zl", d) for d in (1, 2, 3)]
    all_rows = jnp.concatenate(by_index(got, t), axis=0)
    return jnp.dot(all_rows, wo, preferred_element_type=F32).astype(BF)


def solution(mesh):
    fine = Mesh(mesh.devices.reshape(SIZES), AXES)
    rows = ("y", "zh", "x", "core")
    placed = (P(rows, "zl"), P("zl"), P(rows, "zl"), P(rows, "zl"), P(rows, "zl"), P(rows))
    return jax.shard_map(body, mesh=fine, in_specs=placed, out_specs=P(rows, "zl"), check_vma=False)
```

```python
import math

import jax
import jax.numpy as jnp
import numpy as np
from jax import lax
from jax.experimental import pallas as pl
from jax.experimental.pallas import tpu as pltpu
from jax.sharding import Mesh
from jax.sharding import PartitionSpec as P

AXES = ("y", "zh", "x", "core", "zl")
SIZES = (4, 2, 4, 2, 4)
D = 16384
HD = 128
ROWS = 128
BF = jnp.bfloat16
F32 = jnp.float32


def flat(*coords):
    index = 0
    for size, coord in zip(SIZES, coords):
        index = index * size + coord
    return index


def every():
    for y in range(4):
        for zh in range(2):
            for x in range(4):
                for c in range(2):
                    for t in range(4):
                        yield y, zh, x, c, t


def swap(value, axis, d):
    n = SIZES[AXES.index(axis)]
    return lax.ppermute(value, axis, [(i, i ^ d) for i in range(n)])


def move(value, where):
    return lax.ppermute(value, AXES, [(flat(*at), flat(*where(*at))) for at in every()])


def tables():
    freqs = np.exp(np.arange(HD // 2, dtype=np.float32) * np.float32(-2.0 * math.log(500000.0) / HD))
    angle = np.arange(ROWS, dtype=np.float32)[:, None] * freqs.astype(np.float32)[None, :]
    cosine = np.repeat(np.cos(angle), 2, axis=1).astype(np.float32)
    sine = np.repeat(np.sin(angle), 2, axis=1).astype(np.float32)
    sine[:, 0::2] *= -1.0
    return cosine, sine


COSINE, SINE = tables()


def order_of(zh):
    order = np.arange(384).reshape(2, 8, 24)
    order = np.stack([order[zh], order[1 - zh]], axis=1).reshape(384)
    return np.eye(384, dtype=np.float32)[:, order].astype(jnp.bfloat16)


ORDER = (order_of(0), order_of(1))


def rotate(values, cosine, sine):
    shape = (values.shape[0],) + (1,) * (values.ndim - 2) + (HD,)
    even = jnp.arange(HD) % 2 == 0
    partner = jnp.where(even, jnp.roll(values, -1, axis=-1), jnp.roll(values, 1, axis=-1))
    return values * cosine.reshape(shape) + partner * sine.reshape(shape)


def pick(flag, first, second):
    return jnp.where(flag, second, first)


def by_index(parts, at):
    odd = (at & 1) == 1
    high = (at >> 1) == 1
    a, b = pick(odd, parts[0], parts[1]), pick(odd, parts[1], parts[0])
    c, d = pick(odd, parts[2], parts[3]), pick(odd, parts[3], parts[2])
    return [pick(high, a, c), pick(high, b, d), pick(high, c, a), pick(high, d, b)]


def whole(shape):
    return pl.BlockSpec(memory_space=pltpu.VMEM)


def pack_kernel(q_ref, kv_ref, out_ref):
    for h in range(3):
        out_ref[256 * h : 256 * h + 256, :] = q_ref[:, 128 * h : 128 * h + 128]
    for h in range(2):
        out_ref[768 + 64 * h : 832 + 64 * h, :] = kv_ref[:, 128 * h : 128 * h + 128]


def pack(query_weight, kv_turned):
    return pl.pallas_call(
        pack_kernel,
        out_shape=jax.ShapeDtypeStruct((896, 128), BF),
        in_specs=[whole(0)] * 2,
        out_specs=whole(0),
        compiler_params=pltpu.CompilerParams(vmem_limit_bytes=32 * 2**20),
        cost_estimate=pl.CostEstimate(flops=0, bytes_accessed=460000, transcendentals=0),
    )(query_weight, kv_turned)


def project_kernel(x_ref, a0, b0, a1, b1, out_ref, own_ref):
    q_columns = []
    kv_rows = []
    for pair in ((a0, b0), (a1, b1)):
        for h in range(3):
            q_columns.append(
                jnp.concatenate([ref[a, 256 * h : 256 * h + 256, :] for ref in pair for a in (0, 1)], axis=0)
            )
        kv_rows.append(
            jnp.concatenate(
                [ref[a, 768 + 64 * h : 832 + 64 * h, :] for ref in pair for a in (0, 1) for h in (0, 1)], axis=1
            )
        )
    inputs = x_ref[...]
    q = jnp.dot(inputs, jnp.concatenate(q_columns, axis=1), preferred_element_type=F32)
    kv = lax.dot_general(
        inputs, jnp.concatenate(kv_rows, axis=0), (((1,), (1,)), ((), ())), preferred_element_type=F32
    )
    own_ref[:, :768] = q[:ROWS]
    own_ref[:, 768:] = kv[:ROWS]
    for e in (1, 2, 3):
        at = ROWS * e
        for half in (0, 1):
            to = half ^ (e & 1)
            out_ref[e - 1, :, 384 * to : 384 * to + 384] = q[at : at + ROWS, 384 * half : 384 * half + 384].astype(BF)
            out_ref[e - 1, :, 768 + 64 * to : 832 + 64 * to] = kv[at : at + ROWS, 64 * half : 64 * half + 64].astype(BF)


def project(inputs, first, second):
    return pl.pallas_call(
        project_kernel,
        out_shape=(jax.ShapeDtypeStruct((3, ROWS, 896), BF), jax.ShapeDtypeStruct((ROWS, 896), F32)),
        in_specs=[whole(0)] * 5,
        out_specs=(whole(0),) * 2,
        compiler_params=pltpu.CompilerParams(vmem_limit_bytes=32 * 2**20),
        cost_estimate=pl.CostEstimate(flops=2 * 512 * 1024 * 896, bytes_accessed=4000000, transcendentals=0),
    )(inputs, *first, *second)


def attend(query, keys, values, limit, first):
    scores = jnp.einsum("qhd,kd->hqk", query, keys, preferred_element_type=F32) * HD ** (-0.5)
    keys_at = jnp.arange(ROWS, dtype=jnp.int32)
    rows_at = first + jnp.arange(32, dtype=jnp.int32)
    valid = (keys_at[None, :] <= rows_at[:, None]) & (keys_at[None, :] < limit)
    scores = jnp.where(valid[None], scores, -jnp.inf)
    raised = jnp.exp(scores - jnp.max(scores, axis=-1, keepdims=True))
    weights = (raised / jnp.sum(raised, axis=-1, keepdims=True)).astype(BF)
    output = jnp.einsum("hqk,kd->qhd", weights, values, preferred_element_type=F32)
    return jnp.where((rows_at < limit)[:, None, None], output, 0.0).astype(BF)


def body(tokens, norm_gain, query_weight, kv_weight, out_weight, lengths):
    y, zh, x, c, t = (lax.axis_index(name) for name in AXES)

    packed = pack(query_weight, kv_weight.T)
    near = move(packed, lambda y, zh, x, c, t: (x ^ y, zh, t ^ x, c, y))
    far = move(packed, lambda y, zh, x, c, t: (x ^ y, zh ^ 1, t ^ x, c, y))
    wo_other, near, far = lax.optimization_barrier((swap(out_weight, "zh", 1), near, far))
    wo_piece = jnp.concatenate([out_weight, wo_other], axis=0)
    wo = lax.all_gather(wo_piece, ("y", "x", "core"), axis=0, tiled=True)

    mine = jnp.stack([near, far])
    blocks = [mine] + [swap(mine, "x", d) for d in (1, 2, 3)]
    pairs = [(block, swap(block, "core", 1)) for block in blocks]

    widened = tokens.astype(F32)
    squares = jnp.sum(widened * widened, axis=1)
    gained = (widened * norm_gain[None, :]).astype(BF)

    def features(d):
        s = y ^ d ^ t
        picked = [
            lax.dynamic_slice(gained, (0, (((zh ^ a) * 4 + s) * 2 + (c ^ b)) * 256), (ROWS, 256))
            for b in (0, 1)
            for a in (0, 1)
        ]
        return jnp.concatenate(picked, axis=1)

    inputs = jnp.concatenate([features(0)] + [swap(features(d), "y", d) for d in (1, 2, 3)], axis=0)

    sent_a, own_a = project(inputs, pairs[0], pairs[1])
    sent_b, own_b = project(inputs, pairs[2], pairs[3])
    got_a = [swap(sent_a[d - 1], "y", d) for d in (1, 2, 3)]
    got_b = [swap(sent_b[d - 1], "y", d) for d in (1, 2, 3)]
    summed = [
        own + sum(part.astype(F32) for part in parts)
        for own, parts in ((own_a, (got_a[0], got_b[1], got_b[2])), (own_b, (got_b[0], got_a[1], got_a[2])))
    ]
    base = x ^ y ^ t
    q_sum = jnp.concatenate(by_index([half[:, at : at + 384] for half in summed for at in (0, 384)], base), axis=1)
    kv_sum = jnp.concatenate(by_index([half[:, at : at + 64] for half in summed for at in (768, 832)], base), axis=1)

    kv_short = kv_sum.astype(BF)
    high = lax.reduce_precision(squares, 8, 7)
    middle = lax.reduce_precision(squares - high, 8, 7)
    low = squares - high - middle
    note = jnp.pad(jnp.stack([high, middle, low]), ((0, 29), (0, 0))).astype(BF)
    shared = jnp.concatenate([kv_short[32 * r : 32 * r + 32] for r in range(4)] + [note], axis=1)

    def rows_for(d):
        return lax.dynamic_slice(q_sum, ((t ^ d) * 32, 0), (32, 1536))

    q_raw, kv_raw, total = rows_for(0), kv_sum, squares
    for d in (1, 2, 3):
        came = swap(jnp.concatenate([rows_for(d).astype(BF), shared], axis=1), "zl", d).astype(F32)
        q_raw = q_raw + came[:, :1536]
        kv_raw = kv_raw + jnp.concatenate([came[:, 1536 + 256 * r : 1792 + 256 * r] for r in range(4)], axis=0)
        total = total + ((came[2, 2560:] + came[1, 2560:]) + came[0, 2560:])
    scales = lax.rsqrt(total / D + 1e-05)

    limit = lengths[0]
    kv = (kv_raw * scales[:, None]).astype(BF)
    keys = rotate(kv[:, :HD].astype(F32), COSINE, SINE).astype(BF)
    values = kv[:, HD:]
    mine_rows = [lax.dynamic_slice(table, (t * 32, 0), (32, HD)) for table in (COSINE, SINE)]
    scale_here = lax.dynamic_slice(scales, (t * 32,), (32,))
    query = rotate((q_raw * scale_here[:, None]).reshape(32, 12, HD), *mine_rows).astype(BF)
    attended = attend(query, keys, values, limit, t * 32).reshape(32, 1536)
    stacked = jnp.concatenate([attended[:, 384 * d : 384 * d + 384] for d in range(4)], axis=0)
    stacked = jnp.dot(stacked, pick(zh == 1, ORDER[0], ORDER[1]), preferred_element_type=F32).astype(BF)
    attended = jnp.concatenate([stacked[32 * d : 32 * d + 32] for d in range(4)], axis=1)

    got = [attended] + [swap(attended, "zl", d) for d in (1, 2, 3)]
    all_rows = jnp.concatenate(by_index(got, t), axis=0)
    return jnp.dot(all_rows, wo, preferred_element_type=F32).astype(BF)


def solution(mesh):
    fine = Mesh(mesh.devices.reshape(SIZES), AXES)
    rows = ("y", "zh", "x", "core")
    placed = (P(rows, "zl"), P("zl"), P(rows, "zl"), P(rows, "zl"), P(rows, "zl"), P(rows))
    return jax.shard_map(body, mesh=fine, in_specs=placed, out_specs=P(rows, "zl"), check_vma=False)
```

```python
import math

import jax
import jax.numpy as jnp
import numpy as np
from jax import lax
from jax.experimental import pallas as pl
from jax.experimental.pallas import tpu as pltpu
from jax.sharding import Mesh
from jax.sharding import PartitionSpec as P

AXES = ("y", "zh", "x", "core", "zl")
SIZES = (4, 2, 4, 2, 4)
D = 16384
HD = 128
ROWS = 128
BF = jnp.bfloat16
F32 = jnp.float32


def flat(*coords):
    index = 0
    for size, coord in zip(SIZES, coords):
        index = index * size + coord
    return index


def every():
    for y in range(4):
        for zh in range(2):
            for x in range(4):
                for c in range(2):
                    for t in range(4):
                        yield y, zh, x, c, t


def swap(value, axis, d):
    n = SIZES[AXES.index(axis)]
    return lax.ppermute(value, axis, [(i, i ^ d) for i in range(n)])


def move(value, where):
    return lax.ppermute(value, AXES, [(flat(*at), flat(*where(*at))) for at in every()])


def tables():
    freqs = np.exp(np.arange(HD // 2, dtype=np.float32) * np.float32(-2.0 * math.log(500000.0) / HD))
    angle = np.arange(ROWS, dtype=np.float32)[:, None] * freqs.astype(np.float32)[None, :]
    cosine = np.repeat(np.cos(angle), 2, axis=1).astype(np.float32)
    sine = np.repeat(np.sin(angle), 2, axis=1).astype(np.float32)
    sine[:, 0::2] *= -1.0
    return cosine, sine


COSINE, SINE = tables()


def order_of(zh):
    order = np.arange(384).reshape(2, 8, 24)
    order = np.stack([order[zh], order[1 - zh]], axis=1).reshape(384)
    return np.eye(384, dtype=np.float32)[:, order].astype(jnp.bfloat16)


ORDER = (order_of(0), order_of(1))


def rotate(values, cosine, sine):
    shape = (values.shape[0],) + (1,) * (values.ndim - 2) + (HD,)
    even = jnp.arange(HD) % 2 == 0
    partner = jnp.where(even, jnp.roll(values, -1, axis=-1), jnp.roll(values, 1, axis=-1))
    return values * cosine.reshape(shape) + partner * sine.reshape(shape)


def pick(flag, first, second):
    return jnp.where(flag, second, first)


def by_index(parts, at):
    odd = (at & 1) == 1
    high = (at >> 1) == 1
    a, b = pick(odd, parts[0], parts[1]), pick(odd, parts[1], parts[0])
    c, d = pick(odd, parts[2], parts[3]), pick(odd, parts[3], parts[2])
    return [pick(high, a, c), pick(high, b, d), pick(high, c, a), pick(high, d, b)]


def whole(shape):
    return pl.BlockSpec(memory_space=pltpu.VMEM)


def pack_kernel(q_ref, kv_ref, out_ref):
    for h in range(3):
        out_ref[256 * h : 256 * h + 256, :] = q_ref[:, 128 * h : 128 * h + 128]
    for h in range(2):
        out_ref[768 + 64 * h : 832 + 64 * h, :] = kv_ref[:, 128 * h : 128 * h + 128]


def pack(query_weight, kv_turned):
    return pl.pallas_call(
        pack_kernel,
        out_shape=jax.ShapeDtypeStruct((896, 128), BF),
        in_specs=[whole(0)] * 2,
        out_specs=whole(0),
        compiler_params=pltpu.CompilerParams(vmem_limit_bytes=32 * 2**20),
        cost_estimate=pl.CostEstimate(flops=0, bytes_accessed=460000, transcendentals=0),
    )(query_weight, kv_turned)


def project_kernel(x_ref, here_ref, there_ref, out_ref, own_ref):
    inputs = x_ref[...]
    for slot, ref in enumerate((here_ref, there_ref)):
        heads = [
            jnp.concatenate([ref[d, 256 * h : 256 * h + 256, :] for d in range(4)], axis=0) for h in range(3)
        ]
        q = jnp.dot(inputs, jnp.concatenate(heads, axis=1), preferred_element_type=F32)
        own_ref[:, 384 * slot : 384 * slot + 384] = q[:ROWS]
        for e in (1, 2, 3):
            out_ref[e - 1, :, 384 * slot : 384 * slot + 384] = q[ROWS * e : ROWS * e + ROWS].astype(BF)
    kv_rows = [
        jnp.concatenate([ref[d, 768 + 64 * h : 832 + 64 * h, :] for d in range(4) for h in (0, 1)], axis=1)
        for ref in (here_ref, there_ref)
    ]
    kv = lax.dot_general(
        inputs, jnp.concatenate(kv_rows, axis=0), (((1,), (1,)), ((), ())), preferred_element_type=F32
    )
    own_ref[:, 768:] = kv[:ROWS]
    for e in (1, 2, 3):
        out_ref[e - 1, :, 768:] = kv[ROWS * e : ROWS * e + ROWS].astype(BF)


def project(inputs, here, there):
    return pl.pallas_call(
        project_kernel,
        out_shape=(jax.ShapeDtypeStruct((3, ROWS, 896), BF), jax.ShapeDtypeStruct((ROWS, 896), F32)),
        in_specs=[whole(0)] * 3,
        out_specs=(whole(0),) * 2,
        compiler_params=pltpu.CompilerParams(vmem_limit_bytes=32 * 2**20),
        cost_estimate=pl.CostEstimate(flops=2 * 512 * 1024 * 896, bytes_accessed=4000000, transcendentals=0),
    )(inputs, here, there)


def attend(query, keys, values, limit, first):
    scores = jnp.einsum("qhd,kd->hqk", query, keys, preferred_element_type=F32) * HD ** (-0.5)
    keys_at = jnp.arange(ROWS, dtype=jnp.int32)
    rows_at = first + jnp.arange(32, dtype=jnp.int32)
    valid = (keys_at[None, :] <= rows_at[:, None]) & (keys_at[None, :] < limit)
    scores = jnp.where(valid[None], scores, -jnp.inf)
    raised = jnp.exp(scores - jnp.max(scores, axis=-1, keepdims=True))
    weights = (raised / jnp.sum(raised, axis=-1, keepdims=True)).astype(BF)
    output = jnp.einsum("hqk,kd->qhd", weights, values, preferred_element_type=F32)
    return jnp.where((rows_at < limit)[:, None, None], output, 0.0).astype(BF)


def body(tokens, norm_gain, query_weight, kv_weight, out_weight, lengths):
    y, zh, x, c, t = (lax.axis_index(name) for name in AXES)

    packed = pack(query_weight, kv_weight.T)
    first = move(packed, lambda y, zh, x, c, t: ((2 * zh + c) ^ y, t & 1, x, t >> 1, y))
    wo_other = swap(out_weight, "zh", 1)

    widened = tokens.astype(F32)
    squares = jnp.sum(widened * widened, axis=1)
    gained = (widened * norm_gain[None, :]).astype(BF)

    def features(e):
        s = y ^ e ^ t
        picked = [
            lax.dynamic_slice(gained, (0, (((s >> 1) * 4 + (x ^ d)) * 2 + (s & 1)) * 256), (ROWS, 256))
            for d in range(4)
        ]
        return jnp.concatenate(picked, axis=1)

    ring = [swap(features(e), "y", e) for e in (1, 2, 3)]
    first, wo_other, packed, *ring = lax.optimization_barrier((first, wo_other, packed, *ring))
    second = move(packed, lambda y, zh, x, c, t: ((2 * zh + c) ^ y, 1 - (t & 1), x, t >> 1, y))
    inputs = jnp.concatenate([features(0)] + ring, axis=0)

    wo_piece = jnp.concatenate([out_weight, wo_other], axis=0)
    wo = lax.all_gather(wo_piece, ("y", "x", "core"), axis=0, tiled=True)

    summed = []
    for block in (first, second):
        here = jnp.stack([block] + [swap(block, "x", d) for d in (1, 2, 3)])
        sent, total = project(inputs, here, swap(here, "core", 1))
        for e in (1, 2, 3):
            total = total + swap(sent[e - 1], "y", e).astype(F32)
        summed.append(total)
    base = 2 * c + zh
    q_slots = [half[:, at : at + 384] for at in (0, 384) for half in summed]
    kv_slots = [half[:, at : at + 64] for at in (768, 832) for half in summed]
    q_sum = jnp.concatenate(by_index(q_slots, base), axis=1)
    kv_sum = jnp.concatenate(by_index(kv_slots, base), axis=1)

    kv_short = kv_sum.astype(BF)
    high = lax.reduce_precision(squares, 8, 7)
    middle = lax.reduce_precision(squares - high, 8, 7)
    low = squares - high - middle
    note = jnp.pad(jnp.stack([high, middle, low]), ((0, 29), (0, 0))).astype(BF)
    shared = jnp.concatenate([kv_short[32 * r : 32 * r + 32] for r in range(4)] + [note], axis=1)

    def rows_for(d):
        return lax.dynamic_slice(q_sum, ((t ^ d) * 32, 0), (32, 1536))

    q_raw, kv_raw, total = rows_for(0), kv_sum, squares
    for d in (1, 2, 3):
        came = swap(jnp.concatenate([rows_for(d).astype(BF), shared], axis=1), "zl", d).astype(F32)
        q_raw = q_raw + came[:, :1536]
        kv_raw = kv_raw + jnp.concatenate([came[:, 1536 + 256 * r : 1792 + 256 * r] for r in range(4)], axis=0)
        total = total + ((came[2, 2560:] + came[1, 2560:]) + came[0, 2560:])
    scales = lax.rsqrt(total / D + 1e-05)

    limit = lengths[0]
    kv = (kv_raw * scales[:, None]).astype(BF)
    keys = rotate(kv[:, :HD].astype(F32), COSINE, SINE).astype(BF)
    values = kv[:, HD:]
    mine_rows = [lax.dynamic_slice(table, (t * 32, 0), (32, HD)) for table in (COSINE, SINE)]
    scale_here = lax.dynamic_slice(scales, (t * 32,), (32,))
    query = rotate((q_raw * scale_here[:, None]).reshape(32, 12, HD), *mine_rows).astype(BF)
    attended = attend(query, keys, values, limit, t * 32).reshape(32, 1536)
    stacked = jnp.concatenate([attended[:, 384 * d : 384 * d + 384] for d in range(4)], axis=0)
    stacked = jnp.dot(stacked, pick(zh == 1, ORDER[0], ORDER[1]), preferred_element_type=F32).astype(BF)
    attended = jnp.concatenate([stacked[32 * d : 32 * d + 32] for d in range(4)], axis=1)

    got = [attended] + [swap(attended, "zl", d) for d in (1, 2, 3)]
    all_rows = jnp.concatenate(by_index(got, t), axis=0)
    return jnp.dot(all_rows, wo, preferred_element_type=F32).astype(BF)


def solution(mesh):
    fine = Mesh(mesh.devices.reshape(SIZES), AXES)
    rows = ("y", "zh", "x", "core")
    placed = (P(rows, "zl"), P("zl"), P(rows, "zl"), P(rows, "zl"), P(rows, "zl"), P(rows))
    return jax.shard_map(body, mesh=fine, in_specs=placed, out_specs=P(rows, "zl"), check_vma=False)
```

```python
import math

import jax
import jax.numpy as jnp
import numpy as np
from jax import lax
from jax.experimental import pallas as pl
from jax.experimental.pallas import tpu as pltpu
from jax.sharding import Mesh
from jax.sharding import PartitionSpec as P

AXES = ("y", "zh", "x", "core", "zl")
SIZES = (4, 2, 4, 2, 4)
D = 16384
HD = 128
ROWS = 128
BF = jnp.bfloat16
F32 = jnp.float32


def flat(*coords):
    index = 0
    for size, coord in zip(SIZES, coords):
        index = index * size + coord
    return index


def every():
    for y in range(4):
        for zh in range(2):
            for x in range(4):
                for c in range(2):
                    for t in range(4):
                        yield y, zh, x, c, t


def swap(value, axis, d):
    n = SIZES[AXES.index(axis)]
    return lax.ppermute(value, axis, [(i, i ^ d) for i in range(n)])


def move(value, where):
    return lax.ppermute(value, AXES, [(flat(*at), flat(*where(*at))) for at in every()])


def tables():
    freqs = np.exp(np.arange(HD // 2, dtype=np.float32) * np.float32(-2.0 * math.log(500000.0) / HD))
    angle = np.arange(ROWS, dtype=np.float32)[:, None] * freqs.astype(np.float32)[None, :]
    cosine = np.repeat(np.cos(angle), 2, axis=1).astype(np.float32)
    sine = np.repeat(np.sin(angle), 2, axis=1).astype(np.float32)
    sine[:, 0::2] *= -1.0
    return cosine, sine


COSINE, SINE = tables()


def order_of(zh):
    order = np.arange(384).reshape(2, 8, 24)
    order = np.stack([order[zh], order[1 - zh]], axis=1).reshape(384)
    return np.eye(384, dtype=np.float32)[:, order].astype(jnp.bfloat16)


ORDER = (order_of(0), order_of(1))


def rotate(values, cosine, sine):
    shape = (values.shape[0],) + (1,) * (values.ndim - 2) + (HD,)
    even = jnp.arange(HD) % 2 == 0
    partner = jnp.where(even, jnp.roll(values, -1, axis=-1), jnp.roll(values, 1, axis=-1))
    return values * cosine.reshape(shape) + partner * sine.reshape(shape)


def pick(flag, first, second):
    return jnp.where(flag, second, first)


def by_index(parts, at):
    odd = (at & 1) == 1
    high = (at >> 1) == 1
    a, b = pick(odd, parts[0], parts[1]), pick(odd, parts[1], parts[0])
    c, d = pick(odd, parts[2], parts[3]), pick(odd, parts[3], parts[2])
    return [pick(high, a, c), pick(high, b, d), pick(high, c, a), pick(high, d, b)]


def whole(shape):
    return pl.BlockSpec(memory_space=pltpu.VMEM)


def pack_kernel(q_ref, kv_ref, out_ref):
    for h in range(3):
        out_ref[256 * h : 256 * h + 256, :] = q_ref[:, 128 * h : 128 * h + 128]
    for h in range(2):
        out_ref[768 + 64 * h : 832 + 64 * h, :] = kv_ref[:, 128 * h : 128 * h + 128]


def pack(query_weight, kv_turned):
    return pl.pallas_call(
        pack_kernel,
        out_shape=jax.ShapeDtypeStruct((896, 128), BF),
        in_specs=[whole(0)] * 2,
        out_specs=whole(0),
        compiler_params=pltpu.CompilerParams(vmem_limit_bytes=32 * 2**20),
        cost_estimate=pl.CostEstimate(flops=0, bytes_accessed=460000, transcendentals=0),
    )(query_weight, kv_turned)


def project_kernel(x_ref, here_ref, there_ref, out_ref, own_ref):
    inputs = x_ref[...]
    for slot, ref in enumerate((here_ref, there_ref)):
        heads = [
            jnp.concatenate([ref[d, 256 * h : 256 * h + 256, :] for d in range(4)], axis=0) for h in range(3)
        ]
        q = jnp.dot(inputs, jnp.concatenate(heads, axis=1), preferred_element_type=F32)
        own_ref[:, 384 * slot : 384 * slot + 384] = q[:ROWS]
        for e in (1, 2, 3):
            out_ref[e - 1, :, 384 * slot : 384 * slot + 384] = q[ROWS * e : ROWS * e + ROWS].astype(BF)
    kv_rows = [
        jnp.concatenate([ref[d, 768 + 64 * h : 832 + 64 * h, :] for d in range(4) for h in (0, 1)], axis=1)
        for ref in (here_ref, there_ref)
    ]
    kv = lax.dot_general(
        inputs, jnp.concatenate(kv_rows, axis=0), (((1,), (1,)), ((), ())), preferred_element_type=F32
    )
    own_ref[:, 768:] = kv[:ROWS]
    for e in (1, 2, 3):
        out_ref[e - 1, :, 768:] = kv[ROWS * e : ROWS * e + ROWS].astype(BF)


def project(inputs, here, there):
    return pl.pallas_call(
        project_kernel,
        out_shape=(jax.ShapeDtypeStruct((3, ROWS, 896), BF), jax.ShapeDtypeStruct((ROWS, 896), F32)),
        in_specs=[whole(0)] * 3,
        out_specs=(whole(0),) * 2,
        compiler_params=pltpu.CompilerParams(vmem_limit_bytes=32 * 2**20),
        cost_estimate=pl.CostEstimate(flops=2 * 512 * 1024 * 896, bytes_accessed=4000000, transcendentals=0),
    )(inputs, here, there)


def mix_kernel(x_ref, w_ref, out_ref):
    out_ref[...] = jnp.dot(x_ref[...], w_ref[...], preferred_element_type=F32).astype(BF)


def mix(attended, weight):
    columns = weight.shape[1]
    return pl.pallas_call(
        mix_kernel,
        out_shape=jax.ShapeDtypeStruct((ROWS, columns), BF),
        grid=(columns // 512,),
        in_specs=[
            pl.BlockSpec((ROWS, 1536), lambda i: (0, 0)),
            pl.BlockSpec((1536, 512), lambda i: (0, i)),
        ],
        out_specs=pl.BlockSpec((ROWS, 512), lambda i: (0, i)),
        compiler_params=pltpu.CompilerParams(vmem_limit_bytes=32 * 2**20),
        cost_estimate=pl.CostEstimate(flops=2 * ROWS * 1536 * columns, bytes_accessed=14000000, transcendentals=0),
    )(attended, weight)


def attend(query, keys, values, limit, first):
    scores = jnp.einsum("qhd,kd->hqk", query, keys, preferred_element_type=F32) * HD ** (-0.5)
    keys_at = jnp.arange(ROWS, dtype=jnp.int32)
    rows_at = first + jnp.arange(32, dtype=jnp.int32)
    valid = (keys_at[None, :] <= rows_at[:, None]) & (keys_at[None, :] < limit)
    scores = jnp.where(valid[None], scores, -jnp.inf)
    raised = jnp.exp(scores - jnp.max(scores, axis=-1, keepdims=True))
    weights = (raised / jnp.sum(raised, axis=-1, keepdims=True)).astype(BF)
    output = jnp.einsum("hqk,kd->qhd", weights, values, preferred_element_type=F32)
    return jnp.where((rows_at < limit)[:, None, None], output, 0.0).astype(BF)


def body(tokens, norm_gain, query_weight, kv_weight, out_weight, lengths):
    y, zh, x, c, t = (lax.axis_index(name) for name in AXES)

    packed = pack(query_weight, kv_weight.T)
    first = move(packed, lambda y, zh, x, c, t: ((2 * zh + c) ^ y, t & 1, x, t >> 1, y))

    widened = tokens.astype(F32)
    squares = jnp.sum(widened * widened, axis=1)
    gained = (widened * norm_gain[None, :]).astype(BF)

    def features(e):
        s = y ^ e ^ t
        picked = [
            lax.dynamic_slice(gained, (0, (((s >> 1) * 4 + (x ^ d)) * 2 + (s & 1)) * 256), (ROWS, 256))
            for d in range(4)
        ]
        return jnp.concatenate(picked, axis=1)

    ring = [swap(features(e), "y", e) for e in (1, 2, 3)]
    first, packed, out_weight, *ring = lax.optimization_barrier((first, packed, out_weight, *ring))
    second = move(packed, lambda y, zh, x, c, t: ((2 * zh + c) ^ y, 1 - (t & 1), x, t >> 1, y))
    inputs = jnp.concatenate([features(0)] + ring, axis=0)

    wo_other = swap(out_weight, "zh", 1)
    first_blocks = [first] + [swap(first, "x", d) for d in (1, 2, 3)]
    wo_other, second, *first_blocks = lax.optimization_barrier((wo_other, second, *first_blocks))
    wo_piece = jnp.concatenate([out_weight, wo_other], axis=0)
    wo = lax.all_gather(wo_piece, ("y", "x", "core"), axis=0, tiled=True)

    summed = []
    for blocks in (first_blocks, [second] + [swap(second, "x", d) for d in (1, 2, 3)]):
        here = jnp.stack(blocks)
        sent, total = project(inputs, here, swap(here, "core", 1))
        for e in (1, 2, 3):
            total = total + swap(sent[e - 1], "y", e).astype(F32)
        summed.append(total)
    base = 2 * c + zh
    q_slots = [half[:, at : at + 384] for at in (0, 384) for half in summed]
    kv_slots = [half[:, at : at + 64] for at in (768, 832) for half in summed]
    q_sum = jnp.concatenate(by_index(q_slots, base), axis=1)
    kv_sum = jnp.concatenate(by_index(kv_slots, base), axis=1)

    kv_short = kv_sum.astype(BF)
    high = lax.reduce_precision(squares, 8, 7)
    middle = lax.reduce_precision(squares - high, 8, 7)
    low = squares - high - middle
    note = jnp.pad(jnp.stack([high, middle, low]), ((0, 29), (0, 0))).astype(BF)
    shared = jnp.concatenate([kv_short[32 * r : 32 * r + 32] for r in range(4)] + [note], axis=1)

    def rows_for(d):
        return lax.dynamic_slice(q_sum, ((t ^ d) * 32, 0), (32, 1536))

    q_raw, kv_raw, total = rows_for(0), kv_sum, squares
    for d in (1, 2, 3):
        came = swap(jnp.concatenate([rows_for(d).astype(BF), shared], axis=1), "zl", d).astype(F32)
        q_raw = q_raw + came[:, :1536]
        kv_raw = kv_raw + jnp.concatenate([came[:, 1536 + 256 * r : 1792 + 256 * r] for r in range(4)], axis=0)
        total = total + ((came[2, 2560:] + came[1, 2560:]) + came[0, 2560:])
    scales = lax.rsqrt(total / D + 1e-05)

    limit = lengths[0]
    kv = (kv_raw * scales[:, None]).astype(BF)
    keys = rotate(kv[:, :HD].astype(F32), COSINE, SINE).astype(BF)
    values = kv[:, HD:]
    mine_rows = [lax.dynamic_slice(table, (t * 32, 0), (32, HD)) for table in (COSINE, SINE)]
    scale_here = lax.dynamic_slice(scales, (t * 32,), (32,))
    query = rotate((q_raw * scale_here[:, None]).reshape(32, 12, HD), *mine_rows).astype(BF)
    attended = attend(query, keys, values, limit, t * 32).reshape(32, 1536)
    stacked = jnp.concatenate([attended[:, 384 * d : 384 * d + 384] for d in range(4)], axis=0)
    stacked = jnp.dot(stacked, pick(zh == 1, ORDER[0], ORDER[1]), preferred_element_type=F32).astype(BF)
    attended = jnp.concatenate([stacked[32 * d : 32 * d + 32] for d in range(4)], axis=1)

    got = [attended] + [swap(attended, "zl", d) for d in (1, 2, 3)]
    all_rows = jnp.concatenate(by_index(got, t), axis=0)
    return mix(all_rows, wo)


def solution(mesh):
    fine = Mesh(mesh.devices.reshape(SIZES), AXES)
    rows = ("y", "zh", "x", "core")
    placed = (P(rows, "zl"), P("zl"), P(rows, "zl"), P(rows, "zl"), P(rows, "zl"), P(rows))
    return jax.shard_map(body, mesh=fine, in_specs=placed, out_specs=P(rows, "zl"), check_vma=False)
```

```python
import math

import jax
import jax.numpy as jnp
import numpy as np
from jax import lax
from jax.experimental import pallas as pl
from jax.experimental.pallas import tpu as pltpu
from jax.sharding import Mesh
from jax.sharding import PartitionSpec as P

AXES = ("y", "zh", "x", "core", "zl")
SIZES = (4, 2, 4, 2, 4)
D = 16384
HD = 128
ROWS = 128
BF = jnp.bfloat16
F32 = jnp.float32


def flat(*coords):
    index = 0
    for size, coord in zip(SIZES, coords):
        index = index * size + coord
    return index


def every():
    for y in range(4):
        for zh in range(2):
            for x in range(4):
                for c in range(2):
                    for t in range(4):
                        yield y, zh, x, c, t


def swap(value, axis, d):
    n = SIZES[AXES.index(axis)]
    return lax.ppermute(value, axis, [(i, i ^ d) for i in range(n)])


def move(value, where):
    return lax.ppermute(value, AXES, [(flat(*at), flat(*where(*at))) for at in every()])


def tables():
    freqs = np.exp(np.arange(HD // 2, dtype=np.float32) * np.float32(-2.0 * math.log(500000.0) / HD))
    angle = np.arange(ROWS, dtype=np.float32)[:, None] * freqs.astype(np.float32)[None, :]
    cosine = np.repeat(np.cos(angle), 2, axis=1).astype(np.float32)
    sine = np.repeat(np.sin(angle), 2, axis=1).astype(np.float32)
    sine[:, 0::2] *= -1.0
    return cosine, sine


COSINE, SINE = tables()


def rotate(values, cosine, sine):
    shape = (values.shape[0],) + (1,) * (values.ndim - 2) + (HD,)
    even = jnp.arange(HD) % 2 == 0
    partner = jnp.where(even, jnp.roll(values, -1, axis=-1), jnp.roll(values, 1, axis=-1))
    return values * cosine.reshape(shape) + partner * sine.reshape(shape)


def pick(flag, first, second):
    return jnp.where(flag, second, first)


def by_index(parts, at):
    odd = (at & 1) == 1
    high = (at >> 1) == 1
    a, b = pick(odd, parts[0], parts[1]), pick(odd, parts[1], parts[0])
    c, d = pick(odd, parts[2], parts[3]), pick(odd, parts[3], parts[2])
    return [pick(high, a, c), pick(high, b, d), pick(high, c, a), pick(high, d, b)]


def whole(shape):
    return pl.BlockSpec(memory_space=pltpu.VMEM)


def pack_kernel(q_ref, kv_ref, out_ref):
    for h in range(3):
        out_ref[256 * h : 256 * h + 256, :] = q_ref[:, 128 * h : 128 * h + 128]
    for h in range(2):
        out_ref[768 + 64 * h : 832 + 64 * h, :] = kv_ref[:, 128 * h : 128 * h + 128]


def pack(query_weight, kv_turned):
    return pl.pallas_call(
        pack_kernel,
        out_shape=jax.ShapeDtypeStruct((896, 128), BF),
        in_specs=[whole(0)] * 2,
        out_specs=whole(0),
        compiler_params=pltpu.CompilerParams(vmem_limit_bytes=32 * 2**20),
        cost_estimate=pl.CostEstimate(flops=0, bytes_accessed=460000, transcendentals=0),
    )(query_weight, kv_turned)


def project_kernel(x_ref, here_ref, there_ref, out_ref, own_ref):
    inputs = x_ref[...]
    for slot, ref in enumerate((here_ref, there_ref)):
        heads = [
            jnp.concatenate([ref[d, 256 * h : 256 * h + 256, :] for d in range(4)], axis=0) for h in range(3)
        ]
        q = jnp.dot(inputs, jnp.concatenate(heads, axis=1), preferred_element_type=F32)
        own_ref[:, 384 * slot : 384 * slot + 384] = q[:ROWS]
        for e in (1, 2, 3):
            out_ref[e - 1, :, 384 * slot : 384 * slot + 384] = q[ROWS * e : ROWS * e + ROWS].astype(BF)
    kv_rows = [
        jnp.concatenate([ref[d, 768 + 64 * h : 832 + 64 * h, :] for d in range(4) for h in (0, 1)], axis=1)
        for ref in (here_ref, there_ref)
    ]
    kv = lax.dot_general(
        inputs, jnp.concatenate(kv_rows, axis=0), (((1,), (1,)), ((), ())), preferred_element_type=F32
    )
    own_ref[:, 768:] = kv[:ROWS]
    for e in (1, 2, 3):
        out_ref[e - 1, :, 768:] = kv[ROWS * e : ROWS * e + ROWS].astype(BF)


def project(inputs, here, there):
    return pl.pallas_call(
        project_kernel,
        out_shape=(jax.ShapeDtypeStruct((3, ROWS, 896), BF), jax.ShapeDtypeStruct((ROWS, 896), F32)),
        in_specs=[whole(0)] * 3,
        out_specs=(whole(0),) * 2,
        compiler_params=pltpu.CompilerParams(vmem_limit_bytes=32 * 2**20),
        cost_estimate=pl.CostEstimate(flops=2 * 512 * 1024 * 896, bytes_accessed=4000000, transcendentals=0),
    )(inputs, here, there)


def mix_kernel(x_ref, near_ref, far_ref, out_ref):
    out = jnp.dot(x_ref[:, :768], near_ref[...], preferred_element_type=F32)
    out_ref[...] = (out + jnp.dot(x_ref[:, 768:], far_ref[...], preferred_element_type=F32)).astype(BF)


def mix(attended, near, far):
    columns = near.shape[1]
    return pl.pallas_call(
        mix_kernel,
        out_shape=jax.ShapeDtypeStruct((ROWS, columns), BF),
        grid=(columns // 512,),
        in_specs=[
            pl.BlockSpec((ROWS, 1536), lambda i: (0, 0)),
            pl.BlockSpec((768, 512), lambda i: (0, i)),
            pl.BlockSpec((768, 512), lambda i: (0, i)),
        ],
        out_specs=pl.BlockSpec((ROWS, 512), lambda i: (0, i)),
        compiler_params=pltpu.CompilerParams(vmem_limit_bytes=58 * 2**20),
        cost_estimate=pl.CostEstimate(flops=2 * ROWS * 1536 * columns, bytes_accessed=14000000, transcendentals=0),
    )(attended, near, far)


def attend(query, keys, values, limit, first):
    scores = jnp.einsum("qhd,kd->hqk", query, keys, preferred_element_type=F32) * HD ** (-0.5)
    keys_at = jnp.arange(ROWS, dtype=jnp.int32)
    rows_at = first + jnp.arange(32, dtype=jnp.int32)
    valid = (keys_at[None, :] <= rows_at[:, None]) & (keys_at[None, :] < limit)
    scores = jnp.where(valid[None], scores, -jnp.inf)
    raised = jnp.exp(scores - jnp.max(scores, axis=-1, keepdims=True))
    weights = (raised / jnp.sum(raised, axis=-1, keepdims=True)).astype(BF)
    output = jnp.einsum("hqk,kd->qhd", weights, values, preferred_element_type=F32)
    return jnp.where((rows_at < limit)[:, None, None], output, 0.0).astype(BF)


def body(tokens, norm_gain, query_weight, kv_weight, out_weight, lengths):
    y, zh, x, c, t = (lax.axis_index(name) for name in AXES)

    packed = pack(query_weight, kv_weight.T)
    first = move(packed, lambda y, zh, x, c, t: ((2 * zh + c) ^ y, t & 1, x, t >> 1, y))

    widened = tokens.astype(F32)
    squares = jnp.sum(widened * widened, axis=1)
    gained = (widened * norm_gain[None, :]).astype(BF)

    def features(e):
        s = y ^ e ^ t
        picked = [
            lax.dynamic_slice(gained, (0, (((s >> 1) * 4 + (x ^ d)) * 2 + (s & 1)) * 256), (ROWS, 256))
            for d in range(4)
        ]
        return jnp.concatenate(picked, axis=1)

    ring = [swap(features(e), "y", e) for e in (1, 2, 3)]
    first, packed, *ring = lax.optimization_barrier((first, packed, *ring))
    second = move(packed, lambda y, zh, x, c, t: ((2 * zh + c) ^ y, 1 - (t & 1), x, t >> 1, y))
    inputs = jnp.concatenate([features(0)] + ring, axis=0)

    wo_near = lax.all_gather(out_weight, ("y", "x", "core"), axis=0, tiled=True)

    def along(block):
        return jnp.stack([block] + [swap(block, "x", d) for d in (1, 2, 3)])

    def reduced(here, there):
        sent, total = project(inputs, here, there)
        for e in (1, 2, 3):
            total = total + swap(sent[e - 1], "y", e).astype(F32)
        return total

    here = along(first)
    here, second, out_weight = lax.optimization_barrier((here, second, out_weight))
    total = reduced(here, swap(here, "core", 1))
    here = along(second)
    there = swap(here, "core", 1)
    wo_other = swap(out_weight, "zh", 1)
    total, there, wo_other = lax.optimization_barrier((total, there, wo_other))
    wo_far = lax.all_gather(wo_other, ("y", "x", "core"), axis=0, tiled=True)
    summed = [total, reduced(here, there)]
    base = 2 * c + zh
    q_slots = [half[:, at : at + 384] for at in (0, 384) for half in summed]
    kv_slots = [half[:, at : at + 64] for at in (768, 832) for half in summed]
    q_sum = jnp.concatenate(by_index(q_slots, base), axis=1)
    kv_sum = jnp.concatenate(by_index(kv_slots, base), axis=1)

    kv_short = kv_sum.astype(BF)
    high = lax.reduce_precision(squares, 8, 7)
    middle = lax.reduce_precision(squares - high, 8, 7)
    low = squares - high - middle
    note = jnp.pad(jnp.stack([high, middle, low]), ((0, 29), (0, 0))).astype(BF)
    shared = jnp.concatenate([kv_short[32 * r : 32 * r + 32] for r in range(4)] + [note], axis=1)

    def rows_for(d):
        return lax.dynamic_slice(q_sum, ((t ^ d) * 32, 0), (32, 1536))

    q_raw, kv_raw, total = rows_for(0), kv_sum, squares
    for d in (1, 2, 3):
        came = swap(jnp.concatenate([rows_for(d).astype(BF), shared], axis=1), "zl", d).astype(F32)
        q_raw = q_raw + came[:, :1536]
        kv_raw = kv_raw + jnp.concatenate([came[:, 1536 + 256 * r : 1792 + 256 * r] for r in range(4)], axis=0)
        total = total + ((came[2, 2560:] + came[1, 2560:]) + came[0, 2560:])
    scales = lax.rsqrt(total / D + 1e-05)

    limit = lengths[0]
    kv = (kv_raw * scales[:, None]).astype(BF)
    keys = rotate(kv[:, :HD].astype(F32), COSINE, SINE).astype(BF)
    values = kv[:, HD:]
    mine_rows = [lax.dynamic_slice(table, (t * 32, 0), (32, HD)) for table in (COSINE, SINE)]
    scale_here = lax.dynamic_slice(scales, (t * 32,), (32,))
    query = rotate((q_raw * scale_here[:, None]).reshape(32, 12, HD), *mine_rows).astype(BF)
    attended = attend(query, keys, values, limit, t * 32).reshape(32, 1536)
    lows = jnp.concatenate([attended[:, 384 * d : 384 * d + 192] for d in range(4)], axis=1)
    highs = jnp.concatenate([attended[:, 384 * d + 192 : 384 * d + 384] for d in range(4)], axis=1)
    attended = jnp.concatenate([pick(zh == 1, lows, highs), pick(zh == 1, highs, lows)], axis=1)

    got = [attended] + [swap(attended, "zl", d) for d in (1, 2, 3)]
    all_rows = jnp.concatenate(by_index(got, t), axis=0)
    return mix(all_rows, wo_near, wo_far)


def solution(mesh):
    fine = Mesh(mesh.devices.reshape(SIZES), AXES)
    rows = ("y", "zh", "x", "core")
    placed = (P(rows, "zl"), P("zl"), P(rows, "zl"), P(rows, "zl"), P(rows, "zl"), P(rows))
    return jax.shard_map(body, mesh=fine, in_specs=placed, out_specs=P(rows, "zl"), check_vma=False)
```

```python
import math

import jax
import jax.numpy as jnp
import numpy as np
from jax import lax
from jax.experimental import pallas as pl
from jax.experimental.pallas import tpu as pltpu
from jax.sharding import Mesh
from jax.sharding import PartitionSpec as P

AXES = ("y", "zh", "x", "core", "zl")
SIZES = (4, 2, 4, 2, 4)
D = 16384
HD = 128
ROWS = 128
BF = jnp.bfloat16
F32 = jnp.float32


def flat(*coords):
    index = 0
    for size, coord in zip(SIZES, coords):
        index = index * size + coord
    return index


def every():
    for y in range(4):
        for zh in range(2):
            for x in range(4):
                for c in range(2):
                    for t in range(4):
                        yield y, zh, x, c, t


def swap(value, axis, d):
    n = SIZES[AXES.index(axis)]
    return lax.ppermute(value, axis, [(i, i ^ d) for i in range(n)])


def move(value, where):
    return lax.ppermute(value, AXES, [(flat(*at), flat(*where(*at))) for at in every()])


def tables():
    freqs = np.exp(np.arange(HD // 2, dtype=np.float32) * np.float32(-2.0 * math.log(500000.0) / HD))
    angle = np.arange(ROWS, dtype=np.float32)[:, None] * freqs.astype(np.float32)[None, :]
    cosine = np.repeat(np.cos(angle), 2, axis=1).astype(np.float32)
    sine = np.repeat(np.sin(angle), 2, axis=1).astype(np.float32)
    sine[:, 0::2] *= -1.0
    return cosine, sine


COSINE, SINE = tables()


def order_of(zh):
    order = np.arange(384).reshape(2, 8, 24)
    order = np.stack([order[zh], order[1 - zh]], axis=1).reshape(384)
    return np.eye(384, dtype=np.float32)[:, order].astype(jnp.bfloat16)


ORDER = (order_of(0), order_of(1))


def rotate(values, cosine, sine):
    shape = (values.shape[0],) + (1,) * (values.ndim - 2) + (HD,)
    even = jnp.arange(HD) % 2 == 0
    partner = jnp.where(even, jnp.roll(values, -1, axis=-1), jnp.roll(values, 1, axis=-1))
    return values * cosine.reshape(shape) + partner * sine.reshape(shape)


def pick(flag, first, second):
    return jnp.where(flag, second, first)


def by_index(parts, at):
    odd = (at & 1) == 1
    high = (at >> 1) == 1
    a, b = pick(odd, parts[0], parts[1]), pick(odd, parts[1], parts[0])
    c, d = pick(odd, parts[2], parts[3]), pick(odd, parts[3], parts[2])
    return [pick(high, a, c), pick(high, b, d), pick(high, c, a), pick(high, d, b)]


def whole(shape):
    return pl.BlockSpec(memory_space=pltpu.VMEM)


def pack_kernel(q_ref, kv_ref, out_ref):
    for h in range(3):
        out_ref[256 * h : 256 * h + 256, :] = q_ref[:, 128 * h : 128 * h + 128]
    for h in range(2):
        out_ref[768 + 64 * h : 832 + 64 * h, :] = kv_ref[:, 128 * h : 128 * h + 128]


def pack(query_weight, kv_turned):
    return pl.pallas_call(
        pack_kernel,
        out_shape=jax.ShapeDtypeStruct((896, 128), BF),
        in_specs=[whole(0)] * 2,
        out_specs=whole(0),
        compiler_params=pltpu.CompilerParams(vmem_limit_bytes=32 * 2**20),
        cost_estimate=pl.CostEstimate(flops=0, bytes_accessed=460000, transcendentals=0),
    )(query_weight, kv_turned)


def project_kernel(x_ref, here_ref, there_ref, out_ref, own_ref):
    inputs = x_ref[...]
    for slot, ref in enumerate((here_ref, there_ref)):
        heads = [
            jnp.concatenate([ref[d, 256 * h : 256 * h + 256, :] for d in range(4)], axis=0) for h in range(3)
        ]
        q = jnp.dot(inputs, jnp.concatenate(heads, axis=1), preferred_element_type=F32)
        own_ref[:, 384 * slot : 384 * slot + 384] = q[:ROWS]
        for e in (1, 2, 3):
            out_ref[e - 1, :, 384 * slot : 384 * slot + 384] = q[ROWS * e : ROWS * e + ROWS].astype(BF)
    kv_rows = [
        jnp.concatenate([ref[d, 768 + 64 * h : 832 + 64 * h, :] for d in range(4) for h in (0, 1)], axis=1)
        for ref in (here_ref, there_ref)
    ]
    kv = lax.dot_general(
        inputs, jnp.concatenate(kv_rows, axis=0), (((1,), (1,)), ((), ())), preferred_element_type=F32
    )
    own_ref[:, 768:] = kv[:ROWS]
    for e in (1, 2, 3):
        out_ref[e - 1, :, 768:] = kv[ROWS * e : ROWS * e + ROWS].astype(BF)


def project(inputs, here, there):
    return pl.pallas_call(
        project_kernel,
        out_shape=(jax.ShapeDtypeStruct((3, ROWS, 896), BF), jax.ShapeDtypeStruct((ROWS, 896), F32)),
        in_specs=[whole(0)] * 3,
        out_specs=(whole(0),) * 2,
        compiler_params=pltpu.CompilerParams(vmem_limit_bytes=32 * 2**20),
        cost_estimate=pl.CostEstimate(flops=2 * 512 * 1024 * 896, bytes_accessed=4000000, transcendentals=0),
    )(inputs, here, there)


def attend(query, keys, values, limit, first):
    scores = jnp.einsum("qhd,kd->hqk", query, keys, preferred_element_type=F32) * HD ** (-0.5)
    keys_at = jnp.arange(ROWS, dtype=jnp.int32)
    rows_at = first + jnp.arange(32, dtype=jnp.int32)
    valid = (keys_at[None, :] <= rows_at[:, None]) & (keys_at[None, :] < limit)
    scores = jnp.where(valid[None], scores, -jnp.inf)
    raised = jnp.exp(scores - jnp.max(scores, axis=-1, keepdims=True))
    weights = (raised / jnp.sum(raised, axis=-1, keepdims=True)).astype(BF)
    output = jnp.einsum("hqk,kd->qhd", weights, values, preferred_element_type=F32)
    return jnp.where((rows_at < limit)[:, None, None], output, 0.0).astype(BF)


def body(tokens, norm_gain, query_weight, kv_weight, out_weight, lengths):
    y, zh, x, c, t = (lax.axis_index(name) for name in AXES)

    packed = pack(query_weight, kv_weight.T)
    wo_other = swap(out_weight, "zh", 1)
    first = move(packed, lambda y, zh, x, c, t: ((2 * zh + c) ^ y, t >> 1, x, t & 1, y))
    second = move(packed, lambda y, zh, x, c, t: ((2 * zh + c) ^ y, 1 - (t >> 1), x, t & 1, y))

    widened = tokens.astype(F32)
    squares = jnp.sum(widened * widened, axis=1)
    gained = (widened * norm_gain[None, :]).astype(BF)

    def features(pairs_at):
        picked = [
            lax.dynamic_slice(gained, (0, (((s >> 1) * 4 + at) * 2 + (s & 1)) * 256), (ROWS, 256))
            for s, at in pairs_at
        ]
        return jnp.concatenate(picked, axis=1)

    def features_a(e):
        return features([(y ^ e ^ t, x ^ d) for d in range(4)])

    def features_b(e):
        return features([(y ^ d ^ t, x ^ e) for d in range(4)])

    ring_a = [swap(features_a(e), "y", e) for e in (1, 2, 3)]
    ring_b = [swap(features_b(e), "x", e) for e in (1, 2, 3)]
    ring_a[0], wo_other = lax.optimization_barrier((ring_a[0], wo_other))
    first, second, *rings = lax.optimization_barrier((first, second, *ring_a, *ring_b))
    inputs_a = jnp.concatenate([features_a(0)] + rings[:3], axis=0)
    inputs_b = jnp.concatenate([features_b(0)] + rings[3:], axis=0)

    wo_piece = jnp.concatenate([out_weight, wo_other], axis=0)
    wo = lax.all_gather(wo_piece, ("y", "x", "core"), axis=0, tiled=True)

    block_a = pick(zh == 1, first, second)
    block_b = pick(zh == 1, second, first)
    came_a = [swap(block_a, "x", d) for d in (1, 2, 3)]
    came_b = [swap(block_b, "y", d) for d in (1, 2, 3)]
    here_a = jnp.stack([block_a] + came_a)
    here_b = jnp.stack([block_b] + came_b)
    sent_a, total_a = project(inputs_a, here_a, swap(here_a, "core", 1))
    sent_b, total_b = project(inputs_b, here_b, swap(here_b, "core", 1))
    got_a = [swap(sent_a[e - 1], "y", e) for e in (1, 2, 3)]
    got_b = [swap(sent_b[e - 1], "x", e) for e in (1, 2, 3)]
    summed = [
        total + sum(part.astype(F32) for part in parts) for total, parts in ((total_a, got_a), (total_b, got_b))
    ]

    def ordered(width, at):
        columns = []
        for half in summed:
            here, there = half[:, at : at + width], half[:, at + width : at + 2 * width]
            columns += [pick(c == 1, here, there), pick(c == 1, there, here)]
        return jnp.concatenate(columns, axis=1)

    q_sum = ordered(384, 0)
    kv_sum = ordered(64, 768)

    kv_short = kv_sum.astype(BF)
    high = lax.reduce_precision(squares, 8, 7)
    middle = lax.reduce_precision(squares - high, 8, 7)
    low = squares - high - middle
    note = jnp.pad(jnp.stack([high, middle, low]), ((0, 29), (0, 0))).astype(BF)
    shared = jnp.concatenate([kv_short[32 * r : 32 * r + 32] for r in range(4)] + [note], axis=1)

    def rows_for(d):
        return lax.dynamic_slice(q_sum, ((t ^ d) * 32, 0), (32, 1536))

    q_raw, kv_raw, total = rows_for(0), kv_sum, squares
    for d in (1, 2, 3):
        came = swap(jnp.concatenate([rows_for(d).astype(BF), shared], axis=1), "zl", d).astype(F32)
        q_raw = q_raw + came[:, :1536]
        kv_raw = kv_raw + jnp.concatenate([came[:, 1536 + 256 * r : 1792 + 256 * r] for r in range(4)], axis=0)
        total = total + ((came[2, 2560:] + came[1, 2560:]) + came[0, 2560:])
    scales = lax.rsqrt(total / D + 1e-05)

    limit = lengths[0]
    kv = (kv_raw * scales[:, None]).astype(BF)
    keys = rotate(kv[:, :HD].astype(F32), COSINE, SINE).astype(BF)
    values = kv[:, HD:]
    mine_rows = [lax.dynamic_slice(table, (t * 32, 0), (32, HD)) for table in (COSINE, SINE)]
    scale_here = lax.dynamic_slice(scales, (t * 32,), (32,))
    query = rotate((q_raw * scale_here[:, None]).reshape(32, 12, HD), *mine_rows).astype(BF)
    attended = attend(query, keys, values, limit, t * 32).reshape(32, 1536)
    stacked = jnp.concatenate([attended[:, 384 * d : 384 * d + 384] for d in range(4)], axis=0)
    stacked = jnp.dot(stacked, pick(zh == 1, ORDER[0], ORDER[1]), preferred_element_type=F32).astype(BF)
    attended = jnp.concatenate([stacked[32 * d : 32 * d + 32] for d in range(4)], axis=1)

    got = [attended] + [swap(attended, "zl", d) for d in (1, 2, 3)]
    all_rows = jnp.concatenate(by_index(got, t), axis=0)
    return jnp.dot(all_rows, wo, preferred_element_type=F32).astype(BF)


def solution(mesh):
    fine = Mesh(mesh.devices.reshape(SIZES), AXES)
    rows = ("y", "zh", "x", "core")
    placed = (P(rows, "zl"), P("zl"), P(rows, "zl"), P(rows, "zl"), P(rows, "zl"), P(rows))
    return jax.shard_map(body, mesh=fine, in_specs=placed, out_specs=P(rows, "zl"), check_vma=False)
```

```python
import math

import jax
import jax.numpy as jnp
import numpy as np
from jax import lax
from jax.experimental import pallas as pl
from jax.experimental.pallas import tpu as pltpu
from jax.sharding import Mesh
from jax.sharding import PartitionSpec as P

AXES = ("y", "zh", "x", "core", "zl")
SIZES = (4, 2, 4, 2, 4)
D = 16384
HD = 128
ROWS = 128
BF = jnp.bfloat16
F32 = jnp.float32


def flat(*coords):
    index = 0
    for size, coord in zip(SIZES, coords):
        index = index * size + coord
    return index


def every():
    for y in range(4):
        for zh in range(2):
            for x in range(4):
                for c in range(2):
                    for t in range(4):
                        yield y, zh, x, c, t


def swap(value, axis, d):
    n = SIZES[AXES.index(axis)]
    return lax.ppermute(value, axis, [(i, i ^ d) for i in range(n)])


def move(value, where):
    return lax.ppermute(value, AXES, [(flat(*at), flat(*where(*at))) for at in every()])


def along(value, e, first, second):
    def target(*at):
        at = list(at)
        at[AXES.index((first, second)[at[3]])] ^= e
        return at

    return move(value, target)


def tables():
    freqs = np.exp(np.arange(HD // 2, dtype=np.float32) * np.float32(-2.0 * math.log(500000.0) / HD))
    angle = np.arange(ROWS, dtype=np.float32)[:, None] * freqs.astype(np.float32)[None, :]
    cosine = np.repeat(np.cos(angle), 2, axis=1).astype(np.float32)
    sine = np.repeat(np.sin(angle), 2, axis=1).astype(np.float32)
    sine[:, 0::2] *= -1.0
    return cosine, sine


COSINE, SINE = tables()


def order_of(zh):
    order = np.arange(384).reshape(2, 8, 24)
    order = np.stack([order[zh], order[1 - zh]], axis=1).reshape(384)
    return np.eye(384, dtype=np.float32)[:, order].astype(jnp.bfloat16)


ORDER = (order_of(0), order_of(1))


def rotate(values, cosine, sine):
    shape = (values.shape[0],) + (1,) * (values.ndim - 2) + (HD,)
    even = jnp.arange(HD) % 2 == 0
    partner = jnp.where(even, jnp.roll(values, -1, axis=-1), jnp.roll(values, 1, axis=-1))
    return values * cosine.reshape(shape) + partner * sine.reshape(shape)


def pick(flag, first, second):
    return jnp.where(flag, second, first)


def by_index(parts, at):
    odd = (at & 1) == 1
    high = (at >> 1) == 1
    a, b = pick(odd, parts[0], parts[1]), pick(odd, parts[1], parts[0])
    c, d = pick(odd, parts[2], parts[3]), pick(odd, parts[3], parts[2])
    return [pick(high, a, c), pick(high, b, d), pick(high, c, a), pick(high, d, b)]


def whole(shape):
    return pl.BlockSpec(memory_space=pltpu.VMEM)


def pack_kernel(q_ref, kv_ref, out_ref):
    for h in range(3):
        out_ref[256 * h : 256 * h + 256, :] = q_ref[:, 128 * h : 128 * h + 128]
    for h in range(2):
        out_ref[768 + 64 * h : 832 + 64 * h, :] = kv_ref[:, 128 * h : 128 * h + 128]


def pack(query_weight, kv_turned):
    return pl.pallas_call(
        pack_kernel,
        out_shape=jax.ShapeDtypeStruct((896, 128), BF),
        in_specs=[whole(0)] * 2,
        out_specs=whole(0),
        compiler_params=pltpu.CompilerParams(vmem_limit_bytes=32 * 2**20),
        cost_estimate=pl.CostEstimate(flops=0, bytes_accessed=460000, transcendentals=0),
    )(query_weight, kv_turned)


def project_kernel(x_ref, *refs):
    blocks, (out_ref, own_ref) = refs[:4], refs[4:]
    inputs = x_ref[...]
    for slot in (0, 1):
        heads = [
            jnp.concatenate([ref[slot, 256 * h : 256 * h + 256, :] for ref in blocks], axis=0) for h in range(3)
        ]
        q = jnp.dot(inputs, jnp.concatenate(heads, axis=1), preferred_element_type=F32)
        own_ref[:, 384 * slot : 384 * slot + 384] = q[:ROWS]
        for e in (1, 2, 3):
            out_ref[e - 1, :, 384 * slot : 384 * slot + 384] = q[ROWS * e : ROWS * e + ROWS].astype(BF)
    kv_rows = [
        jnp.concatenate([ref[slot, 768 + 64 * h : 832 + 64 * h, :] for ref in blocks for h in (0, 1)], axis=1)
        for slot in (0, 1)
    ]
    kv = lax.dot_general(
        inputs, jnp.concatenate(kv_rows, axis=0), (((1,), (1,)), ((), ())), preferred_element_type=F32
    )
    own_ref[:, 768:] = kv[:ROWS]
    for e in (1, 2, 3):
        out_ref[e - 1, :, 768:] = kv[ROWS * e : ROWS * e + ROWS].astype(BF)


def project(inputs, blocks):
    return pl.pallas_call(
        project_kernel,
        out_shape=(jax.ShapeDtypeStruct((3, ROWS, 896), BF), jax.ShapeDtypeStruct((ROWS, 896), F32)),
        in_specs=[whole(0)] * 5,
        out_specs=(whole(0),) * 2,
        compiler_params=pltpu.CompilerParams(vmem_limit_bytes=32 * 2**20),
        cost_estimate=pl.CostEstimate(flops=2 * 512 * 1024 * 896, bytes_accessed=4000000, transcendentals=0),
    )(inputs, *blocks)


def attend(query, keys, values, limit, first):
    scores = jnp.einsum("qhd,kd->hqk", query, keys, preferred_element_type=F32) * HD ** (-0.5)
    keys_at = jnp.arange(ROWS, dtype=jnp.int32)
    rows_at = first + jnp.arange(32, dtype=jnp.int32)
    valid = (keys_at[None, :] <= rows_at[:, None]) & (keys_at[None, :] < limit)
    scores = jnp.where(valid[None], scores, -jnp.inf)
    raised = jnp.exp(scores - jnp.max(scores, axis=-1, keepdims=True))
    weights = (raised / jnp.sum(raised, axis=-1, keepdims=True)).astype(BF)
    output = jnp.einsum("hqk,kd->qhd", weights, values, preferred_element_type=F32)
    return jnp.where((rows_at < limit)[:, None, None], output, 0.0).astype(BF)


def body(tokens, norm_gain, query_weight, kv_weight, out_weight, lengths):
    y, zh, x, c, t = (lax.axis_index(name) for name in AXES)

    packed = pack(query_weight, kv_weight.T)
    first = move(packed, lambda y, zh, x, c, t: ((2 * zh + c) ^ y, t & 1, x, t >> 1, y))
    wo_other = swap(out_weight, "zh", 1)

    widened = tokens.astype(F32)
    squares = jnp.sum(widened * widened, axis=1)
    gained = (widened * norm_gain[None, :]).astype(BF)

    def features(e):
        picked = []
        for d in range(4):
            s = y ^ t ^ jnp.where(c == 0, e, d)
            at = x ^ jnp.where(c == 0, d, e)
            picked.append(lax.dynamic_slice(gained, (0, (((s >> 1) * 4 + at) * 2 + (s & 1)) * 256), (ROWS, 256)))
        return jnp.concatenate(picked, axis=1)

    ring = [along(features(e), e, "y", "x") for e in (1, 2, 3)]
    first, packed, wo_other, *ring = lax.optimization_barrier((first, packed, wo_other, *ring))
    second = move(packed, lambda y, zh, x, c, t: ((2 * zh + c) ^ y, 1 - (t & 1), x, t >> 1, y))
    inputs = jnp.concatenate([features(0)] + ring, axis=0)

    wo_piece = jnp.concatenate([out_weight, wo_other], axis=0)
    wo = lax.all_gather(wo_piece, ("y", "x", "core"), axis=0, tiled=True)

    def gathered(block):
        pair = jnp.stack([block, swap(block, "core", 1)])
        return [pair] + [along(pair, d, "x", "y") for d in (1, 2, 3)]

    def reduced(blocks):
        sent, total = project(inputs, blocks)
        for e in (1, 2, 3):
            total = total + along(sent[e - 1], e, "y", "x").astype(F32)
        return total

    second, *blocks = lax.optimization_barrier((second, *gathered(first)))
    total, *blocks = lax.optimization_barrier((reduced(blocks), *gathered(second)))
    summed = [total, reduced(blocks)]
    base = 2 * c + zh
    q_slots = [half[:, at : at + 384] for at in (0, 384) for half in summed]
    kv_slots = [half[:, at : at + 64] for at in (768, 832) for half in summed]
    q_sum = jnp.concatenate(by_index(q_slots, base), axis=1)
    kv_sum = jnp.concatenate(by_index(kv_slots, base), axis=1)

    kv_short = kv_sum.astype(BF)
    high = lax.reduce_precision(squares, 8, 7)
    middle = lax.reduce_precision(squares - high, 8, 7)
    low = squares - high - middle
    note = jnp.pad(jnp.stack([high, middle, low]), ((0, 29), (0, 0))).astype(BF)
    shared = jnp.concatenate([kv_short[32 * r : 32 * r + 32] for r in range(4)] + [note], axis=1)

    def rows_for(d):
        return lax.dynamic_slice(q_sum, ((t ^ d) * 32, 0), (32, 1536))

    q_raw, kv_raw, total = rows_for(0), kv_sum, squares
    for d in (1, 2, 3):
        came = swap(jnp.concatenate([rows_for(d).astype(BF), shared], axis=1), "zl", d).astype(F32)
        q_raw = q_raw + came[:, :1536]
        kv_raw = kv_raw + jnp.concatenate([came[:, 1536 + 256 * r : 1792 + 256 * r] for r in range(4)], axis=0)
        total = total + ((came[2, 2560:] + came[1, 2560:]) + came[0, 2560:])
    scales = lax.rsqrt(total / D + 1e-05)

    limit = lengths[0]
    kv = (kv_raw * scales[:, None]).astype(BF)
    keys = rotate(kv[:, :HD].astype(F32), COSINE, SINE).astype(BF)
    values = kv[:, HD:]
    mine_rows = [lax.dynamic_slice(table, (t * 32, 0), (32, HD)) for table in (COSINE, SINE)]
    scale_here = lax.dynamic_slice(scales, (t * 32,), (32,))
    query = rotate((q_raw * scale_here[:, None]).reshape(32, 12, HD), *mine_rows).astype(BF)
    attended = attend(query, keys, values, limit, t * 32).reshape(32, 1536)
    stacked = jnp.concatenate([attended[:, 384 * d : 384 * d + 384] for d in range(4)], axis=0)
    stacked = jnp.dot(stacked, pick(zh == 1, ORDER[0], ORDER[1]), preferred_element_type=F32).astype(BF)
    attended = jnp.concatenate([stacked[32 * d : 32 * d + 32] for d in range(4)], axis=1)

    got = [attended] + [swap(attended, "zl", d) for d in (1, 2, 3)]
    all_rows = jnp.concatenate(by_index(got, t), axis=0)
    return jnp.dot(all_rows, wo, preferred_element_type=F32).astype(BF)


def solution(mesh):
    fine = Mesh(mesh.devices.reshape(SIZES), AXES)
    rows = ("y", "zh", "x", "core")
    placed = (P(rows, "zl"), P("zl"), P(rows, "zl"), P(rows, "zl"), P(rows, "zl"), P(rows))
    return jax.shard_map(body, mesh=fine, in_specs=placed, out_specs=P(rows, "zl"), check_vma=False)
```

```python
import math

import jax
import jax.numpy as jnp
import numpy as np
from jax import lax
from jax.experimental import pallas as pl
from jax.experimental.pallas import tpu as pltpu
from jax.sharding import Mesh
from jax.sharding import PartitionSpec as P

AXES = ("y", "zh", "x", "core", "zl")
SIZES = (4, 2, 4, 2, 4)
D = 16384
HD = 128
ROWS = 128
BF = jnp.bfloat16
F32 = jnp.float32


def flat(*coords):
    index = 0
    for size, coord in zip(SIZES, coords):
        index = index * size + coord
    return index


def every():
    for y in range(4):
        for zh in range(2):
            for x in range(4):
                for c in range(2):
                    for t in range(4):
                        yield y, zh, x, c, t


def swap(value, axis, d):
    n = SIZES[AXES.index(axis)]
    return lax.ppermute(value, axis, [(i, i ^ d) for i in range(n)])


def move(value, where):
    return lax.ppermute(value, AXES, [(flat(*at), flat(*where(*at))) for at in every()])


def along(value, e, first, second):
    def target(*at):
        at = list(at)
        at[AXES.index((first, second)[at[3]])] ^= e
        return at

    return move(value, target)


def tables():
    freqs = np.exp(np.arange(HD // 2, dtype=np.float32) * np.float32(-2.0 * math.log(500000.0) / HD))
    angle = np.arange(ROWS, dtype=np.float32)[:, None] * freqs.astype(np.float32)[None, :]
    cosine = np.repeat(np.cos(angle), 2, axis=1).astype(np.float32)
    sine = np.repeat(np.sin(angle), 2, axis=1).astype(np.float32)
    sine[:, 0::2] *= -1.0
    return cosine, sine


COSINE, SINE = tables()


def order_of(zh):
    order = np.arange(384).reshape(2, 8, 24)
    order = np.stack([order[zh], order[1 - zh]], axis=1).reshape(384)
    return np.eye(384, dtype=np.float32)[:, order].astype(jnp.bfloat16)


ORDER = (order_of(0), order_of(1))


def rotate(values, cosine, sine):
    shape = (values.shape[0],) + (1,) * (values.ndim - 2) + (HD,)
    even = jnp.arange(HD) % 2 == 0
    partner = jnp.where(even, jnp.roll(values, -1, axis=-1), jnp.roll(values, 1, axis=-1))
    return values * cosine.reshape(shape) + partner * sine.reshape(shape)


def pick(flag, first, second):
    return jnp.where(flag, second, first)


def by_index(parts, at):
    odd = (at & 1) == 1
    high = (at >> 1) == 1
    a, b = pick(odd, parts[0], parts[1]), pick(odd, parts[1], parts[0])
    c, d = pick(odd, parts[2], parts[3]), pick(odd, parts[3], parts[2])
    return [pick(high, a, c), pick(high, b, d), pick(high, c, a), pick(high, d, b)]


def whole(shape):
    return pl.BlockSpec(memory_space=pltpu.VMEM)


def pack_kernel(q_ref, kv_ref, out_ref):
    for h in range(3):
        out_ref[256 * h : 256 * h + 256, :] = q_ref[:, 128 * h : 128 * h + 128]
    for h in range(2):
        out_ref[768 + 64 * h : 832 + 64 * h, :] = kv_ref[:, 128 * h : 128 * h + 128]


def pack(query_weight, kv_turned):
    return pl.pallas_call(
        pack_kernel,
        out_shape=jax.ShapeDtypeStruct((896, 128), BF),
        in_specs=[whole(0)] * 2,
        out_specs=whole(0),
        compiler_params=pltpu.CompilerParams(vmem_limit_bytes=32 * 2**20),
        cost_estimate=pl.CostEstimate(flops=0, bytes_accessed=460000, transcendentals=0),
    )(query_weight, kv_turned)


def project_kernel(x_ref, *refs):
    blocks, (out_ref, own_ref) = refs[:4], refs[4:]
    inputs = x_ref[...]
    for slot in (0, 1):
        heads = [
            jnp.concatenate([ref[slot, 256 * h : 256 * h + 256, :] for ref in blocks], axis=0) for h in range(3)
        ]
        q = jnp.dot(inputs, jnp.concatenate(heads, axis=1), preferred_element_type=F32)
        own_ref[:, 384 * slot : 384 * slot + 384] = q[:ROWS]
        for e in (1, 2, 3):
            out_ref[e - 1, :, 384 * slot : 384 * slot + 384] = q[ROWS * e : ROWS * e + ROWS].astype(BF)
    kv_rows = [
        jnp.concatenate([ref[slot, 768 + 64 * h : 832 + 64 * h, :] for ref in blocks for h in (0, 1)], axis=1)
        for slot in (0, 1)
    ]
    kv = lax.dot_general(
        inputs, jnp.concatenate(kv_rows, axis=0), (((1,), (1,)), ((), ())), preferred_element_type=F32
    )
    own_ref[:, 768:] = kv[:ROWS]
    for e in (1, 2, 3):
        out_ref[e - 1, :, 768:] = kv[ROWS * e : ROWS * e + ROWS].astype(BF)


def project(inputs, blocks):
    return pl.pallas_call(
        project_kernel,
        out_shape=(jax.ShapeDtypeStruct((3, ROWS, 896), BF), jax.ShapeDtypeStruct((ROWS, 896), F32)),
        in_specs=[whole(0)] * 5,
        out_specs=(whole(0),) * 2,
        compiler_params=pltpu.CompilerParams(vmem_limit_bytes=32 * 2**20),
        cost_estimate=pl.CostEstimate(flops=2 * 512 * 1024 * 896, bytes_accessed=4000000, transcendentals=0),
    )(inputs, *blocks)


def attend(query, keys, values, limit, first):
    scores = jnp.einsum("qhd,kd->hqk", query, keys, preferred_element_type=F32) * HD ** (-0.5)
    keys_at = jnp.arange(ROWS, dtype=jnp.int32)
    rows_at = first + jnp.arange(32, dtype=jnp.int32)
    valid = (keys_at[None, :] <= rows_at[:, None]) & (keys_at[None, :] < limit)
    scores = jnp.where(valid[None], scores, -jnp.inf)
    raised = jnp.exp(scores - jnp.max(scores, axis=-1, keepdims=True))
    weights = (raised / jnp.sum(raised, axis=-1, keepdims=True)).astype(BF)
    output = jnp.einsum("hqk,kd->qhd", weights, values, preferred_element_type=F32)
    return jnp.where((rows_at < limit)[:, None, None], output, 0.0).astype(BF)


def body(tokens, norm_gain, query_weight, kv_weight, out_weight, lengths):
    y, zh, x, c, t = (lax.axis_index(name) for name in AXES)

    packed = pack(query_weight, kv_weight.T)
    first = move(packed, lambda y, zh, x, c, t: ((2 * zh + c) ^ y, t & 1, x, t >> 1, y))
    wo_other = swap(out_weight, "zh", 1)

    widened = tokens.astype(F32)
    squares = jnp.sum(widened * widened, axis=1)
    gained = (widened * norm_gain[None, :]).astype(BF)

    def features(e):
        picked = []
        for d in range(4):
            s = y ^ t ^ jnp.where(c == 0, e, d)
            at = x ^ jnp.where(c == 0, d, e)
            picked.append(lax.dynamic_slice(gained, (0, (((s >> 1) * 4 + at) * 2 + (s & 1)) * 256), (ROWS, 256)))
        return jnp.concatenate(picked, axis=1)

    ring = [along(features(e), e, "y", "x") for e in (1, 2, 3)]
    second = move(packed, lambda y, zh, x, c, t: ((2 * zh + c) ^ y, 1 - (t & 1), x, t >> 1, y))
    first, second, wo_other, *ring = lax.optimization_barrier((first, second, wo_other, *ring))
    inputs = jnp.concatenate([features(0)] + ring, axis=0)

    wo_piece = jnp.concatenate([out_weight, wo_other], axis=0)
    wo = lax.all_gather(wo_piece, ("y", "x", "core"), axis=0, tiled=True)

    def gathered(pair):
        return [pair] + [along(pair, d, "x", "y") for d in (1, 2, 3)]

    def reduced(blocks):
        sent, total = project(inputs, blocks)
        for e in (1, 2, 3):
            total = total + along(sent[e - 1], e, "y", "x").astype(F32)
        return total

    def over_zl(total, note):
        kv = total[:, 768:]
        kv_short = kv.astype(BF)
        shared = [kv_short[32 * r : 32 * r + 32] for r in range(4)] + note

        def rows_for(d):
            return lax.dynamic_slice(total, ((t ^ d) * 32, 0), (32, 768))

        q, extra = rows_for(0), 0.0
        for d in (1, 2, 3):
            came = swap(jnp.concatenate([rows_for(d).astype(BF)] + shared, axis=1), "zl", d).astype(F32)
            q = q + came[:, :768]
            kv = kv + jnp.concatenate([came[:, 768 + 128 * r : 896 + 128 * r] for r in range(4)], axis=0)
            if note:
                extra = extra + ((came[2, 1280:] + came[1, 1280:]) + came[0, 1280:])
        return (q, kv, extra) if note else (q, kv)

    high = lax.reduce_precision(squares, 8, 7)
    middle = lax.reduce_precision(squares - high, 8, 7)
    low = squares - high - middle
    note = jnp.pad(jnp.stack([high, middle, low]), ((0, 29), (0, 0))).astype(BF)

    others = swap(jnp.stack([first, second]), "core", 1)
    near_pair, far_pair = jnp.stack([first, others[0]]), jnp.stack([second, others[1]])
    far_pair, *blocks = lax.optimization_barrier((far_pair, *gathered(near_pair)))
    total, *blocks = lax.optimization_barrier((reduced(blocks), *gathered(far_pair)))
    far_total, *near_sums = lax.optimization_barrier((reduced(blocks), *over_zl(total, [note])))
    far_sums = over_zl(far_total, [])
    scales = lax.rsqrt((squares + near_sums[2]) / D + 1e-05)

    base = 2 * c + zh

    def ordered(near, far, width):
        return jnp.concatenate(
            by_index([half[:, at : at + width] for at in (0, width) for half in (near, far)], base), axis=1
        )

    q_raw = ordered(near_sums[0], far_sums[0], 384)
    kv_raw = ordered(near_sums[1], far_sums[1], 64)

    limit = lengths[0]
    kv = (kv_raw * scales[:, None]).astype(BF)
    keys = rotate(kv[:, :HD].astype(F32), COSINE, SINE).astype(BF)
    values = kv[:, HD:]
    mine_rows = [lax.dynamic_slice(table, (t * 32, 0), (32, HD)) for table in (COSINE, SINE)]
    scale_here = lax.dynamic_slice(scales, (t * 32,), (32,))
    query = rotate((q_raw * scale_here[:, None]).reshape(32, 12, HD), *mine_rows).astype(BF)
    attended = attend(query, keys, values, limit, t * 32).reshape(32, 1536)
    stacked = jnp.concatenate([attended[:, 384 * d : 384 * d + 384] for d in range(4)], axis=0)
    stacked = jnp.dot(stacked, pick(zh == 1, ORDER[0], ORDER[1]), preferred_element_type=F32).astype(BF)
    attended = jnp.concatenate([stacked[32 * d : 32 * d + 32] for d in range(4)], axis=1)

    got = [attended] + [swap(attended, "zl", d) for d in (1, 2, 3)]
    all_rows = jnp.concatenate(by_index(got, t), axis=0)
    return jnp.dot(all_rows, wo, preferred_element_type=F32).astype(BF)


def solution(mesh):
    fine = Mesh(mesh.devices.reshape(SIZES), AXES)
    rows = ("y", "zh", "x", "core")
    placed = (P(rows, "zl"), P("zl"), P(rows, "zl"), P(rows, "zl"), P(rows, "zl"), P(rows))
    return jax.shard_map(body, mesh=fine, in_specs=placed, out_specs=P(rows, "zl"), check_vma=False)
```

```python
import math

import jax
import jax.numpy as jnp
import numpy as np
from jax import lax
from jax.experimental import pallas as pl
from jax.experimental.pallas import tpu as pltpu
from jax.sharding import Mesh
from jax.sharding import PartitionSpec as P

AXES = ("y", "zh", "x", "core", "zl")
SIZES = (4, 2, 4, 2, 4)
D = 16384
HD = 128
ROWS = 128
BF = jnp.bfloat16
F32 = jnp.float32


def flat(*coords):
    index = 0
    for size, coord in zip(SIZES, coords):
        index = index * size + coord
    return index


def every():
    for y in range(4):
        for zh in range(2):
            for x in range(4):
                for c in range(2):
                    for t in range(4):
                        yield y, zh, x, c, t


def swap(value, axis, d):
    n = SIZES[AXES.index(axis)]
    return lax.ppermute(value, axis, [(i, i ^ d) for i in range(n)])


def move(value, where):
    return lax.ppermute(value, AXES, [(flat(*at), flat(*where(*at))) for at in every()])


def along(value, e, first, second):
    def target(*at):
        at = list(at)
        at[AXES.index((first, second)[at[3]])] ^= e
        return at

    return move(value, target)


def tables():
    freqs = np.exp(np.arange(HD // 2, dtype=np.float32) * np.float32(-2.0 * math.log(500000.0) / HD))
    angle = np.arange(ROWS, dtype=np.float32)[:, None] * freqs.astype(np.float32)[None, :]
    cosine = np.repeat(np.cos(angle), 2, axis=1).astype(np.float32)
    sine = np.repeat(np.sin(angle), 2, axis=1).astype(np.float32)
    sine[:, 0::2] *= -1.0
    return cosine, sine


COSINE, SINE = tables()


def rotate(values, cosine, sine):
    shape = (values.shape[0],) + (1,) * (values.ndim - 2) + (HD,)
    even = jnp.arange(HD) % 2 == 0
    partner = jnp.where(even, jnp.roll(values, -1, axis=-1), jnp.roll(values, 1, axis=-1))
    return values * cosine.reshape(shape) + partner * sine.reshape(shape)


def pick(flag, first, second):
    return jnp.where(flag, second, first)


def by_index(parts, at):
    odd = (at & 1) == 1
    high = (at >> 1) == 1
    a, b = pick(odd, parts[0], parts[1]), pick(odd, parts[1], parts[0])
    c, d = pick(odd, parts[2], parts[3]), pick(odd, parts[3], parts[2])
    return [pick(high, a, c), pick(high, b, d), pick(high, c, a), pick(high, d, b)]


def whole(shape):
    return pl.BlockSpec(memory_space=pltpu.VMEM)


def pack_kernel(q_ref, kv_ref, out_ref):
    for h in range(3):
        out_ref[256 * h : 256 * h + 256, :] = q_ref[:, 128 * h : 128 * h + 128]
    for h in range(2):
        out_ref[768 + 64 * h : 832 + 64 * h, :] = kv_ref[:, 128 * h : 128 * h + 128]


def pack(query_weight, kv_turned):
    return pl.pallas_call(
        pack_kernel,
        out_shape=jax.ShapeDtypeStruct((896, 128), BF),
        in_specs=[whole(0)] * 2,
        out_specs=whole(0),
        compiler_params=pltpu.CompilerParams(vmem_limit_bytes=32 * 2**20),
        cost_estimate=pl.CostEstimate(flops=0, bytes_accessed=460000, transcendentals=0),
    )(query_weight, kv_turned)


def project_kernel(x_ref, *refs):
    blocks, (out_ref, own_ref) = refs[:4], refs[4:]
    inputs = x_ref[...]
    for slot in (0, 1):
        heads = [
            jnp.concatenate([ref[slot, 256 * h : 256 * h + 256, :] for ref in blocks], axis=0) for h in range(3)
        ]
        q = jnp.dot(inputs, jnp.concatenate(heads, axis=1), preferred_element_type=F32)
        own_ref[:, 384 * slot : 384 * slot + 384] = q[:ROWS]
        for e in (1, 2, 3):
            out_ref[e - 1, :, 384 * slot : 384 * slot + 384] = q[ROWS * e : ROWS * e + ROWS].astype(BF)
    kv_rows = [
        jnp.concatenate([ref[slot, 768 + 64 * h : 832 + 64 * h, :] for ref in blocks for h in (0, 1)], axis=1)
        for slot in (0, 1)
    ]
    kv = lax.dot_general(
        inputs, jnp.concatenate(kv_rows, axis=0), (((1,), (1,)), ((), ())), preferred_element_type=F32
    )
    own_ref[:, 768:] = kv[:ROWS]
    for e in (1, 2, 3):
        out_ref[e - 1, :, 768:] = kv[ROWS * e : ROWS * e + ROWS].astype(BF)


def project(inputs, blocks):
    return pl.pallas_call(
        project_kernel,
        out_shape=(jax.ShapeDtypeStruct((3, ROWS, 896), BF), jax.ShapeDtypeStruct((ROWS, 896), F32)),
        in_specs=[whole(0)] * 5,
        out_specs=(whole(0),) * 2,
        compiler_params=pltpu.CompilerParams(vmem_limit_bytes=32 * 2**20),
        cost_estimate=pl.CostEstimate(flops=2 * 512 * 1024 * 896, bytes_accessed=4000000, transcendentals=0),
    )(inputs, *blocks)


def mix_kernel(core_ref, mine_ref, other_ref, *refs):
    near, far, (kept_ref, sent_ref) = refs[:4], refs[4:8], refs[8:]

    def run(rows_of):
        for at in range(0, 2048, 512):
            parts = [part for d in range(4) for half in (near, far) for part in rows_of(half, d, slice(at, at + 512))]
            weight = jnp.concatenate(parts, axis=0)
            kept_ref[:, at : at + 512] = jnp.dot(mine_ref[...], weight, preferred_element_type=F32).astype(BF)
            sent_ref[:, at : at + 512] = jnp.dot(other_ref[...], weight, preferred_element_type=F32).astype(BF)

    @pl.when(core_ref[0] == 0)
    def _():
        run(lambda half, d, columns: [half[d][:, columns]])

    @pl.when(core_ref[0] == 1)
    def _():
        run(lambda half, d, columns: [half[e][48 * d : 48 * d + 48, columns] for e in range(4)])


def mix(core, mine, other, near, far):
    return pl.pallas_call(
        mix_kernel,
        out_shape=(jax.ShapeDtypeStruct((ROWS, 2048), BF),) * 2,
        in_specs=[pl.BlockSpec(memory_space=pltpu.SMEM)] + [whole(0)] * 10,
        out_specs=(whole(0),) * 2,
        compiler_params=pltpu.CompilerParams(vmem_limit_bytes=48 * 2**20),
        cost_estimate=pl.CostEstimate(flops=2 * 256 * 1536 * 2048, bytes_accessed=9000000, transcendentals=0),
    )(core.reshape(1), mine, other, *near, *far)


def attend(query, keys, values, limit, first):
    scores = jnp.einsum("qhd,kd->hqk", query, keys, preferred_element_type=F32) * HD ** (-0.5)
    keys_at = jnp.arange(ROWS, dtype=jnp.int32)
    rows_at = first + jnp.arange(32, dtype=jnp.int32)
    valid = (keys_at[None, :] <= rows_at[:, None]) & (keys_at[None, :] < limit)
    scores = jnp.where(valid[None], scores, -jnp.inf)
    raised = jnp.exp(scores - jnp.max(scores, axis=-1, keepdims=True))
    weights = (raised / jnp.sum(raised, axis=-1, keepdims=True)).astype(BF)
    output = jnp.einsum("hqk,kd->qhd", weights, values, preferred_element_type=F32)
    return jnp.where((rows_at < limit)[:, None, None], output, 0.0).astype(BF)


def body(tokens, norm_gain, query_weight, kv_weight, out_weight, lengths):
    y, zh, x, c, t = (lax.axis_index(name) for name in AXES)

    packed = pack(query_weight, kv_weight.T)
    first = move(packed, lambda y, zh, x, c, t: ((2 * zh + c) ^ y, t & 1, x, t >> 1, y))
    wo_here = lax.dynamic_slice(out_weight, (0, c * 2048), (24, 2048))
    wo_there = swap(lax.dynamic_slice(out_weight, (0, (1 - c) * 2048), (24, 2048)), "core", 1)
    wo_pair = jnp.concatenate([pick(c == 1, wo_here, wo_there), pick(c == 1, wo_there, wo_here)], axis=0)

    def first_ring(piece):
        return jnp.concatenate([piece] + [along(piece, d, "x", "y") for d in (1, 2, 3)], axis=0)

    wo_near = first_ring(wo_pair)
    wo_near = [wo_near] + [along(wo_near, e, "y", "x") for e in (1, 2, 3)]

    widened = tokens.astype(F32)
    squares = jnp.sum(widened * widened, axis=1)
    gained = (widened * norm_gain[None, :]).astype(BF)

    def features(e):
        picked = []
        for d in range(4):
            s = y ^ t ^ jnp.where(c == 0, e, d)
            at = x ^ jnp.where(c == 0, d, e)
            picked.append(lax.dynamic_slice(gained, (0, (((s >> 1) * 4 + at) * 2 + (s & 1)) * 256), (ROWS, 256)))
        return jnp.concatenate(picked, axis=1)

    ring = [along(features(e), e, "y", "x") for e in (1, 2, 3)]
    second = move(packed, lambda y, zh, x, c, t: ((2 * zh + c) ^ y, 1 - (t & 1), x, t >> 1, y))
    first, second, wo_pair, *rest = lax.optimization_barrier((first, second, wo_pair, *ring, *wo_near))
    ring, wo_near = rest[:3], rest[3:]
    inputs = jnp.concatenate([features(0)] + ring, axis=0)

    def gathered(pair):
        return [pair] + [along(pair, d, "x", "y") for d in (1, 2, 3)]

    def reduced(blocks):
        sent, total = project(inputs, blocks)
        for e in (1, 2, 3):
            total = total + along(sent[e - 1], e, "y", "x").astype(F32)
        return total

    def over_zl(total, note):
        kv = total[:, 768:]
        kv_short = kv.astype(BF)
        shared = [kv_short[32 * r : 32 * r + 32] for r in range(4)] + note

        def rows_for(d):
            return lax.dynamic_slice(total, ((t ^ d) * 32, 0), (32, 768))

        q, extra = rows_for(0), 0.0
        for d in (1, 2, 3):
            came = swap(jnp.concatenate([rows_for(d).astype(BF)] + shared, axis=1), "zl", d).astype(F32)
            q = q + came[:, :768]
            kv = kv + jnp.concatenate([came[:, 768 + 128 * r : 896 + 128 * r] for r in range(4)], axis=0)
            if note:
                extra = extra + ((came[2, 1280:] + came[1, 1280:]) + came[0, 1280:])
        return (q, kv, extra) if note else (q, kv)

    high = lax.reduce_precision(squares, 8, 7)
    middle = lax.reduce_precision(squares - high, 8, 7)
    low = squares - high - middle
    note = jnp.pad(jnp.stack([high, middle, low]), ((0, 29), (0, 0))).astype(BF)

    others = swap(jnp.stack([first, second]), "core", 1)
    near_pair, far_pair = jnp.stack([first, others[0]]), jnp.stack([second, others[1]])
    far_pair, wo_far, *blocks = lax.optimization_barrier((far_pair, swap(wo_pair, "zh", 1), *gathered(near_pair)))
    total, *blocks = lax.optimization_barrier((reduced(blocks), *gathered(far_pair)))
    far_total, wo_far, *near_sums = lax.optimization_barrier(
        (reduced(blocks), first_ring(wo_far), *over_zl(total, [note]))
    )
    wo_first, *far_sums = lax.optimization_barrier((along(wo_far, 1, "y", "x"), *over_zl(far_total, [])))
    scales = lax.rsqrt((squares + near_sums[2]) / D + 1e-05)

    base = 2 * c + zh

    def ordered(near, far, width):
        return jnp.concatenate(
            by_index([half[:, at : at + width] for at in (0, width) for half in (near, far)], base), axis=1
        )

    q_raw = ordered(near_sums[0], far_sums[0], 384)
    kv_raw = ordered(near_sums[1], far_sums[1], 64)

    limit = lengths[0]
    kv = (kv_raw * scales[:, None]).astype(BF)
    keys = rotate(kv[:, :HD].astype(F32), COSINE, SINE).astype(BF)
    values = kv[:, HD:]
    mine_rows = [lax.dynamic_slice(table, (t * 32, 0), (32, HD)) for table in (COSINE, SINE)]
    scale_here = lax.dynamic_slice(scales, (t * 32,), (32,))
    query = rotate((q_raw * scale_here[:, None]).reshape(32, 12, HD), *mine_rows).astype(BF)
    attended = attend(query, keys, values, limit, t * 32).reshape(32, 1536)
    stacked = jnp.concatenate(by_index([attended[:, 384 * d : 384 * d + 384] for d in range(4)], y), axis=0)
    at = jnp.arange(384, dtype=jnp.int32)
    source = (((at // 192) ^ zh) * 4 + ((at // 48) % 4 ^ x)) * 48 + at % 48
    order = (at[:, None] == source[None, :]).astype(BF)
    stacked = jnp.dot(stacked, order, preferred_element_type=F32).astype(BF)
    attended = jnp.concatenate([stacked[32 * d : 32 * d + 32] for d in range(4)], axis=1)

    got = [attended] + [swap(attended, "zl", d) for d in (1, 2, 3)]
    wo_rest = [along(wo_far, e, "y", "x") for e in (2, 3)]
    *got, wo_second, wo_third = lax.optimization_barrier((*got, *wo_rest))
    mine = jnp.concatenate(by_index(got, t), axis=0)
    kept, sent = mix(c, mine, swap(mine, "core", 1), wo_near, [wo_far, wo_first, wo_second, wo_third])
    came = swap(sent, "core", 1)
    return jnp.concatenate([pick(c == 1, kept, came), pick(c == 1, came, kept)], axis=1)


def solution(mesh):
    fine = Mesh(mesh.devices.reshape(SIZES), AXES)
    rows = ("y", "zh", "x", "core")
    placed = (P(rows, "zl"), P("zl"), P(rows, "zl"), P(rows, "zl"), P(rows, "zl"), P(rows))
    return jax.shard_map(body, mesh=fine, in_specs=placed, out_specs=P(rows, "zl"), check_vma=False)
```

```python
import math

import jax
import jax.numpy as jnp
import numpy as np
from jax import lax
from jax.experimental import pallas as pl
from jax.experimental.pallas import tpu as pltpu
from jax.sharding import Mesh
from jax.sharding import PartitionSpec as P

AXES = ("y", "zh", "x", "core", "zl")
SIZES = (4, 2, 4, 2, 4)
D = 16384
HD = 128
ROWS = 128
BF = jnp.bfloat16
F32 = jnp.float32


def flat(*coords):
    index = 0
    for size, coord in zip(SIZES, coords):
        index = index * size + coord
    return index


def every():
    for y in range(4):
        for zh in range(2):
            for x in range(4):
                for c in range(2):
                    for t in range(4):
                        yield y, zh, x, c, t


def swap(value, axis, d):
    n = SIZES[AXES.index(axis)]
    return lax.ppermute(value, axis, [(i, i ^ d) for i in range(n)])


def move(value, where):
    return lax.ppermute(value, AXES, [(flat(*at), flat(*where(*at))) for at in every()])


def tables():
    freqs = np.exp(np.arange(HD // 2, dtype=np.float32) * np.float32(-2.0 * math.log(500000.0) / HD))
    angle = np.arange(ROWS, dtype=np.float32)[:, None] * freqs.astype(np.float32)[None, :]
    cosine = np.repeat(np.cos(angle), 2, axis=1).astype(np.float32)
    sine = np.repeat(np.sin(angle), 2, axis=1).astype(np.float32)
    sine[:, 0::2] *= -1.0
    return cosine, sine


COSINE, SINE = tables()


def order_of(zh):
    order = np.arange(384).reshape(2, 8, 24)
    order = np.stack([order[zh], order[1 - zh]], axis=1).reshape(384)
    return np.eye(384, dtype=np.float32)[:, order].astype(jnp.bfloat16)


ORDER = (order_of(0), order_of(1))


def rotate(values, cosine, sine):
    shape = (values.shape[0],) + (1,) * (values.ndim - 2) + (HD,)
    even = jnp.arange(HD) % 2 == 0
    partner = jnp.where(even, jnp.roll(values, -1, axis=-1), jnp.roll(values, 1, axis=-1))
    return values * cosine.reshape(shape) + partner * sine.reshape(shape)


def pick(flag, first, second):
    return jnp.where(flag, second, first)


def by_index(parts, at):
    odd = (at & 1) == 1
    high = (at >> 1) == 1
    a, b = pick(odd, parts[0], parts[1]), pick(odd, parts[1], parts[0])
    c, d = pick(odd, parts[2], parts[3]), pick(odd, parts[3], parts[2])
    return [pick(high, a, c), pick(high, b, d), pick(high, c, a), pick(high, d, b)]


def whole(shape):
    return pl.BlockSpec(memory_space=pltpu.VMEM)


def pack_kernel(q_ref, kv_ref, out_ref):
    for h in range(3):
        out_ref[256 * h : 256 * h + 256, :] = q_ref[:, 128 * h : 128 * h + 128]
    for h in range(2):
        out_ref[768 + 64 * h : 832 + 64 * h, :] = kv_ref[:, 128 * h : 128 * h + 128]


def pack(query_weight, kv_turned):
    return pl.pallas_call(
        pack_kernel,
        out_shape=jax.ShapeDtypeStruct((896, 128), BF),
        in_specs=[whole(0)] * 2,
        out_specs=whole(0),
        compiler_params=pltpu.CompilerParams(vmem_limit_bytes=32 * 2**20),
        cost_estimate=pl.CostEstimate(flops=0, bytes_accessed=460000, transcendentals=0),
    )(query_weight, kv_turned)


def project_kernel(x_ref, here_ref, there_ref, out_ref, own_ref):
    inputs = x_ref[...]
    for slot, ref in enumerate((here_ref, there_ref)):
        heads = [
            jnp.concatenate([ref[d, 256 * h : 256 * h + 256, :] for d in range(4)], axis=0) for h in range(3)
        ]
        q = jnp.dot(inputs, jnp.concatenate(heads, axis=1), preferred_element_type=F32)
        own_ref[:, 384 * slot : 384 * slot + 384] = q[:ROWS]
        for e in (1, 2, 3):
            out_ref[e - 1, :, 384 * slot : 384 * slot + 384] = q[ROWS * e : ROWS * e + ROWS].astype(BF)
    kv_rows = [
        jnp.concatenate([ref[d, 768 + 64 * h : 832 + 64 * h, :] for d in range(4) for h in (0, 1)], axis=1)
        for ref in (here_ref, there_ref)
    ]
    kv = lax.dot_general(
        inputs, jnp.concatenate(kv_rows, axis=0), (((1,), (1,)), ((), ())), preferred_element_type=F32
    )
    own_ref[:, 768:] = kv[:ROWS]
    for e in (1, 2, 3):
        out_ref[e - 1, :, 768:] = kv[ROWS * e : ROWS * e + ROWS].astype(BF)


def project(inputs, here, there):
    return pl.pallas_call(
        project_kernel,
        out_shape=(jax.ShapeDtypeStruct((3, ROWS, 896), BF), jax.ShapeDtypeStruct((ROWS, 896), F32)),
        in_specs=[whole(0)] * 3,
        out_specs=(whole(0),) * 2,
        compiler_params=pltpu.CompilerParams(vmem_limit_bytes=32 * 2**20),
        cost_estimate=pl.CostEstimate(flops=2 * 512 * 1024 * 896, bytes_accessed=4000000, transcendentals=0),
    )(inputs, here, there)


def attend(query, keys, values, limit, first):
    scores = jnp.einsum("qhd,kd->hqk", query, keys, preferred_element_type=F32) * HD ** (-0.5)
    keys_at = jnp.arange(ROWS, dtype=jnp.int32)
    rows_at = first + jnp.arange(32, dtype=jnp.int32)
    valid = (keys_at[None, :] <= rows_at[:, None]) & (keys_at[None, :] < limit)
    scores = jnp.where(valid[None], scores, -jnp.inf)
    raised = jnp.exp(scores - jnp.max(scores, axis=-1, keepdims=True))
    weights = (raised / jnp.sum(raised, axis=-1, keepdims=True)).astype(BF)
    output = jnp.einsum("hqk,kd->qhd", weights, values, preferred_element_type=F32)
    return jnp.where((rows_at < limit)[:, None, None], output, 0.0).astype(BF)


def body(tokens, norm_gain, query_weight, kv_weight, out_weight, lengths):
    y, zh, x, c, t = (lax.axis_index(name) for name in AXES)

    packed = pack(query_weight, kv_weight.T)
    first = move(packed, lambda y, zh, x, c, t: ((2 * zh + c) ^ y, t & 1, x, t >> 1, y))
    second = move(packed, lambda y, zh, x, c, t: ((2 * zh + c) ^ y, 1 - (t & 1), x, t >> 1, y))
    wo_other = swap(out_weight, "zh", 1)

    widened = tokens.astype(F32)
    squares = jnp.sum(widened * widened, axis=1)
    gained = (widened * norm_gain[None, :]).astype(BF)

    def features(e):
        s = y ^ e ^ t
        picked = [
            lax.dynamic_slice(gained, (0, (((s >> 1) * 4 + (x ^ d)) * 2 + (s & 1)) * 256), (ROWS, 256))
            for d in range(4)
        ]
        return jnp.concatenate(picked, axis=1)

    ring = [swap(features(e), "y", e) for e in (1, 2, 3)]
    first, second, wo_other, *ring = lax.optimization_barrier((first, second, wo_other, *ring))
    inputs = jnp.concatenate([features(0)] + ring, axis=0)

    wo_piece = jnp.concatenate([out_weight, wo_other], axis=0)
    wo = lax.all_gather(wo_piece, ("y", "x", "core"), axis=0, tiled=True)

    def gathered(block):
        return jnp.stack([block] + [swap(block, "x", d) for d in (1, 2, 3)])

    def reduced(here, there):
        sent, total = project(inputs, here, there)
        for e in (1, 2, 3):
            total = total + swap(sent[e - 1], "y", e).astype(F32)
        return total

    def over_zl(total, note):
        kv = total[:, 768:]
        kv_short = kv.astype(BF)
        shared = [kv_short[32 * r : 32 * r + 32] for r in range(4)] + note

        def rows_for(d):
            return lax.dynamic_slice(total, ((t ^ d) * 32, 0), (32, 768))

        q, extra = rows_for(0), 0.0
        for d in (1, 2, 3):
            came = swap(jnp.concatenate([rows_for(d).astype(BF)] + shared, axis=1), "zl", d).astype(F32)
            q = q + came[:, :768]
            kv = kv + jnp.concatenate([came[:, 768 + 128 * r : 896 + 128 * r] for r in range(4)], axis=0)
            if note:
                extra = extra + ((came[2, 1280:] + came[1, 1280:]) + came[0, 1280:])
        return (q, kv, extra) if note else (q, kv)

    high = lax.reduce_precision(squares, 8, 7)
    middle = lax.reduce_precision(squares - high, 8, 7)
    low = squares - high - middle
    note = jnp.pad(jnp.stack([high, middle, low]), ((0, 29), (0, 0))).astype(BF)

    second, here = lax.optimization_barrier((second, gathered(first)))
    total = reduced(here, swap(here, "core", 1))
    here = gathered(second)
    total, there = lax.optimization_barrier((total, swap(here, "core", 1)))
    far_total, *near_sums = lax.optimization_barrier((reduced(here, there), *over_zl(total, [note])))
    far_sums = over_zl(far_total, [])
    scales = lax.rsqrt((squares + near_sums[2]) / D + 1e-05)

    base = 2 * c + zh

    def ordered(near, far, width):
        return jnp.concatenate(
            by_index([half[:, at : at + width] for at in (0, width) for half in (near, far)], base), axis=1
        )

    q_raw = ordered(near_sums[0], far_sums[0], 384)
    kv_raw = ordered(near_sums[1], far_sums[1], 64)

    limit = lengths[0]
    kv = (kv_raw * scales[:, None]).astype(BF)
    keys = rotate(kv[:, :HD].astype(F32), COSINE, SINE).astype(BF)
    values = kv[:, HD:]
    mine_rows = [lax.dynamic_slice(table, (t * 32, 0), (32, HD)) for table in (COSINE, SINE)]
    scale_here = lax.dynamic_slice(scales, (t * 32,), (32,))
    query = rotate((q_raw * scale_here[:, None]).reshape(32, 12, HD), *mine_rows).astype(BF)
    attended = attend(query, keys, values, limit, t * 32).reshape(32, 1536)
    stacked = jnp.concatenate([attended[:, 384 * d : 384 * d + 384] for d in range(4)], axis=0)
    stacked = jnp.dot(stacked, pick(zh == 1, ORDER[0], ORDER[1]), preferred_element_type=F32).astype(BF)
    attended = jnp.concatenate([stacked[32 * d : 32 * d + 32] for d in range(4)], axis=1)

    got = [attended] + [swap(attended, "zl", d) for d in (1, 2, 3)]
    all_rows = jnp.concatenate(by_index(got, t), axis=0)
    return jnp.dot(all_rows, wo, preferred_element_type=F32).astype(BF)


def solution(mesh):
    fine = Mesh(mesh.devices.reshape(SIZES), AXES)
    rows = ("y", "zh", "x", "core")
    placed = (P(rows, "zl"), P("zl"), P(rows, "zl"), P(rows, "zl"), P(rows, "zl"), P(rows))
    return jax.shard_map(body, mesh=fine, in_specs=placed, out_specs=P(rows, "zl"), check_vma=False)
```

```python
import math

import jax
import jax.numpy as jnp
import numpy as np
from jax import lax
from jax.experimental import pallas as pl
from jax.experimental.pallas import tpu as pltpu
from jax.sharding import Mesh
from jax.sharding import PartitionSpec as P

AXES = ("y", "zh", "x", "core", "zl")
SIZES = (4, 2, 4, 2, 4)
D = 16384
HD = 128
ROWS = 128
BF = jnp.bfloat16
F32 = jnp.float32


def flat(*coords):
    index = 0
    for size, coord in zip(SIZES, coords):
        index = index * size + coord
    return index


def every():
    for y in range(4):
        for zh in range(2):
            for x in range(4):
                for c in range(2):
                    for t in range(4):
                        yield y, zh, x, c, t


def swap(value, axis, d):
    n = SIZES[AXES.index(axis)]
    return lax.ppermute(value, axis, [(i, i ^ d) for i in range(n)])


def move(value, where):
    return lax.ppermute(value, AXES, [(flat(*at), flat(*where(*at))) for at in every()])


def along(value, e, first, second):
    def target(*at):
        at = list(at)
        at[AXES.index((first, second)[at[3]])] ^= e
        return at

    return move(value, target)


def tables():
    freqs = np.exp(np.arange(HD // 2, dtype=np.float32) * np.float32(-2.0 * math.log(500000.0) / HD))
    angle = np.arange(ROWS, dtype=np.float32)[:, None] * freqs.astype(np.float32)[None, :]
    cosine = np.repeat(np.cos(angle), 2, axis=1).astype(np.float32)
    sine = np.repeat(np.sin(angle), 2, axis=1).astype(np.float32)
    sine[:, 0::2] *= -1.0
    return cosine, sine


COSINE, SINE = tables()


def order_of(zh):
    order = np.arange(384).reshape(2, 8, 24)
    order = np.stack([order[zh], order[1 - zh]], axis=1).reshape(384)
    return np.eye(384, dtype=np.float32)[:, order].astype(jnp.bfloat16)


ORDER = (order_of(0), order_of(1))


def rotate(values, cosine, sine):
    shape = (values.shape[0],) + (1,) * (values.ndim - 2) + (HD,)
    even = jnp.arange(HD) % 2 == 0
    partner = jnp.where(even, jnp.roll(values, -1, axis=-1), jnp.roll(values, 1, axis=-1))
    return values * cosine.reshape(shape) + partner * sine.reshape(shape)


def pick(flag, first, second):
    return jnp.where(flag, second, first)


def by_index(parts, at):
    odd = (at & 1) == 1
    high = (at >> 1) == 1
    a, b = pick(odd, parts[0], parts[1]), pick(odd, parts[1], parts[0])
    c, d = pick(odd, parts[2], parts[3]), pick(odd, parts[3], parts[2])
    return [pick(high, a, c), pick(high, b, d), pick(high, c, a), pick(high, d, b)]


def whole(shape):
    return pl.BlockSpec(memory_space=pltpu.VMEM)


def pack_kernel(q_ref, kv_ref, out_ref):
    for h in range(3):
        out_ref[256 * h : 256 * h + 256, :] = q_ref[:, 128 * h : 128 * h + 128]
    for h in range(2):
        out_ref[768 + 64 * h : 832 + 64 * h, :] = kv_ref[:, 128 * h : 128 * h + 128]


def pack(query_weight, kv_turned):
    return pl.pallas_call(
        pack_kernel,
        out_shape=jax.ShapeDtypeStruct((896, 128), BF),
        in_specs=[whole(0)] * 2,
        out_specs=whole(0),
        compiler_params=pltpu.CompilerParams(vmem_limit_bytes=32 * 2**20),
        cost_estimate=pl.CostEstimate(flops=0, bytes_accessed=460000, transcendentals=0),
    )(query_weight, kv_turned)


def project_kernel(x_ref, *refs):
    blocks, (out_ref, own_ref) = refs[:4], refs[4:]
    inputs = x_ref[...]
    for slot in range(4):
        heads = [
            jnp.concatenate([ref[slot, 256 * h : 256 * h + 256, :] for ref in blocks], axis=0) for h in range(3)
        ]
        q = jnp.dot(inputs, jnp.concatenate(heads, axis=1), preferred_element_type=F32)
        own_ref[:, 384 * slot : 384 * slot + 384] = q[:ROWS]
        for e in (1, 2, 3):
            out_ref[e - 1, :, 384 * slot : 384 * slot + 384] = q[ROWS * e : ROWS * e + ROWS].astype(BF)
    kv_rows = [
        jnp.concatenate([ref[slot, 768 + 64 * h : 832 + 64 * h, :] for ref in blocks for h in (0, 1)], axis=1)
        for slot in range(4)
    ]
    kv = lax.dot_general(
        inputs, jnp.concatenate(kv_rows, axis=0), (((1,), (1,)), ((), ())), preferred_element_type=F32
    )
    own_ref[:, 1536:] = kv[:ROWS]
    for e in (1, 2, 3):
        out_ref[e - 1, :, 1536:] = kv[ROWS * e : ROWS * e + ROWS].astype(BF)


def project(inputs, blocks):
    return pl.pallas_call(
        project_kernel,
        out_shape=(jax.ShapeDtypeStruct((3, ROWS, 1792), BF), jax.ShapeDtypeStruct((ROWS, 1792), F32)),
        in_specs=[whole(0)] * 5,
        out_specs=(whole(0),) * 2,
        compiler_params=pltpu.CompilerParams(vmem_limit_bytes=32 * 2**20),
        cost_estimate=pl.CostEstimate(flops=2 * 512 * 1024 * 1792, bytes_accessed=8000000, transcendentals=0),
    )(inputs, *blocks)


def attend(query, keys, values, limit, first):
    scores = jnp.einsum("qhd,kd->hqk", query, keys, preferred_element_type=F32) * HD ** (-0.5)
    keys_at = jnp.arange(ROWS, dtype=jnp.int32)
    rows_at = first + jnp.arange(32, dtype=jnp.int32)
    valid = (keys_at[None, :] <= rows_at[:, None]) & (keys_at[None, :] < limit)
    scores = jnp.where(valid[None], scores, -jnp.inf)
    raised = jnp.exp(scores - jnp.max(scores, axis=-1, keepdims=True))
    weights = (raised / jnp.sum(raised, axis=-1, keepdims=True)).astype(BF)
    output = jnp.einsum("hqk,kd->qhd", weights, values, preferred_element_type=F32)
    return jnp.where((rows_at < limit)[:, None, None], output, 0.0).astype(BF)


def body(tokens, norm_gain, query_weight, kv_weight, out_weight, lengths):
    y, zh, x, c, t = (lax.axis_index(name) for name in AXES)

    packed = pack(query_weight, kv_weight.T)
    first = move(packed, lambda y, zh, x, c, t: ((2 * zh + c) ^ y, t & 1, x, t >> 1, y))
    wo_other = swap(out_weight, "zh", 1)

    widened = tokens.astype(F32)
    squares = jnp.sum(widened * widened, axis=1)
    gained = (widened * norm_gain[None, :]).astype(BF)

    def features(e):
        picked = []
        for d in range(4):
            s = y ^ t ^ jnp.where(c == 0, e, d)
            at = x ^ jnp.where(c == 0, d, e)
            picked.append(lax.dynamic_slice(gained, (0, (((s >> 1) * 4 + at) * 2 + (s & 1)) * 256), (ROWS, 256)))
        return jnp.concatenate(picked, axis=1)

    ring = [along(features(e), e, "y", "x") for e in (1, 2, 3)]
    second = move(packed, lambda y, zh, x, c, t: ((2 * zh + c) ^ y, 1 - (t & 1), x, t >> 1, y))
    first, second, wo_other, *ring = lax.optimization_barrier((first, second, wo_other, *ring))
    inputs = jnp.concatenate([features(0)] + ring, axis=0)

    wo_piece = jnp.concatenate([out_weight, wo_other], axis=0)
    wo = lax.all_gather(wo_piece, ("y", "x", "core"), axis=0, tiled=True)

    pair = jnp.stack([first, second])
    pair = jnp.concatenate([pair, swap(pair, "core", 1)], axis=0)
    sent, total = project(inputs, [pair] + [along(pair, d, "x", "y") for d in (1, 2, 3)])
    for e in (1, 2, 3):
        total = total + along(sent[e - 1], e, "y", "x").astype(F32)

    kv_raw = total[:, 1536:]
    kv_short = kv_raw.astype(BF)
    high = lax.reduce_precision(squares, 8, 7)
    middle = lax.reduce_precision(squares - high, 8, 7)
    low = squares - high - middle
    note = jnp.pad(jnp.stack([high, middle, low]), ((0, 29), (0, 0))).astype(BF)
    shared = [kv_short[32 * r : 32 * r + 32] for r in range(4)] + [note]

    def rows_for(d):
        return lax.dynamic_slice(total, ((t ^ d) * 32, 0), (32, 1536))

    q_raw = rows_for(0)
    for d in (1, 2, 3):
        came = swap(jnp.concatenate([rows_for(d).astype(BF)] + shared, axis=1), "zl", d).astype(F32)
        q_raw = q_raw + came[:, :1536]
        kv_raw = kv_raw + jnp.concatenate([came[:, 1536 + 256 * r : 1792 + 256 * r] for r in range(4)], axis=0)
        squares = squares + ((came[2, 2560:] + came[1, 2560:]) + came[0, 2560:])
    scales = lax.rsqrt(squares / D + 1e-05)

    base = 2 * c + zh
    q_raw = jnp.concatenate(by_index([q_raw[:, 384 * d : 384 * d + 384] for d in range(4)], base), axis=1)
    kv_raw = jnp.concatenate(by_index([kv_raw[:, 64 * d : 64 * d + 64] for d in range(4)], base), axis=1)

    limit = lengths[0]
    kv = (kv_raw * scales[:, None]).astype(BF)
    keys = rotate(kv[:, :HD].astype(F32), COSINE, SINE).astype(BF)
    values = kv[:, HD:]
    mine_rows = [lax.dynamic_slice(table, (t * 32, 0), (32, HD)) for table in (COSINE, SINE)]
    scale_here = lax.dynamic_slice(scales, (t * 32,), (32,))
    query = rotate((q_raw * scale_here[:, None]).reshape(32, 12, HD), *mine_rows).astype(BF)
    attended = attend(query, keys, values, limit, t * 32).reshape(32, 1536)
    stacked = jnp.concatenate([attended[:, 384 * d : 384 * d + 384] for d in range(4)], axis=0)
    stacked = jnp.dot(stacked, pick(zh == 1, ORDER[0], ORDER[1]), preferred_element_type=F32).astype(BF)
    attended = jnp.concatenate([stacked[32 * d : 32 * d + 32] for d in range(4)], axis=1)

    got = [attended] + [swap(attended, "zl", d) for d in (1, 2, 3)]
    all_rows = jnp.concatenate(by_index(got, t), axis=0)
    return jnp.dot(all_rows, wo, preferred_element_type=F32).astype(BF)


def solution(mesh):
    fine = Mesh(mesh.devices.reshape(SIZES), AXES)
    rows = ("y", "zh", "x", "core")
    placed = (P(rows, "zl"), P("zl"), P(rows, "zl"), P(rows, "zl"), P(rows, "zl"), P(rows))
    return jax.shard_map(body, mesh=fine, in_specs=placed, out_specs=P(rows, "zl"), check_vma=False)
```

```python
import math

import jax
import jax.numpy as jnp
import numpy as np
from jax import lax
from jax.experimental import pallas as pl
from jax.experimental.pallas import tpu as pltpu
from jax.sharding import Mesh
from jax.sharding import PartitionSpec as P

AXES = ("y", "zh", "x", "core", "zl")
SIZES = (4, 2, 4, 2, 4)
D = 16384
HD = 128
ROWS = 128
BF = jnp.bfloat16
F32 = jnp.float32


def flat(*coords):
    index = 0
    for size, coord in zip(SIZES, coords):
        index = index * size + coord
    return index


def every():
    for y in range(4):
        for zh in range(2):
            for x in range(4):
                for c in range(2):
                    for t in range(4):
                        yield y, zh, x, c, t


def swap(value, axis, d):
    n = SIZES[AXES.index(axis)]
    return lax.ppermute(value, axis, [(i, i ^ d) for i in range(n)])


def move(value, where):
    return lax.ppermute(value, AXES, [(flat(*at), flat(*where(*at))) for at in every()])


def along(value, e, first, second):
    def target(*at):
        at = list(at)
        at[AXES.index((first, second)[at[3]])] ^= e
        return at

    return move(value, target)


def tables():
    freqs = np.exp(np.arange(HD // 2, dtype=np.float32) * np.float32(-2.0 * math.log(500000.0) / HD))
    angle = np.arange(ROWS, dtype=np.float32)[:, None] * freqs.astype(np.float32)[None, :]
    cosine = np.repeat(np.cos(angle), 2, axis=1).astype(np.float32)
    sine = np.repeat(np.sin(angle), 2, axis=1).astype(np.float32)
    sine[:, 0::2] *= -1.0
    return cosine, sine


COSINE, SINE = tables()


def order_of(zh):
    order = np.arange(384).reshape(2, 8, 24)
    order = np.stack([order[zh], order[1 - zh]], axis=1).reshape(384)
    return np.eye(384, dtype=np.float32)[:, order].astype(jnp.bfloat16)


ORDER = (order_of(0), order_of(1))


def rotate(values, cosine, sine):
    shape = (values.shape[0],) + (1,) * (values.ndim - 2) + (HD,)
    even = jnp.arange(HD) % 2 == 0
    partner = jnp.where(even, jnp.roll(values, -1, axis=-1), jnp.roll(values, 1, axis=-1))
    return values * cosine.reshape(shape) + partner * sine.reshape(shape)


def pick(flag, first, second):
    return jnp.where(flag, second, first)


def by_index(parts, at):
    odd = (at & 1) == 1
    high = (at >> 1) == 1
    a, b = pick(odd, parts[0], parts[1]), pick(odd, parts[1], parts[0])
    c, d = pick(odd, parts[2], parts[3]), pick(odd, parts[3], parts[2])
    return [pick(high, a, c), pick(high, b, d), pick(high, c, a), pick(high, d, b)]


def whole(shape):
    return pl.BlockSpec(memory_space=pltpu.VMEM)


def pack_kernel(q_ref, kv_ref, out_ref):
    for h in range(3):
        out_ref[256 * h : 256 * h + 256, :] = q_ref[:, 128 * h : 128 * h + 128]
    for h in range(2):
        out_ref[768 + 64 * h : 832 + 64 * h, :] = kv_ref[:, 128 * h : 128 * h + 128]


def pack(query_weight, kv_turned):
    return pl.pallas_call(
        pack_kernel,
        out_shape=jax.ShapeDtypeStruct((896, 128), BF),
        in_specs=[whole(0)] * 2,
        out_specs=whole(0),
        compiler_params=pltpu.CompilerParams(vmem_limit_bytes=32 * 2**20),
        cost_estimate=pl.CostEstimate(flops=0, bytes_accessed=460000, transcendentals=0),
    )(query_weight, kv_turned)


def project_kernel(x_ref, *refs):
    blocks, (out_ref, own_ref) = refs[:4], refs[4:]
    inputs = x_ref[...]
    for slot in range(4):
        heads = [
            jnp.concatenate([ref[slot, 256 * h : 256 * h + 256, :] for ref in blocks], axis=0) for h in range(3)
        ]
        q = jnp.dot(inputs, jnp.concatenate(heads, axis=1), preferred_element_type=F32)
        own_ref[:, 384 * slot : 384 * slot + 384] = q[:ROWS]
        for e in (1, 2, 3):
            out_ref[e - 1, :, 384 * slot : 384 * slot + 384] = q[ROWS * e : ROWS * e + ROWS].astype(BF)
    kv_rows = [
        jnp.concatenate([ref[slot, 768 + 64 * h : 832 + 64 * h, :] for ref in blocks for h in (0, 1)], axis=1)
        for slot in range(4)
    ]
    kv = lax.dot_general(
        inputs, jnp.concatenate(kv_rows, axis=0), (((1,), (1,)), ((), ())), preferred_element_type=F32
    )
    own_ref[:, 1536:] = kv[:ROWS]
    for e in (1, 2, 3):
        out_ref[e - 1, :, 1536:] = kv[ROWS * e : ROWS * e + ROWS].astype(BF)


def project(inputs, blocks):
    return pl.pallas_call(
        project_kernel,
        out_shape=(jax.ShapeDtypeStruct((3, ROWS, 1792), BF), jax.ShapeDtypeStruct((ROWS, 1792), F32)),
        in_specs=[whole(0)] * 5,
        out_specs=(whole(0),) * 2,
        compiler_params=pltpu.CompilerParams(vmem_limit_bytes=32 * 2**20),
        cost_estimate=pl.CostEstimate(flops=2 * 512 * 1024 * 1792, bytes_accessed=8000000, transcendentals=0),
    )(inputs, *blocks)


def attend(query, keys, values, limit, first):
    scores = jnp.einsum("qhd,kd->hqk", query, keys, preferred_element_type=F32) * HD ** (-0.5)
    keys_at = jnp.arange(ROWS, dtype=jnp.int32)
    rows_at = first + jnp.arange(32, dtype=jnp.int32)
    valid = (keys_at[None, :] <= rows_at[:, None]) & (keys_at[None, :] < limit)
    scores = jnp.where(valid[None], scores, -jnp.inf)
    raised = jnp.exp(scores - jnp.max(scores, axis=-1, keepdims=True))
    weights = (raised / jnp.sum(raised, axis=-1, keepdims=True)).astype(BF)
    output = jnp.einsum("hqk,kd->qhd", weights, values, preferred_element_type=F32)
    return jnp.where((rows_at < limit)[:, None, None], output, 0.0).astype(BF)


def body(tokens, norm_gain, query_weight, kv_weight, out_weight, lengths):
    y, zh, x, c, t = (lax.axis_index(name) for name in AXES)

    packed = pack(query_weight, kv_weight.T)
    first = move(packed, lambda y, zh, x, c, t: ((2 * zh + c) ^ y, t & 1, x, t >> 1, y))

    widened = tokens.astype(F32)
    squares = jnp.sum(widened * widened, axis=1)
    gained = (widened * norm_gain[None, :]).astype(BF)

    def features(e):
        picked = []
        for d in range(4):
            s = y ^ t ^ jnp.where(c == 0, e, d)
            at = x ^ jnp.where(c == 0, d, e)
            picked.append(lax.dynamic_slice(gained, (0, (((s >> 1) * 4 + at) * 2 + (s & 1)) * 256), (ROWS, 256)))
        return jnp.concatenate(picked, axis=1)

    ring = [along(features(e), e, "y", "x") for e in (1, 2, 3)]
    second = move(packed, lambda y, zh, x, c, t: ((2 * zh + c) ^ y, 1 - (t & 1), x, t >> 1, y))
    first, second, out_weight, *ring = lax.optimization_barrier((first, second, out_weight, *ring))
    inputs = jnp.concatenate([features(0)] + ring, axis=0)

    wo_piece = jnp.concatenate([out_weight, swap(out_weight, "zh", 1)], axis=0)
    wo = lax.all_gather(wo_piece, ("y", "x", "core"), axis=0, tiled=True)

    pair = jnp.stack([first, second])
    pair = jnp.concatenate([pair, swap(pair, "core", 1)], axis=0)
    sent, total = project(inputs, [pair] + [along(pair, d, "x", "y") for d in (1, 2, 3)])
    for e in (1, 2, 3):
        total = total + along(sent[e - 1], e, "y", "x").astype(F32)

    kv_raw = total[:, 1536:]
    kv_short = kv_raw.astype(BF)
    high = lax.reduce_precision(squares, 8, 7)
    middle = lax.reduce_precision(squares - high, 8, 7)
    low = squares - high - middle
    note = jnp.pad(jnp.stack([high, middle, low]), ((0, 29), (0, 0))).astype(BF)
    shared = [kv_short[32 * r : 32 * r + 32] for r in range(4)] + [note]

    def rows_for(d):
        return lax.dynamic_slice(total, ((t ^ d) * 32, 0), (32, 1536))

    q_raw = rows_for(0)
    for d in (1, 2, 3):
        came = swap(jnp.concatenate([rows_for(d).astype(BF)] + shared, axis=1), "zl", d).astype(F32)
        q_raw = q_raw + came[:, :1536]
        kv_raw = kv_raw + jnp.concatenate([came[:, 1536 + 256 * r : 1792 + 256 * r] for r in range(4)], axis=0)
        squares = squares + ((came[2, 2560:] + came[1, 2560:]) + came[0, 2560:])
    scales = lax.rsqrt(squares / D + 1e-05)

    base = 2 * c + zh
    q_raw = jnp.concatenate(by_index([q_raw[:, 384 * d : 384 * d + 384] for d in range(4)], base), axis=1)
    kv_raw = jnp.concatenate(by_index([kv_raw[:, 64 * d : 64 * d + 64] for d in range(4)], base), axis=1)

    limit = lengths[0]
    kv = (kv_raw * scales[:, None]).astype(BF)
    keys = rotate(kv[:, :HD].astype(F32), COSINE, SINE).astype(BF)
    values = kv[:, HD:]
    mine_rows = [lax.dynamic_slice(table, (t * 32, 0), (32, HD)) for table in (COSINE, SINE)]
    scale_here = lax.dynamic_slice(scales, (t * 32,), (32,))
    query = rotate((q_raw * scale_here[:, None]).reshape(32, 12, HD), *mine_rows).astype(BF)
    attended = attend(query, keys, values, limit, t * 32).reshape(32, 1536)
    stacked = jnp.concatenate([attended[:, 384 * d : 384 * d + 384] for d in range(4)], axis=0)
    stacked = jnp.dot(stacked, pick(zh == 1, ORDER[0], ORDER[1]), preferred_element_type=F32).astype(BF)
    attended = jnp.concatenate([stacked[32 * d : 32 * d + 32] for d in range(4)], axis=1)

    got = [attended] + [swap(attended, "zl", d) for d in (1, 2, 3)]
    all_rows = jnp.concatenate(by_index(got, t), axis=0)
    return jnp.dot(all_rows, wo, preferred_element_type=F32).astype(BF)


def solution(mesh):
    fine = Mesh(mesh.devices.reshape(SIZES), AXES)
    rows = ("y", "zh", "x", "core")
    placed = (P(rows, "zl"), P("zl"), P(rows, "zl"), P(rows, "zl"), P(rows, "zl"), P(rows))
    return jax.shard_map(body, mesh=fine, in_specs=placed, out_specs=P(rows, "zl"), check_vma=False)
```

```python
import math

import jax
import jax.numpy as jnp
import numpy as np
from jax import lax
from jax.experimental import pallas as pl
from jax.experimental.pallas import tpu as pltpu
from jax.sharding import Mesh
from jax.sharding import PartitionSpec as P

AXES = ("y", "zh", "x", "core", "zl")
SIZES = (4, 2, 4, 2, 4)
D = 16384
HD = 128
ROWS = 128
BF = jnp.bfloat16
F32 = jnp.float32


def flat(*coords):
    index = 0
    for size, coord in zip(SIZES, coords):
        index = index * size + coord
    return index


def every():
    for y in range(4):
        for zh in range(2):
            for x in range(4):
                for c in range(2):
                    for t in range(4):
                        yield y, zh, x, c, t


def swap(value, axis, d):
    n = SIZES[AXES.index(axis)]
    return lax.ppermute(value, axis, [(i, i ^ d) for i in range(n)])


def move(value, where):
    return lax.ppermute(value, AXES, [(flat(*at), flat(*where(*at))) for at in every()])


def along(value, e, first, second):
    def target(*at):
        at = list(at)
        at[AXES.index((first, second)[at[3]])] ^= e
        return at

    return move(value, target)


def tables():
    freqs = np.exp(np.arange(HD // 2, dtype=np.float32) * np.float32(-2.0 * math.log(500000.0) / HD))
    angle = np.arange(ROWS, dtype=np.float32)[:, None] * freqs.astype(np.float32)[None, :]
    cosine = np.repeat(np.cos(angle), 2, axis=1).astype(np.float32)
    sine = np.repeat(np.sin(angle), 2, axis=1).astype(np.float32)
    sine[:, 0::2] *= -1.0
    return cosine, sine


COSINE, SINE = tables()


def order_of(zh):
    order = np.arange(384).reshape(2, 8, 24)
    order = np.stack([order[zh], order[1 - zh]], axis=1).reshape(384)
    return np.eye(384, dtype=np.float32)[:, order].astype(jnp.bfloat16)


ORDER = (order_of(0), order_of(1))


def rotate(values, cosine, sine):
    shape = (values.shape[0],) + (1,) * (values.ndim - 2) + (HD,)
    even = jnp.arange(HD) % 2 == 0
    partner = jnp.where(even, jnp.roll(values, -1, axis=-1), jnp.roll(values, 1, axis=-1))
    return values * cosine.reshape(shape) + partner * sine.reshape(shape)


def pick(flag, first, second):
    return jnp.where(flag, second, first)


def by_index(parts, at):
    odd = (at & 1) == 1
    high = (at >> 1) == 1
    a, b = pick(odd, parts[0], parts[1]), pick(odd, parts[1], parts[0])
    c, d = pick(odd, parts[2], parts[3]), pick(odd, parts[3], parts[2])
    return [pick(high, a, c), pick(high, b, d), pick(high, c, a), pick(high, d, b)]


def whole(shape):
    return pl.BlockSpec(memory_space=pltpu.VMEM)


def pack_kernel(q_ref, kv_ref, out_ref):
    for h in range(3):
        out_ref[256 * h : 256 * h + 256, :] = q_ref[:, 128 * h : 128 * h + 128]
    for h in range(2):
        out_ref[768 + 64 * h : 832 + 64 * h, :] = kv_ref[:, 128 * h : 128 * h + 128]


def pack(query_weight, kv_turned):
    return pl.pallas_call(
        pack_kernel,
        out_shape=jax.ShapeDtypeStruct((896, 128), BF),
        in_specs=[whole(0)] * 2,
        out_specs=whole(0),
        compiler_params=pltpu.CompilerParams(vmem_limit_bytes=32 * 2**20),
        cost_estimate=pl.CostEstimate(flops=0, bytes_accessed=460000, transcendentals=0),
    )(query_weight, kv_turned)


def project_kernel(x_ref, *refs):
    blocks, (out_ref, own_ref) = refs[:4], refs[4:]
    inputs = x_ref[...]
    for slot in range(4):
        heads = [
            jnp.concatenate([ref[slot, 256 * h : 256 * h + 256, :] for ref in blocks], axis=0) for h in range(3)
        ]
        q = jnp.dot(inputs, jnp.concatenate(heads, axis=1), preferred_element_type=F32)
        own_ref[:, 384 * slot : 384 * slot + 384] = q[:ROWS]
        for e in (1, 2, 3):
            out_ref[e - 1, :, 384 * slot : 384 * slot + 384] = q[ROWS * e : ROWS * e + ROWS].astype(BF)
    kv_rows = [
        jnp.concatenate([ref[slot, 768 + 64 * h : 832 + 64 * h, :] for ref in blocks for h in (0, 1)], axis=1)
        for slot in range(4)
    ]
    kv = lax.dot_general(
        inputs, jnp.concatenate(kv_rows, axis=0), (((1,), (1,)), ((), ())), preferred_element_type=F32
    )
    own_ref[:, 1536:] = kv[:ROWS]
    for e in (1, 2, 3):
        out_ref[e - 1, :, 1536:] = kv[ROWS * e : ROWS * e + ROWS].astype(BF)


def project(inputs, blocks):
    return pl.pallas_call(
        project_kernel,
        out_shape=(jax.ShapeDtypeStruct((3, ROWS, 1792), BF), jax.ShapeDtypeStruct((ROWS, 1792), F32)),
        in_specs=[whole(0)] * 5,
        out_specs=(whole(0),) * 2,
        compiler_params=pltpu.CompilerParams(vmem_limit_bytes=32 * 2**20),
        cost_estimate=pl.CostEstimate(flops=2 * 512 * 1024 * 1792, bytes_accessed=8000000, transcendentals=0),
    )(inputs, *blocks)


def attend(query, keys, values, limit, first):
    scores = jnp.einsum("qhd,kd->hqk", query, keys, preferred_element_type=F32) * HD ** (-0.5)
    keys_at = jnp.arange(ROWS, dtype=jnp.int32)
    rows_at = first + jnp.arange(32, dtype=jnp.int32)
    valid = (keys_at[None, :] <= rows_at[:, None]) & (keys_at[None, :] < limit)
    scores = jnp.where(valid[None], scores, -jnp.inf)
    raised = jnp.exp(scores - jnp.max(scores, axis=-1, keepdims=True))
    weights = (raised / jnp.sum(raised, axis=-1, keepdims=True)).astype(BF)
    output = jnp.einsum("hqk,kd->qhd", weights, values, preferred_element_type=F32)
    return jnp.where((rows_at < limit)[:, None, None], output, 0.0).astype(BF)


def body(tokens, norm_gain, query_weight, kv_weight, out_weight, lengths):
    y, zh, x, c, t = (lax.axis_index(name) for name in AXES)

    packed = pack(query_weight, kv_weight.T)
    first = move(packed, lambda y, zh, x, c, t: ((2 * zh + c) ^ y, t & 1, x, t >> 1, y))

    widened = tokens.astype(F32)
    squares = jnp.sum(widened * widened, axis=1)
    gained = (widened * norm_gain[None, :]).astype(BF)

    def features(e):
        picked = []
        for d in range(4):
            s = y ^ t ^ jnp.where(c == 0, e, d)
            at = x ^ jnp.where(c == 0, d, e)
            picked.append(lax.dynamic_slice(gained, (0, (((s >> 1) * 4 + at) * 2 + (s & 1)) * 256), (ROWS, 256)))
        return jnp.concatenate(picked, axis=1)

    ring = [along(features(e), e, "y", "x") for e in (1, 2, 3)]
    second = move(packed, lambda y, zh, x, c, t: ((2 * zh + c) ^ y, 1 - (t & 1), x, t >> 1, y))
    first, second, out_weight, *ring = lax.optimization_barrier((first, second, out_weight, *ring))
    inputs = jnp.concatenate([features(0)] + ring, axis=0)

    pair = jnp.stack([first, second])
    pair = jnp.concatenate([pair, swap(pair, "core", 1)], axis=0)
    blocks = [along(pair, d, "x", "y") for d in (1, 2, 3)]
    wo_other, *blocks = lax.optimization_barrier((swap(out_weight, "zh", 1), *blocks))
    sent, total = project(inputs, [pair] + blocks)

    wo_piece = jnp.concatenate([out_weight, wo_other], axis=0)
    wo = lax.all_gather(wo_piece, ("y", "x", "core"), axis=0, tiled=True)

    for e in (1, 2, 3):
        total = total + along(sent[e - 1], e, "y", "x").astype(F32)

    kv_raw = total[:, 1536:]
    kv_short = kv_raw.astype(BF)
    high = lax.reduce_precision(squares, 8, 7)
    middle = lax.reduce_precision(squares - high, 8, 7)
    low = squares - high - middle
    note = jnp.pad(jnp.stack([high, middle, low]), ((0, 29), (0, 0))).astype(BF)
    shared = [kv_short[32 * r : 32 * r + 32] for r in range(4)] + [note]

    def rows_for(d):
        return lax.dynamic_slice(total, ((t ^ d) * 32, 0), (32, 1536))

    q_raw = rows_for(0)
    for d in (1, 2, 3):
        came = swap(jnp.concatenate([rows_for(d).astype(BF)] + shared, axis=1), "zl", d).astype(F32)
        q_raw = q_raw + came[:, :1536]
        kv_raw = kv_raw + jnp.concatenate([came[:, 1536 + 256 * r : 1792 + 256 * r] for r in range(4)], axis=0)
        squares = squares + ((came[2, 2560:] + came[1, 2560:]) + came[0, 2560:])
    scales = lax.rsqrt(squares / D + 1e-05)

    base = 2 * c + zh
    q_raw = jnp.concatenate(by_index([q_raw[:, 384 * d : 384 * d + 384] for d in range(4)], base), axis=1)
    kv_raw = jnp.concatenate(by_index([kv_raw[:, 64 * d : 64 * d + 64] for d in range(4)], base), axis=1)

    limit = lengths[0]
    kv = (kv_raw * scales[:, None]).astype(BF)
    keys = rotate(kv[:, :HD].astype(F32), COSINE, SINE).astype(BF)
    values = kv[:, HD:]
    mine_rows = [lax.dynamic_slice(table, (t * 32, 0), (32, HD)) for table in (COSINE, SINE)]
    scale_here = lax.dynamic_slice(scales, (t * 32,), (32,))
    query = rotate((q_raw * scale_here[:, None]).reshape(32, 12, HD), *mine_rows).astype(BF)
    attended = attend(query, keys, values, limit, t * 32).reshape(32, 1536)
    stacked = jnp.concatenate([attended[:, 384 * d : 384 * d + 384] for d in range(4)], axis=0)
    stacked = jnp.dot(stacked, pick(zh == 1, ORDER[0], ORDER[1]), preferred_element_type=F32).astype(BF)
    attended = jnp.concatenate([stacked[32 * d : 32 * d + 32] for d in range(4)], axis=1)

    got = [attended] + [swap(attended, "zl", d) for d in (1, 2, 3)]
    all_rows = jnp.concatenate(by_index(got, t), axis=0)
    return jnp.dot(all_rows, wo, preferred_element_type=F32).astype(BF)


def solution(mesh):
    fine = Mesh(mesh.devices.reshape(SIZES), AXES)
    rows = ("y", "zh", "x", "core")
    placed = (P(rows, "zl"), P("zl"), P(rows, "zl"), P(rows, "zl"), P(rows, "zl"), P(rows))
    return jax.shard_map(body, mesh=fine, in_specs=placed, out_specs=P(rows, "zl"), check_vma=False)
```

```python
import math

import jax
import jax.numpy as jnp
import numpy as np
from jax import lax
from jax.experimental import pallas as pl
from jax.experimental.pallas import tpu as pltpu
from jax.sharding import Mesh
from jax.sharding import PartitionSpec as P

AXES = ("y", "zh", "x", "core", "zl")
SIZES = (4, 2, 4, 2, 4)
D = 16384
HD = 128
ROWS = 128
BF = jnp.bfloat16
F32 = jnp.float32


def flat(*coords):
    index = 0
    for size, coord in zip(SIZES, coords):
        index = index * size + coord
    return index


def every():
    for y in range(4):
        for zh in range(2):
            for x in range(4):
                for c in range(2):
                    for t in range(4):
                        yield y, zh, x, c, t


def swap(value, axis, d):
    n = SIZES[AXES.index(axis)]
    return lax.ppermute(value, axis, [(i, i ^ d) for i in range(n)])


def move(value, where):
    return lax.ppermute(value, AXES, [(flat(*at), flat(*where(*at))) for at in every()])


def along(value, e, first, second):
    def target(*at):
        at = list(at)
        at[AXES.index((first, second)[at[3]])] ^= e
        return at

    return move(value, target)


def tables():
    freqs = np.exp(np.arange(HD // 2, dtype=np.float32) * np.float32(-2.0 * math.log(500000.0) / HD))
    angle = np.arange(ROWS, dtype=np.float32)[:, None] * freqs.astype(np.float32)[None, :]
    cosine = np.repeat(np.cos(angle), 2, axis=1).astype(np.float32)
    sine = np.repeat(np.sin(angle), 2, axis=1).astype(np.float32)
    sine[:, 0::2] *= -1.0
    return cosine, sine


COSINE, SINE = tables()


def order_of(zh):
    order = np.arange(384).reshape(2, 8, 24)
    order = np.stack([order[zh], order[1 - zh]], axis=1).reshape(384)
    return np.eye(384, dtype=np.float32)[:, order].astype(jnp.bfloat16)


ORDER = (order_of(0), order_of(1))


def rotate(values, cosine, sine):
    shape = (values.shape[0],) + (1,) * (values.ndim - 2) + (HD,)
    even = jnp.arange(HD) % 2 == 0
    partner = jnp.where(even, jnp.roll(values, -1, axis=-1), jnp.roll(values, 1, axis=-1))
    return values * cosine.reshape(shape) + partner * sine.reshape(shape)


def pick(flag, first, second):
    return jnp.where(flag, second, first)


def by_index(parts, at):
    odd = (at & 1) == 1
    high = (at >> 1) == 1
    a, b = pick(odd, parts[0], parts[1]), pick(odd, parts[1], parts[0])
    c, d = pick(odd, parts[2], parts[3]), pick(odd, parts[3], parts[2])
    return [pick(high, a, c), pick(high, b, d), pick(high, c, a), pick(high, d, b)]


def whole(shape):
    return pl.BlockSpec(memory_space=pltpu.VMEM)


def pack_kernel(q_ref, kv_ref, out_ref):
    for h in range(3):
        out_ref[256 * h : 256 * h + 256, :] = q_ref[:, 128 * h : 128 * h + 128]
    for h in range(2):
        out_ref[768 + 64 * h : 832 + 64 * h, :] = kv_ref[:, 128 * h : 128 * h + 128]


def pack(query_weight, kv_turned):
    return pl.pallas_call(
        pack_kernel,
        out_shape=jax.ShapeDtypeStruct((896, 128), BF),
        in_specs=[whole(0)] * 2,
        out_specs=whole(0),
        compiler_params=pltpu.CompilerParams(vmem_limit_bytes=32 * 2**20),
        cost_estimate=pl.CostEstimate(flops=0, bytes_accessed=460000, transcendentals=0),
    )(query_weight, kv_turned)


def project_kernel(x_ref, *refs):
    blocks, (out_ref, own_ref) = refs[:4], refs[4:]
    inputs = x_ref[...]
    for slot in range(4):
        heads = [
            jnp.concatenate([ref[slot, 256 * h : 256 * h + 256, :] for ref in blocks], axis=0) for h in range(3)
        ]
        q = jnp.dot(inputs, jnp.concatenate(heads, axis=1), preferred_element_type=F32)
        own_ref[:, 384 * slot : 384 * slot + 384] = q[:ROWS]
        for e in (1, 2, 3):
            out_ref[e - 1, :, 384 * slot : 384 * slot + 384] = q[ROWS * e : ROWS * e + ROWS].astype(BF)
    kv_rows = [
        jnp.concatenate([ref[slot, 768 + 64 * h : 832 + 64 * h, :] for ref in blocks for h in (0, 1)], axis=1)
        for slot in range(4)
    ]
    kv = lax.dot_general(
        inputs, jnp.concatenate(kv_rows, axis=0), (((1,), (1,)), ((), ())), preferred_element_type=F32
    )
    own_ref[:, 1536:] = kv[:ROWS]
    for e in (1, 2, 3):
        out_ref[e - 1, :, 1536:] = kv[ROWS * e : ROWS * e + ROWS].astype(BF)


def project(inputs, blocks):
    return pl.pallas_call(
        project_kernel,
        out_shape=(jax.ShapeDtypeStruct((3, ROWS, 1792), BF), jax.ShapeDtypeStruct((ROWS, 1792), F32)),
        in_specs=[whole(0)] * 5,
        out_specs=(whole(0),) * 2,
        compiler_params=pltpu.CompilerParams(vmem_limit_bytes=32 * 2**20),
        cost_estimate=pl.CostEstimate(flops=2 * 512 * 1024 * 1792, bytes_accessed=8000000, transcendentals=0),
    )(inputs, *blocks)


def attend(query, keys, values, limit, first):
    scores = jnp.einsum("qhd,kd->hqk", query, keys, preferred_element_type=F32) * HD ** (-0.5)
    keys_at = jnp.arange(ROWS, dtype=jnp.int32)
    rows_at = first + jnp.arange(32, dtype=jnp.int32)
    valid = (keys_at[None, :] <= rows_at[:, None]) & (keys_at[None, :] < limit)
    scores = jnp.where(valid[None], scores, -jnp.inf)
    raised = jnp.exp(scores - jnp.max(scores, axis=-1, keepdims=True))
    weights = (raised / jnp.sum(raised, axis=-1, keepdims=True)).astype(BF)
    output = jnp.einsum("hqk,kd->qhd", weights, values, preferred_element_type=F32)
    return jnp.where((rows_at < limit)[:, None, None], output, 0.0).astype(BF)


def body(tokens, norm_gain, query_weight, kv_weight, out_weight, lengths):
    y, zh, x, c, t = (lax.axis_index(name) for name in AXES)

    packed = pack(query_weight, kv_weight.T)
    first = move(packed, lambda y, zh, x, c, t: ((2 * zh + c) ^ y, t & 1, x, t >> 1, y))

    widened = tokens.astype(F32)
    squares = jnp.sum(widened * widened, axis=1)
    gained = (widened * norm_gain[None, :]).astype(BF)

    def features(e):
        picked = []
        for d in range(4):
            s = y ^ t ^ jnp.where(c == 0, e, d)
            at = x ^ jnp.where(c == 0, d, e)
            picked.append(lax.dynamic_slice(gained, (0, (((s >> 1) * 4 + at) * 2 + (s & 1)) * 256), (ROWS, 256)))
        return jnp.concatenate(picked, axis=1)

    ring = [along(features(e), e, "y", "x") for e in (1, 2, 3)]
    second = move(packed, lambda y, zh, x, c, t: ((2 * zh + c) ^ y, 1 - (t & 1), x, t >> 1, y))
    first, second, out_weight, *ring = lax.optimization_barrier((first, second, out_weight, *ring))
    inputs = jnp.concatenate([features(0)] + ring, axis=0)

    pair = jnp.stack([first, second])
    pair = jnp.concatenate([pair, swap(pair, "core", 1)], axis=0)
    wo_other, pair, opposite = lax.optimization_barrier((swap(out_weight, "zh", 1), pair, along(pair, 2, "x", "y")))
    blocks = [pair, along(pair, 1, "x", "y"), opposite, along(pair, 3, "x", "y")]
    sent, total = project(inputs, blocks)

    wo_piece = jnp.concatenate([out_weight, wo_other], axis=0)
    wo = lax.all_gather(wo_piece, ("y", "x", "core"), axis=0, tiled=True)

    for e in (1, 2, 3):
        total = total + along(sent[e - 1], e, "y", "x").astype(F32)

    kv_raw = total[:, 1536:]
    kv_short = kv_raw.astype(BF)
    high = lax.reduce_precision(squares, 8, 7)
    middle = lax.reduce_precision(squares - high, 8, 7)
    low = squares - high - middle
    note = jnp.pad(jnp.stack([high, middle, low]), ((0, 29), (0, 0))).astype(BF)
    shared = [kv_short[32 * r : 32 * r + 32] for r in range(4)] + [note]

    def rows_for(d):
        return lax.dynamic_slice(total, ((t ^ d) * 32, 0), (32, 1536))

    q_raw = rows_for(0)
    for d in (1, 2, 3):
        came = swap(jnp.concatenate([rows_for(d).astype(BF)] + shared, axis=1), "zl", d).astype(F32)
        q_raw = q_raw + came[:, :1536]
        kv_raw = kv_raw + jnp.concatenate([came[:, 1536 + 256 * r : 1792 + 256 * r] for r in range(4)], axis=0)
        squares = squares + ((came[2, 2560:] + came[1, 2560:]) + came[0, 2560:])
    scales = lax.rsqrt(squares / D + 1e-05)

    base = 2 * c + zh
    q_raw = jnp.concatenate(by_index([q_raw[:, 384 * d : 384 * d + 384] for d in range(4)], base), axis=1)
    kv_raw = jnp.concatenate(by_index([kv_raw[:, 64 * d : 64 * d + 64] for d in range(4)], base), axis=1)

    limit = lengths[0]
    kv = (kv_raw * scales[:, None]).astype(BF)
    keys = rotate(kv[:, :HD].astype(F32), COSINE, SINE).astype(BF)
    values = kv[:, HD:]
    mine_rows = [lax.dynamic_slice(table, (t * 32, 0), (32, HD)) for table in (COSINE, SINE)]
    scale_here = lax.dynamic_slice(scales, (t * 32,), (32,))
    query = rotate((q_raw * scale_here[:, None]).reshape(32, 12, HD), *mine_rows).astype(BF)
    attended = attend(query, keys, values, limit, t * 32).reshape(32, 1536)
    stacked = jnp.concatenate([attended[:, 384 * d : 384 * d + 384] for d in range(4)], axis=0)
    stacked = jnp.dot(stacked, pick(zh == 1, ORDER[0], ORDER[1]), preferred_element_type=F32).astype(BF)
    attended = jnp.concatenate([stacked[32 * d : 32 * d + 32] for d in range(4)], axis=1)

    got = [attended] + [swap(attended, "zl", d) for d in (1, 2, 3)]
    all_rows = jnp.concatenate(by_index(got, t), axis=0)
    return jnp.dot(all_rows, wo, preferred_element_type=F32).astype(BF)


def solution(mesh):
    fine = Mesh(mesh.devices.reshape(SIZES), AXES)
    rows = ("y", "zh", "x", "core")
    placed = (P(rows, "zl"), P("zl"), P(rows, "zl"), P(rows, "zl"), P(rows, "zl"), P(rows))
    return jax.shard_map(body, mesh=fine, in_specs=placed, out_specs=P(rows, "zl"), check_vma=False)
```

```python
import math

import jax
import jax.numpy as jnp
import numpy as np
from jax import lax
from jax.experimental import pallas as pl
from jax.experimental.pallas import tpu as pltpu
from jax.sharding import Mesh
from jax.sharding import PartitionSpec as P

AXES = ("y", "zh", "x", "core", "zl")
SIZES = (4, 2, 4, 2, 4)
D = 16384
HD = 128
ROWS = 128
BF = jnp.bfloat16
F32 = jnp.float32


def flat(*coords):
    index = 0
    for size, coord in zip(SIZES, coords):
        index = index * size + coord
    return index


def every():
    for y in range(4):
        for zh in range(2):
            for x in range(4):
                for c in range(2):
                    for t in range(4):
                        yield y, zh, x, c, t


def swap(value, axis, d):
    n = SIZES[AXES.index(axis)]
    return lax.ppermute(value, axis, [(i, i ^ d) for i in range(n)])


def move(value, where):
    return lax.ppermute(value, AXES, [(flat(*at), flat(*where(*at))) for at in every()])


def along(value, e, first, second):
    def target(*at):
        at = list(at)
        at[AXES.index((first, second)[at[3]])] ^= e
        return at

    return move(value, target)


def tables():
    freqs = np.exp(np.arange(HD // 2, dtype=np.float32) * np.float32(-2.0 * math.log(500000.0) / HD))
    angle = np.arange(ROWS, dtype=np.float32)[:, None] * freqs.astype(np.float32)[None, :]
    cosine = np.repeat(np.cos(angle), 2, axis=1).astype(np.float32)
    sine = np.repeat(np.sin(angle), 2, axis=1).astype(np.float32)
    sine[:, 0::2] *= -1.0
    return cosine, sine


COSINE, SINE = tables()


def order_of(zh):
    order = np.arange(384).reshape(2, 8, 24)
    order = np.stack([order[zh], order[1 - zh]], axis=1).reshape(384)
    return np.eye(384, dtype=np.float32)[:, order].astype(jnp.bfloat16)


ORDER = (order_of(0), order_of(1))


def rotate(values, cosine, sine):
    shape = (values.shape[0],) + (1,) * (values.ndim - 2) + (HD,)
    even = jnp.arange(HD) % 2 == 0
    partner = jnp.where(even, jnp.roll(values, -1, axis=-1), jnp.roll(values, 1, axis=-1))
    return values * cosine.reshape(shape) + partner * sine.reshape(shape)


def pick(flag, first, second):
    return jnp.where(flag, second, first)


def by_index(parts, at):
    odd = (at & 1) == 1
    high = (at >> 1) == 1
    a, b = pick(odd, parts[0], parts[1]), pick(odd, parts[1], parts[0])
    c, d = pick(odd, parts[2], parts[3]), pick(odd, parts[3], parts[2])
    return [pick(high, a, c), pick(high, b, d), pick(high, c, a), pick(high, d, b)]


def whole(shape):
    return pl.BlockSpec(memory_space=pltpu.VMEM)


def pack_kernel(q_ref, kv_ref, out_ref):
    for h in range(3):
        out_ref[256 * h : 256 * h + 256, :] = q_ref[:, 128 * h : 128 * h + 128]
    for h in range(2):
        out_ref[768 + 64 * h : 832 + 64 * h, :] = kv_ref[:, 128 * h : 128 * h + 128]


def pack(query_weight, kv_turned):
    return pl.pallas_call(
        pack_kernel,
        out_shape=jax.ShapeDtypeStruct((896, 128), BF),
        in_specs=[whole(0)] * 2,
        out_specs=whole(0),
        compiler_params=pltpu.CompilerParams(vmem_limit_bytes=32 * 2**20),
        cost_estimate=pl.CostEstimate(flops=0, bytes_accessed=460000, transcendentals=0),
    )(query_weight, kv_turned)


def project_kernel(x_ref, *refs):
    blocks, (out_ref, own_ref) = refs[:4], refs[4:]
    inputs = x_ref[...]
    for slot in range(4):
        heads = [
            jnp.concatenate([ref[slot, 256 * h : 256 * h + 256, :] for ref in blocks], axis=0) for h in range(3)
        ]
        q = jnp.dot(inputs, jnp.concatenate(heads, axis=1), preferred_element_type=F32)
        own_ref[:, 384 * slot : 384 * slot + 384] = q[:ROWS]
        for e in (1, 2, 3):
            out_ref[e - 1, :, 384 * slot : 384 * slot + 384] = q[ROWS * e : ROWS * e + ROWS].astype(BF)
    kv_rows = [
        jnp.concatenate([ref[slot, 768 + 64 * h : 832 + 64 * h, :] for ref in blocks for h in (0, 1)], axis=1)
        for slot in range(4)
    ]
    kv = lax.dot_general(
        inputs, jnp.concatenate(kv_rows, axis=0), (((1,), (1,)), ((), ())), preferred_element_type=F32
    )
    own_ref[:, 1536:] = kv[:ROWS]
    for e in (1, 2, 3):
        out_ref[e - 1, :, 1536:] = kv[ROWS * e : ROWS * e + ROWS].astype(BF)


def project(inputs, blocks):
    return pl.pallas_call(
        project_kernel,
        out_shape=(jax.ShapeDtypeStruct((3, ROWS, 1792), BF), jax.ShapeDtypeStruct((ROWS, 1792), F32)),
        in_specs=[whole(0)] * 5,
        out_specs=(whole(0),) * 2,
        compiler_params=pltpu.CompilerParams(vmem_limit_bytes=32 * 2**20),
        cost_estimate=pl.CostEstimate(flops=2 * 512 * 1024 * 1792, bytes_accessed=8000000, transcendentals=0),
    )(inputs, *blocks)


def attend(query, keys, values, limit, first):
    scores = jnp.einsum("qhd,kd->hqk", query, keys, preferred_element_type=F32) * HD ** (-0.5)
    keys_at = jnp.arange(ROWS, dtype=jnp.int32)
    rows_at = first + jnp.arange(32, dtype=jnp.int32)
    valid = (keys_at[None, :] <= rows_at[:, None]) & (keys_at[None, :] < limit)
    scores = jnp.where(valid[None], scores, -jnp.inf)
    raised = jnp.exp(scores - jnp.max(scores, axis=-1, keepdims=True))
    weights = (raised / jnp.sum(raised, axis=-1, keepdims=True)).astype(BF)
    output = jnp.einsum("hqk,kd->qhd", weights, values, preferred_element_type=F32)
    return jnp.where((rows_at < limit)[:, None, None], output, 0.0).astype(BF)


def body(tokens, norm_gain, query_weight, kv_weight, out_weight, lengths):
    y, zh, x, c, t = (lax.axis_index(name) for name in AXES)

    packed = pack(query_weight, kv_weight.T)
    first = move(packed, lambda y, zh, x, c, t: ((2 * zh + c) ^ y, t & 1, x, t >> 1, y))

    widened = tokens.astype(F32)
    squares = jnp.sum(widened * widened, axis=1)
    gained = (widened * norm_gain[None, :]).astype(BF)

    def features(e):
        picked = []
        for d in range(4):
            s = y ^ t ^ jnp.where(c == 0, e, d)
            at = x ^ jnp.where(c == 0, d, e)
            picked.append(lax.dynamic_slice(gained, (0, (((s >> 1) * 4 + at) * 2 + (s & 1)) * 256), (ROWS, 256)))
        return jnp.concatenate(picked, axis=1)

    second = move(packed, lambda y, zh, x, c, t: ((2 * zh + c) ^ y, 1 - (t & 1), x, t >> 1, y))
    first, second, gained, out_weight = lax.optimization_barrier((first, second, gained, out_weight))
    ring = [along(features(e), e, "y", "x") for e in (1, 2, 3)]
    pair = jnp.stack([first, second])
    pair = jnp.concatenate([pair, swap(pair, "core", 1)], axis=0)
    wo_other, pair, *ring = lax.optimization_barrier((swap(out_weight, "zh", 1), pair, *ring))
    inputs = jnp.concatenate([features(0)] + ring, axis=0)
    blocks = [pair] + [along(pair, d, "x", "y") for d in (1, 2, 3)]
    sent, total = project(inputs, blocks)

    wo_piece = jnp.concatenate([out_weight, wo_other], axis=0)
    wo = lax.all_gather(wo_piece, ("y", "x", "core"), axis=0, tiled=True)

    for e in (1, 2, 3):
        total = total + along(sent[e - 1], e, "y", "x").astype(F32)

    kv_raw = total[:, 1536:]
    kv_short = kv_raw.astype(BF)
    high = lax.reduce_precision(squares, 8, 7)
    middle = lax.reduce_precision(squares - high, 8, 7)
    low = squares - high - middle
    note = jnp.pad(jnp.stack([high, middle, low]), ((0, 29), (0, 0))).astype(BF)
    shared = [kv_short[32 * r : 32 * r + 32] for r in range(4)] + [note]

    def rows_for(d):
        return lax.dynamic_slice(total, ((t ^ d) * 32, 0), (32, 1536))

    q_raw = rows_for(0)
    for d in (1, 2, 3):
        came = swap(jnp.concatenate([rows_for(d).astype(BF)] + shared, axis=1), "zl", d).astype(F32)
        q_raw = q_raw + came[:, :1536]
        kv_raw = kv_raw + jnp.concatenate([came[:, 1536 + 256 * r : 1792 + 256 * r] for r in range(4)], axis=0)
        squares = squares + ((came[2, 2560:] + came[1, 2560:]) + came[0, 2560:])
    scales = lax.rsqrt(squares / D + 1e-05)

    base = 2 * c + zh
    q_raw = jnp.concatenate(by_index([q_raw[:, 384 * d : 384 * d + 384] for d in range(4)], base), axis=1)
    kv_raw = jnp.concatenate(by_index([kv_raw[:, 64 * d : 64 * d + 64] for d in range(4)], base), axis=1)

    limit = lengths[0]
    kv = (kv_raw * scales[:, None]).astype(BF)
    keys = rotate(kv[:, :HD].astype(F32), COSINE, SINE).astype(BF)
    values = kv[:, HD:]
    mine_rows = [lax.dynamic_slice(table, (t * 32, 0), (32, HD)) for table in (COSINE, SINE)]
    scale_here = lax.dynamic_slice(scales, (t * 32,), (32,))
    query = rotate((q_raw * scale_here[:, None]).reshape(32, 12, HD), *mine_rows).astype(BF)
    attended = attend(query, keys, values, limit, t * 32).reshape(32, 1536)
    stacked = jnp.concatenate([attended[:, 384 * d : 384 * d + 384] for d in range(4)], axis=0)
    stacked = jnp.dot(stacked, pick(zh == 1, ORDER[0], ORDER[1]), preferred_element_type=F32).astype(BF)
    attended = jnp.concatenate([stacked[32 * d : 32 * d + 32] for d in range(4)], axis=1)

    got = [attended] + [swap(attended, "zl", d) for d in (1, 2, 3)]
    all_rows = jnp.concatenate(by_index(got, t), axis=0)
    return jnp.dot(all_rows, wo, preferred_element_type=F32).astype(BF)


def solution(mesh):
    fine = Mesh(mesh.devices.reshape(SIZES), AXES)
    rows = ("y", "zh", "x", "core")
    placed = (P(rows, "zl"), P("zl"), P(rows, "zl"), P(rows, "zl"), P(rows, "zl"), P(rows))
    return jax.shard_map(body, mesh=fine, in_specs=placed, out_specs=P(rows, "zl"), check_vma=False)
```

```python
import math

import jax
import jax.numpy as jnp
import numpy as np
from jax import lax
from jax.experimental import pallas as pl
from jax.experimental.pallas import tpu as pltpu
from jax.sharding import Mesh
from jax.sharding import PartitionSpec as P

AXES = ("y", "zh", "x", "core", "zl")
SIZES = (4, 2, 4, 2, 4)
D = 16384
HD = 128
ROWS = 128
BF = jnp.bfloat16
F32 = jnp.float32


def flat(*coords):
    index = 0
    for size, coord in zip(SIZES, coords):
        index = index * size + coord
    return index


def every():
    for y in range(4):
        for zh in range(2):
            for x in range(4):
                for c in range(2):
                    for t in range(4):
                        yield y, zh, x, c, t


def swap(value, axis, d):
    n = SIZES[AXES.index(axis)]
    return lax.ppermute(value, axis, [(i, i ^ d) for i in range(n)])


def move(value, where):
    return lax.ppermute(value, AXES, [(flat(*at), flat(*where(*at))) for at in every()])


def along(value, e, first, second):
    def target(*at):
        at = list(at)
        at[AXES.index((first, second)[at[3]])] ^= e
        return at

    return move(value, target)


def tables():
    freqs = np.exp(np.arange(HD // 2, dtype=np.float32) * np.float32(-2.0 * math.log(500000.0) / HD))
    angle = np.arange(ROWS, dtype=np.float32)[:, None] * freqs.astype(np.float32)[None, :]
    cosine = np.repeat(np.cos(angle), 2, axis=1).astype(np.float32)
    sine = np.repeat(np.sin(angle), 2, axis=1).astype(np.float32)
    sine[:, 0::2] *= -1.0
    return cosine, sine


COSINE, SINE = tables()


def order_of(zh):
    order = np.arange(384).reshape(2, 8, 24)
    order = np.stack([order[zh], order[1 - zh]], axis=1).reshape(384)
    return np.eye(384, dtype=np.float32)[:, order].astype(jnp.bfloat16)


ORDER = (order_of(0), order_of(1))


def rotate(values, cosine, sine):
    shape = (values.shape[0],) + (1,) * (values.ndim - 2) + (HD,)
    even = jnp.arange(HD) % 2 == 0
    partner = jnp.where(even, jnp.roll(values, -1, axis=-1), jnp.roll(values, 1, axis=-1))
    return values * cosine.reshape(shape) + partner * sine.reshape(shape)


def pick(flag, first, second):
    return jnp.where(flag, second, first)


def by_index(parts, at):
    odd = (at & 1) == 1
    high = (at >> 1) == 1
    a, b = pick(odd, parts[0], parts[1]), pick(odd, parts[1], parts[0])
    c, d = pick(odd, parts[2], parts[3]), pick(odd, parts[3], parts[2])
    return [pick(high, a, c), pick(high, b, d), pick(high, c, a), pick(high, d, b)]


def whole(shape):
    return pl.BlockSpec(memory_space=pltpu.VMEM)


def pack_kernel(q_ref, kv_ref, out_ref):
    for h in range(3):
        out_ref[256 * h : 256 * h + 256, :] = q_ref[:, 128 * h : 128 * h + 128]
    for h in range(2):
        out_ref[768 + 64 * h : 832 + 64 * h, :] = kv_ref[:, 128 * h : 128 * h + 128]


def pack(query_weight, kv_turned):
    return pl.pallas_call(
        pack_kernel,
        out_shape=jax.ShapeDtypeStruct((896, 128), BF),
        in_specs=[whole(0)] * 2,
        out_specs=whole(0),
        compiler_params=pltpu.CompilerParams(vmem_limit_bytes=32 * 2**20),
        cost_estimate=pl.CostEstimate(flops=0, bytes_accessed=460000, transcendentals=0),
    )(query_weight, kv_turned)


def project_kernel(x_ref, *refs):
    blocks, (out_ref, own_ref) = refs[:4], refs[4:]
    inputs = x_ref[...]
    for slot in range(4):
        heads = [
            jnp.concatenate([ref[slot, 256 * h : 256 * h + 256, :] for ref in blocks], axis=0) for h in range(3)
        ]
        q = jnp.dot(inputs, jnp.concatenate(heads, axis=1), preferred_element_type=F32)
        own_ref[:, 384 * slot : 384 * slot + 384] = q[:ROWS]
        for e in (1, 2, 3):
            out_ref[e - 1, :, 384 * slot : 384 * slot + 384] = q[ROWS * e : ROWS * e + ROWS].astype(BF)
    kv_rows = [
        jnp.concatenate([ref[slot, 768 + 64 * h : 832 + 64 * h, :] for ref in blocks for h in (0, 1)], axis=1)
        for slot in range(4)
    ]
    kv = lax.dot_general(
        inputs, jnp.concatenate(kv_rows, axis=0), (((1,), (1,)), ((), ())), preferred_element_type=F32
    )
    own_ref[:, 1536:] = kv[:ROWS]
    for e in (1, 2, 3):
        out_ref[e - 1, :, 1536:] = kv[ROWS * e : ROWS * e + ROWS].astype(BF)


def project(inputs, blocks):
    return pl.pallas_call(
        project_kernel,
        out_shape=(jax.ShapeDtypeStruct((3, ROWS, 1792), BF), jax.ShapeDtypeStruct((ROWS, 1792), F32)),
        in_specs=[whole(0)] * 5,
        out_specs=(whole(0),) * 2,
        compiler_params=pltpu.CompilerParams(vmem_limit_bytes=32 * 2**20),
        cost_estimate=pl.CostEstimate(flops=2 * 512 * 1024 * 1792, bytes_accessed=8000000, transcendentals=0),
    )(inputs, *blocks)


def attend(query, keys, values, limit, first):
    scores = jnp.einsum("qhd,kd->hqk", query, keys, preferred_element_type=F32) * HD ** (-0.5)
    keys_at = jnp.arange(ROWS, dtype=jnp.int32)
    rows_at = first + jnp.arange(32, dtype=jnp.int32)
    valid = (keys_at[None, :] <= rows_at[:, None]) & (keys_at[None, :] < limit)
    scores = jnp.where(valid[None], scores, -jnp.inf)
    raised = jnp.exp(scores - jnp.max(scores, axis=-1, keepdims=True))
    weights = (raised / jnp.sum(raised, axis=-1, keepdims=True)).astype(BF)
    output = jnp.einsum("hqk,kd->qhd", weights, values, preferred_element_type=F32)
    return jnp.where((rows_at < limit)[:, None, None], output, 0.0).astype(BF)


def body(tokens, norm_gain, query_weight, kv_weight, out_weight, lengths):
    y, zh, x, c, t = (lax.axis_index(name) for name in AXES)

    packed = pack(query_weight, kv_weight.T)
    first = move(packed, lambda y, zh, x, c, t: ((2 * zh + c) ^ y, t & 1, x, t >> 1, y))

    widened = tokens.astype(F32)
    squares = jnp.sum(widened * widened, axis=1)
    gained = (widened * norm_gain[None, :]).astype(BF)

    def features(e):
        picked = []
        for d in range(4):
            s = y ^ t ^ jnp.where(c == 0, e, d)
            at = x ^ jnp.where(c == 0, d, e)
            picked.append(lax.dynamic_slice(gained, (0, (((s >> 1) * 4 + at) * 2 + (s & 1)) * 256), (ROWS, 256)))
        return jnp.concatenate(picked, axis=1)

    second = move(packed, lambda y, zh, x, c, t: ((2 * zh + c) ^ y, 1 - (t & 1), x, t >> 1, y))
    first, second, gained, out_weight = lax.optimization_barrier((first, second, gained, out_weight))
    ring = [along(features(e), e, "y", "x") for e in (1, 2, 3)]
    pair = jnp.stack([first, second])
    pair = jnp.concatenate([pair, swap(pair, "core", 1)], axis=0)
    wo_other, pair, opposite, *ring = lax.optimization_barrier(
        (swap(out_weight, "zh", 1), pair, along(pair, 2, "x", "y"), *ring)
    )
    inputs = jnp.concatenate([features(0)] + ring, axis=0)
    blocks = [pair, along(pair, 1, "x", "y"), opposite, along(pair, 3, "x", "y")]
    sent, total = project(inputs, blocks)

    wo_piece = jnp.concatenate([out_weight, wo_other], axis=0)
    wo = lax.all_gather(wo_piece, ("y", "x", "core"), axis=0, tiled=True)

    for e in (1, 2, 3):
        total = total + along(sent[e - 1], e, "y", "x").astype(F32)

    kv_raw = total[:, 1536:]
    kv_short = kv_raw.astype(BF)
    high = lax.reduce_precision(squares, 8, 7)
    middle = lax.reduce_precision(squares - high, 8, 7)
    low = squares - high - middle
    note = jnp.pad(jnp.stack([high, middle, low]), ((0, 29), (0, 0))).astype(BF)
    shared = [kv_short[32 * r : 32 * r + 32] for r in range(4)] + [note]

    def rows_for(d):
        return lax.dynamic_slice(total, ((t ^ d) * 32, 0), (32, 1536))

    q_raw = rows_for(0)
    for d in (1, 2, 3):
        came = swap(jnp.concatenate([rows_for(d).astype(BF)] + shared, axis=1), "zl", d).astype(F32)
        q_raw = q_raw + came[:, :1536]
        kv_raw = kv_raw + jnp.concatenate([came[:, 1536 + 256 * r : 1792 + 256 * r] for r in range(4)], axis=0)
        squares = squares + ((came[2, 2560:] + came[1, 2560:]) + came[0, 2560:])
    scales = lax.rsqrt(squares / D + 1e-05)

    base = 2 * c + zh
    q_raw = jnp.concatenate(by_index([q_raw[:, 384 * d : 384 * d + 384] for d in range(4)], base), axis=1)
    kv_raw = jnp.concatenate(by_index([kv_raw[:, 64 * d : 64 * d + 64] for d in range(4)], base), axis=1)

    limit = lengths[0]
    kv = (kv_raw * scales[:, None]).astype(BF)
    keys = rotate(kv[:, :HD].astype(F32), COSINE, SINE).astype(BF)
    values = kv[:, HD:]
    mine_rows = [lax.dynamic_slice(table, (t * 32, 0), (32, HD)) for table in (COSINE, SINE)]
    scale_here = lax.dynamic_slice(scales, (t * 32,), (32,))
    query = rotate((q_raw * scale_here[:, None]).reshape(32, 12, HD), *mine_rows).astype(BF)
    attended = attend(query, keys, values, limit, t * 32).reshape(32, 1536)
    stacked = jnp.concatenate([attended[:, 384 * d : 384 * d + 384] for d in range(4)], axis=0)
    stacked = jnp.dot(stacked, pick(zh == 1, ORDER[0], ORDER[1]), preferred_element_type=F32).astype(BF)
    attended = jnp.concatenate([stacked[32 * d : 32 * d + 32] for d in range(4)], axis=1)

    got = [attended] + [swap(attended, "zl", d) for d in (1, 2, 3)]
    all_rows = jnp.concatenate(by_index(got, t), axis=0)
    return jnp.dot(all_rows, wo, preferred_element_type=F32).astype(BF)


def solution(mesh):
    fine = Mesh(mesh.devices.reshape(SIZES), AXES)
    rows = ("y", "zh", "x", "core")
    placed = (P(rows, "zl"), P("zl"), P(rows, "zl"), P(rows, "zl"), P(rows, "zl"), P(rows))
    return jax.shard_map(body, mesh=fine, in_specs=placed, out_specs=P(rows, "zl"), check_vma=False)
```

```python
import math

import jax
import jax.numpy as jnp
import numpy as np
from jax import lax
from jax.experimental import pallas as pl
from jax.experimental.pallas import tpu as pltpu
from jax.sharding import Mesh
from jax.sharding import PartitionSpec as P

AXES = ("y", "zh", "x", "core", "zl")
SIZES = (4, 2, 4, 2, 4)
D = 16384
HD = 128
ROWS = 128
BF = jnp.bfloat16
F32 = jnp.float32


def flat(*coords):
    index = 0
    for size, coord in zip(SIZES, coords):
        index = index * size + coord
    return index


def every():
    for y in range(4):
        for zh in range(2):
            for x in range(4):
                for c in range(2):
                    for t in range(4):
                        yield y, zh, x, c, t


def swap(value, axis, d):
    n = SIZES[AXES.index(axis)]
    return lax.ppermute(value, axis, [(i, i ^ d) for i in range(n)])


def move(value, where):
    return lax.ppermute(value, AXES, [(flat(*at), flat(*where(*at))) for at in every()])


def along(value, e, first, second):
    def target(*at):
        at = list(at)
        at[AXES.index((first, second)[at[3]])] ^= e
        return at

    return move(value, target)


def tables():
    freqs = np.exp(np.arange(HD // 2, dtype=np.float32) * np.float32(-2.0 * math.log(500000.0) / HD))
    angle = np.arange(ROWS, dtype=np.float32)[:, None] * freqs.astype(np.float32)[None, :]
    cosine = np.repeat(np.cos(angle), 2, axis=1).astype(np.float32)
    sine = np.repeat(np.sin(angle), 2, axis=1).astype(np.float32)
    sine[:, 0::2] *= -1.0
    return cosine, sine


COSINE, SINE = tables()


def order_of(zh):
    order = np.arange(384).reshape(2, 8, 24)
    order = np.stack([order[zh], order[1 - zh]], axis=1).reshape(384)
    return np.eye(384, dtype=np.float32)[:, order].astype(jnp.bfloat16)


ORDER = (order_of(0), order_of(1))


def rotate(values, cosine, sine):
    shape = (values.shape[0],) + (1,) * (values.ndim - 2) + (HD,)
    even = jnp.arange(HD) % 2 == 0
    partner = jnp.where(even, jnp.roll(values, -1, axis=-1), jnp.roll(values, 1, axis=-1))
    return values * cosine.reshape(shape) + partner * sine.reshape(shape)


def pick(flag, first, second):
    return jnp.where(flag, second, first)


def by_index(parts, at):
    odd = (at & 1) == 1
    high = (at >> 1) == 1
    a, b = pick(odd, parts[0], parts[1]), pick(odd, parts[1], parts[0])
    c, d = pick(odd, parts[2], parts[3]), pick(odd, parts[3], parts[2])
    return [pick(high, a, c), pick(high, b, d), pick(high, c, a), pick(high, d, b)]


def whole(shape):
    return pl.BlockSpec(memory_space=pltpu.VMEM)


def pack_kernel(q_ref, kv_ref, out_ref):
    for h in range(3):
        out_ref[256 * h : 256 * h + 256, :] = q_ref[:, 128 * h : 128 * h + 128]
    for h in range(2):
        out_ref[768 + 64 * h : 832 + 64 * h, :] = kv_ref[:, 128 * h : 128 * h + 128]


def pack(query_weight, kv_turned):
    return pl.pallas_call(
        pack_kernel,
        out_shape=jax.ShapeDtypeStruct((896, 128), BF),
        in_specs=[whole(0)] * 2,
        out_specs=whole(0),
        compiler_params=pltpu.CompilerParams(vmem_limit_bytes=32 * 2**20),
        cost_estimate=pl.CostEstimate(flops=0, bytes_accessed=460000, transcendentals=0),
    )(query_weight, kv_turned)


def project_kernel(x_ref, *refs):
    blocks, (out_ref, own_ref) = refs[:4], refs[4:]
    inputs = x_ref[...]
    for slot in range(4):
        heads = [
            jnp.concatenate([ref[slot, 256 * h : 256 * h + 256, :] for ref in blocks], axis=0) for h in range(3)
        ]
        q = jnp.dot(inputs, jnp.concatenate(heads, axis=1), preferred_element_type=F32)
        own_ref[:, 384 * slot : 384 * slot + 384] = q[:ROWS]
        for e in (1, 2, 3):
            out_ref[e - 1, :, 384 * slot : 384 * slot + 384] = q[ROWS * e : ROWS * e + ROWS].astype(BF)
    kv_rows = [
        jnp.concatenate([ref[slot, 768 + 64 * h : 832 + 64 * h, :] for ref in blocks for h in (0, 1)], axis=1)
        for slot in range(4)
    ]
    kv = lax.dot_general(
        inputs, jnp.concatenate(kv_rows, axis=0), (((1,), (1,)), ((), ())), preferred_element_type=F32
    )
    own_ref[:, 1536:] = kv[:ROWS]
    for e in (1, 2, 3):
        out_ref[e - 1, :, 1536:] = kv[ROWS * e : ROWS * e + ROWS].astype(BF)


def project(inputs, blocks):
    return pl.pallas_call(
        project_kernel,
        out_shape=(jax.ShapeDtypeStruct((3, ROWS, 1792), BF), jax.ShapeDtypeStruct((ROWS, 1792), F32)),
        in_specs=[whole(0)] * 5,
        out_specs=(whole(0),) * 2,
        compiler_params=pltpu.CompilerParams(vmem_limit_bytes=32 * 2**20),
        cost_estimate=pl.CostEstimate(flops=2 * 512 * 1024 * 1792, bytes_accessed=8000000, transcendentals=0),
    )(inputs, *blocks)


def attend(query, keys, values, limit, first):
    scores = jnp.einsum("qhd,kd->hqk", query, keys, preferred_element_type=F32) * HD ** (-0.5)
    keys_at = jnp.arange(ROWS, dtype=jnp.int32)
    rows_at = first + jnp.arange(32, dtype=jnp.int32)
    valid = (keys_at[None, :] <= rows_at[:, None]) & (keys_at[None, :] < limit)
    scores = jnp.where(valid[None], scores, -jnp.inf)
    raised = jnp.exp(scores - jnp.max(scores, axis=-1, keepdims=True))
    weights = (raised / jnp.sum(raised, axis=-1, keepdims=True)).astype(BF)
    output = jnp.einsum("hqk,kd->qhd", weights, values, preferred_element_type=F32)
    return jnp.where((rows_at < limit)[:, None, None], output, 0.0).astype(BF)


def body(tokens, norm_gain, query_weight, kv_weight, out_weight, lengths):
    y, zh, x, c, t = (lax.axis_index(name) for name in AXES)

    packed = pack(query_weight, kv_weight.T)
    first = move(packed, lambda y, zh, x, c, t: ((2 * zh + c) ^ y, t & 1, x, t >> 1, y))

    widened = tokens.astype(F32)
    squares = jnp.sum(widened * widened, axis=1)
    gained = (widened * norm_gain[None, :]).astype(BF)

    def features(e):
        picked = []
        for d in range(4):
            s = y ^ t ^ jnp.where(c == 0, e, d)
            at = x ^ jnp.where(c == 0, d, e)
            picked.append(lax.dynamic_slice(gained, (0, (((s >> 1) * 4 + at) * 2 + (s & 1)) * 256), (ROWS, 256)))
        return jnp.concatenate(picked, axis=1)

    ring = [along(features(e)[:, at : at + 512], e, "y", "x") for e in (1, 2, 3) for at in (0, 512)]
    second = move(packed, lambda y, zh, x, c, t: ((2 * zh + c) ^ y, 1 - (t & 1), x, t >> 1, y))
    first, second, out_weight, *ring = lax.optimization_barrier((first, second, out_weight, *ring))
    ring = [jnp.concatenate(ring[at : at + 2], axis=1) for at in (0, 2, 4)]
    inputs = jnp.concatenate([features(0)] + ring, axis=0)

    pair = jnp.stack([first, second])
    pair = jnp.concatenate([pair, swap(pair, "core", 1)], axis=0)
    wo_other, pair, opposite = lax.optimization_barrier((swap(out_weight, "zh", 1), pair, along(pair, 2, "x", "y")))
    blocks = [pair, along(pair, 1, "x", "y"), opposite, along(pair, 3, "x", "y")]
    sent, total = project(inputs, blocks)

    wo_piece = jnp.concatenate([out_weight, wo_other], axis=0)
    wo = lax.all_gather(wo_piece, ("y", "x", "core"), axis=0, tiled=True)

    for e in (1, 2, 3):
        total = total + along(sent[e - 1], e, "y", "x").astype(F32)

    kv_raw = total[:, 1536:]
    kv_short = kv_raw.astype(BF)
    high = lax.reduce_precision(squares, 8, 7)
    middle = lax.reduce_precision(squares - high, 8, 7)
    low = squares - high - middle
    note = jnp.pad(jnp.stack([high, middle, low]), ((0, 29), (0, 0))).astype(BF)
    shared = [kv_short[32 * r : 32 * r + 32] for r in range(4)] + [note]

    def rows_for(d):
        return lax.dynamic_slice(total, ((t ^ d) * 32, 0), (32, 1536))

    q_raw = rows_for(0)
    for d in (1, 2, 3):
        came = swap(jnp.concatenate([rows_for(d).astype(BF)] + shared, axis=1), "zl", d).astype(F32)
        q_raw = q_raw + came[:, :1536]
        kv_raw = kv_raw + jnp.concatenate([came[:, 1536 + 256 * r : 1792 + 256 * r] for r in range(4)], axis=0)
        squares = squares + ((came[2, 2560:] + came[1, 2560:]) + came[0, 2560:])
    scales = lax.rsqrt(squares / D + 1e-05)

    base = 2 * c + zh
    q_raw = jnp.concatenate(by_index([q_raw[:, 384 * d : 384 * d + 384] for d in range(4)], base), axis=1)
    kv_raw = jnp.concatenate(by_index([kv_raw[:, 64 * d : 64 * d + 64] for d in range(4)], base), axis=1)

    limit = lengths[0]
    kv = (kv_raw * scales[:, None]).astype(BF)
    keys = rotate(kv[:, :HD].astype(F32), COSINE, SINE).astype(BF)
    values = kv[:, HD:]
    mine_rows = [lax.dynamic_slice(table, (t * 32, 0), (32, HD)) for table in (COSINE, SINE)]
    scale_here = lax.dynamic_slice(scales, (t * 32,), (32,))
    query = rotate((q_raw * scale_here[:, None]).reshape(32, 12, HD), *mine_rows).astype(BF)
    attended = attend(query, keys, values, limit, t * 32).reshape(32, 1536)
    stacked = jnp.concatenate([attended[:, 384 * d : 384 * d + 384] for d in range(4)], axis=0)
    stacked = jnp.dot(stacked, pick(zh == 1, ORDER[0], ORDER[1]), preferred_element_type=F32).astype(BF)
    attended = jnp.concatenate([stacked[32 * d : 32 * d + 32] for d in range(4)], axis=1)

    got = [attended] + [swap(attended, "zl", d) for d in (1, 2, 3)]
    all_rows = jnp.concatenate(by_index(got, t), axis=0)
    return jnp.dot(all_rows, wo, preferred_element_type=F32).astype(BF)


def solution(mesh):
    fine = Mesh(mesh.devices.reshape(SIZES), AXES)
    rows = ("y", "zh", "x", "core")
    placed = (P(rows, "zl"), P("zl"), P(rows, "zl"), P(rows, "zl"), P(rows, "zl"), P(rows))
    return jax.shard_map(body, mesh=fine, in_specs=placed, out_specs=P(rows, "zl"), check_vma=False)
```

```python
import math

import jax
import jax.numpy as jnp
import numpy as np
from jax import lax
from jax.experimental import pallas as pl
from jax.experimental.pallas import tpu as pltpu
from jax.sharding import Mesh
from jax.sharding import PartitionSpec as P

AXES = ("y", "zh", "x", "core", "zl")
SIZES = (4, 2, 4, 2, 4)
D = 16384
HD = 128
ROWS = 128
BF = jnp.bfloat16
F32 = jnp.float32


def flat(*coords):
    index = 0
    for size, coord in zip(SIZES, coords):
        index = index * size + coord
    return index


def every():
    for y in range(4):
        for zh in range(2):
            for x in range(4):
                for c in range(2):
                    for t in range(4):
                        yield y, zh, x, c, t


def swap(value, axis, d):
    n = SIZES[AXES.index(axis)]
    return lax.ppermute(value, axis, [(i, i ^ d) for i in range(n)])


def move(value, where):
    return lax.ppermute(value, AXES, [(flat(*at), flat(*where(*at))) for at in every()])


def along(value, e, first, second):
    def target(*at):
        at = list(at)
        at[AXES.index((first, second)[at[3]])] ^= e
        return at

    return move(value, target)


def tables():
    freqs = np.exp(np.arange(HD // 2, dtype=np.float32) * np.float32(-2.0 * math.log(500000.0) / HD))
    angle = np.arange(ROWS, dtype=np.float32)[:, None] * freqs.astype(np.float32)[None, :]
    cosine = np.repeat(np.cos(angle), 2, axis=1).astype(np.float32)
    sine = np.repeat(np.sin(angle), 2, axis=1).astype(np.float32)
    sine[:, 0::2] *= -1.0
    return cosine, sine


COSINE, SINE = tables()


def order_of(zh):
    order = np.arange(384).reshape(2, 8, 24)
    order = np.stack([order[zh], order[1 - zh]], axis=1).reshape(384)
    return np.eye(384, dtype=np.float32)[:, order].astype(jnp.bfloat16)


ORDER = (order_of(0), order_of(1))


def rotate(values, cosine, sine):
    shape = (values.shape[0],) + (1,) * (values.ndim - 2) + (HD,)
    even = jnp.arange(HD) % 2 == 0
    partner = jnp.where(even, jnp.roll(values, -1, axis=-1), jnp.roll(values, 1, axis=-1))
    return values * cosine.reshape(shape) + partner * sine.reshape(shape)


def pick(flag, first, second):
    return jnp.where(flag, second, first)


def by_index(parts, at):
    odd = (at & 1) == 1
    high = (at >> 1) == 1
    a, b = pick(odd, parts[0], parts[1]), pick(odd, parts[1], parts[0])
    c, d = pick(odd, parts[2], parts[3]), pick(odd, parts[3], parts[2])
    return [pick(high, a, c), pick(high, b, d), pick(high, c, a), pick(high, d, b)]


def whole(shape):
    return pl.BlockSpec(memory_space=pltpu.VMEM)


def pack_kernel(q_ref, kv_ref, out_ref):
    for h in range(3):
        out_ref[256 * h : 256 * h + 256, :] = q_ref[:, 128 * h : 128 * h + 128]
    for h in range(2):
        out_ref[768 + 64 * h : 832 + 64 * h, :] = kv_ref[:, 128 * h : 128 * h + 128]


def pack(query_weight, kv_turned):
    return pl.pallas_call(
        pack_kernel,
        out_shape=jax.ShapeDtypeStruct((896, 128), BF),
        in_specs=[whole(0)] * 2,
        out_specs=whole(0),
        compiler_params=pltpu.CompilerParams(vmem_limit_bytes=32 * 2**20),
        cost_estimate=pl.CostEstimate(flops=0, bytes_accessed=460000, transcendentals=0),
    )(query_weight, kv_turned)


def project_kernel(x_ref, *refs):
    blocks, (out_ref, own_ref) = refs[:4], refs[4:]
    inputs = x_ref[...]
    for slot in range(4):
        heads = [
            jnp.concatenate([ref[slot, 256 * h : 256 * h + 256, :] for ref in blocks], axis=0) for h in range(3)
        ]
        q = jnp.dot(inputs, jnp.concatenate(heads, axis=1), preferred_element_type=F32)
        own_ref[:, 384 * slot : 384 * slot + 384] = q[:ROWS]
        for e in (1, 2, 3):
            out_ref[e - 1, :, 384 * slot : 384 * slot + 384] = q[ROWS * e : ROWS * e + ROWS].astype(BF)
    kv_rows = [
        jnp.concatenate([ref[slot, 768 + 64 * h : 832 + 64 * h, :] for ref in blocks for h in (0, 1)], axis=1)
        for slot in range(4)
    ]
    kv = lax.dot_general(
        inputs, jnp.concatenate(kv_rows, axis=0), (((1,), (1,)), ((), ())), preferred_element_type=F32
    )
    own_ref[:, 1536:] = kv[:ROWS]
    for e in (1, 2, 3):
        out_ref[e - 1, :, 1536:] = kv[ROWS * e : ROWS * e + ROWS].astype(BF)


def project(inputs, blocks):
    return pl.pallas_call(
        project_kernel,
        out_shape=(jax.ShapeDtypeStruct((3, ROWS, 1792), BF), jax.ShapeDtypeStruct((ROWS, 1792), F32)),
        in_specs=[whole(0)] * 5,
        out_specs=(whole(0),) * 2,
        compiler_params=pltpu.CompilerParams(vmem_limit_bytes=32 * 2**20),
        cost_estimate=pl.CostEstimate(flops=2 * 512 * 1024 * 1792, bytes_accessed=8000000, transcendentals=0),
    )(inputs, *blocks)


def attend(query, keys, values, limit, first):
    scores = jnp.einsum("qhd,kd->hqk", query, keys, preferred_element_type=F32) * HD ** (-0.5)
    keys_at = jnp.arange(ROWS, dtype=jnp.int32)
    rows_at = first + jnp.arange(32, dtype=jnp.int32)
    valid = (keys_at[None, :] <= rows_at[:, None]) & (keys_at[None, :] < limit)
    scores = jnp.where(valid[None], scores, -jnp.inf)
    raised = jnp.exp(scores - jnp.max(scores, axis=-1, keepdims=True))
    weights = (raised / jnp.sum(raised, axis=-1, keepdims=True)).astype(BF)
    output = jnp.einsum("hqk,kd->qhd", weights, values, preferred_element_type=F32)
    return jnp.where((rows_at < limit)[:, None, None], output, 0.0).astype(BF)


def body(tokens, norm_gain, query_weight, kv_weight, out_weight, lengths):
    y, zh, x, c, t = (lax.axis_index(name) for name in AXES)

    packed = pack(query_weight, kv_weight.T)
    first = move(packed, lambda y, zh, x, c, t: ((2 * zh + c) ^ y, t & 1, x, t >> 1, y))

    widened = tokens.astype(F32)
    squares = jnp.sum(widened * widened, axis=1)
    gained = (widened * norm_gain[None, :]).astype(BF)

    def features(e):
        picked = []
        for d in range(4):
            s = y ^ t ^ jnp.where(c == 0, e, d)
            at = x ^ jnp.where(c == 0, d, e)
            picked.append(lax.dynamic_slice(gained, (0, (((s >> 1) * 4 + at) * 2 + (s & 1)) * 256), (ROWS, 256)))
        return jnp.concatenate(picked, axis=1)

    second = move(packed, lambda y, zh, x, c, t: ((2 * zh + c) ^ y, 1 - (t & 1), x, t >> 1, y))
    first, second, gained, out_weight = lax.optimization_barrier((first, second, gained, out_weight))
    ring = [along(features(e)[:, at : at + 512], e, "y", "x") for e in (1, 2, 3) for at in (0, 512)]
    pair = jnp.stack([first, second])
    pair = jnp.concatenate([pair, swap(pair, "core", 1)], axis=0)
    wo_other, pair, opposite, *ring = lax.optimization_barrier(
        (swap(out_weight, "zh", 1), pair, along(pair, 2, "x", "y"), *ring)
    )
    ring = [jnp.concatenate(ring[at : at + 2], axis=1) for at in (0, 2, 4)]
    inputs = jnp.concatenate([features(0)] + ring, axis=0)
    blocks = [pair, along(pair, 1, "x", "y"), opposite, along(pair, 3, "x", "y")]
    sent, total = project(inputs, blocks)

    wo_piece = jnp.concatenate([out_weight, wo_other], axis=0)
    wo = lax.all_gather(wo_piece, ("y", "x", "core"), axis=0, tiled=True)

    for e in (1, 2, 3):
        total = total + along(sent[e - 1], e, "y", "x").astype(F32)

    kv_raw = total[:, 1536:]
    kv_short = kv_raw.astype(BF)
    high = lax.reduce_precision(squares, 8, 7)
    middle = lax.reduce_precision(squares - high, 8, 7)
    low = squares - high - middle
    note = jnp.pad(jnp.stack([high, middle, low]), ((0, 29), (0, 0))).astype(BF)
    shared = [kv_short[32 * r : 32 * r + 32] for r in range(4)] + [note]

    def rows_for(d):
        return lax.dynamic_slice(total, ((t ^ d) * 32, 0), (32, 1536))

    q_raw = rows_for(0)
    for d in (1, 2, 3):
        came = swap(jnp.concatenate([rows_for(d).astype(BF)] + shared, axis=1), "zl", d).astype(F32)
        q_raw = q_raw + came[:, :1536]
        kv_raw = kv_raw + jnp.concatenate([came[:, 1536 + 256 * r : 1792 + 256 * r] for r in range(4)], axis=0)
        squares = squares + ((came[2, 2560:] + came[1, 2560:]) + came[0, 2560:])
    scales = lax.rsqrt(squares / D + 1e-05)

    base = 2 * c + zh
    q_raw = jnp.concatenate(by_index([q_raw[:, 384 * d : 384 * d + 384] for d in range(4)], base), axis=1)
    kv_raw = jnp.concatenate(by_index([kv_raw[:, 64 * d : 64 * d + 64] for d in range(4)], base), axis=1)

    limit = lengths[0]
    kv = (kv_raw * scales[:, None]).astype(BF)
    keys = rotate(kv[:, :HD].astype(F32), COSINE, SINE).astype(BF)
    values = kv[:, HD:]
    mine_rows = [lax.dynamic_slice(table, (t * 32, 0), (32, HD)) for table in (COSINE, SINE)]
    scale_here = lax.dynamic_slice(scales, (t * 32,), (32,))
    query = rotate((q_raw * scale_here[:, None]).reshape(32, 12, HD), *mine_rows).astype(BF)
    attended = attend(query, keys, values, limit, t * 32).reshape(32, 1536)
    stacked = jnp.concatenate([attended[:, 384 * d : 384 * d + 384] for d in range(4)], axis=0)
    stacked = jnp.dot(stacked, pick(zh == 1, ORDER[0], ORDER[1]), preferred_element_type=F32).astype(BF)
    attended = jnp.concatenate([stacked[32 * d : 32 * d + 32] for d in range(4)], axis=1)

    got = [attended] + [swap(attended, "zl", d) for d in (1, 2, 3)]
    all_rows = jnp.concatenate(by_index(got, t), axis=0)
    return jnp.dot(all_rows, wo, preferred_element_type=F32).astype(BF)


def solution(mesh):
    fine = Mesh(mesh.devices.reshape(SIZES), AXES)
    rows = ("y", "zh", "x", "core")
    placed = (P(rows, "zl"), P("zl"), P(rows, "zl"), P(rows, "zl"), P(rows, "zl"), P(rows))
    return jax.shard_map(body, mesh=fine, in_specs=placed, out_specs=P(rows, "zl"), check_vma=False)
```
